256 devices in a mesh: band: 4 (over z_hi, core), grid: 64 (over y, x, z_lo).
Axes of the slice: x: 4, y: 4, z: 8 (z_hi: 2, z_lo: 4; z = z_hi * 4 + z_lo), core: 2. Of those that a mesh axis runs over, the one named last changes fastest.
Arguments:
- orbitals: float32 [8, 128, 128, 128], P('band', 'grid'), may hold values from -6 to 6
- occupation: float32 [8], replicated, may hold values from 0.25 to 2
- kept_modes: int32 [128, 128, 128], P(None, 'grid'), may hold values from 0 to 1, as said below
Outputs:
- exchange_action: float32 [8, 128, 128, 128], P('band', 'grid')
The draws below stay inside these ranges and needn't reach their ends.
Inputs may be any that keep to these rules, and one draw needn't show every extreme that they name: 0 or 1; kept_modes[a, b, c] is 0 wherever k(a)^2 + k(b)^2 + k(c)^2 > 57^2, with k as in the kernel's step; kept_modes[a, b, c] equals kept_modes[(128 - a) % 128, (128 - b) % 128, (128 - c) % 128].
All inputs are finite; a program needn't handle non-finite values.
Results may differ from the reference program's by a relative error of at most 0.0003.
Values sent between devices are 32-bit elements; how exact they have to be, the bound alone decides.
A program may use at most 64 MiB of HBM per device.

```python
import math
import jax
import jax.numpy as jnp
from jax import lax

G = 128
CUTOFF = 57
NB = 8


def draw_kept_modes(key, part):
    key = jax.random.fold_in(key, 11)
    indices = jnp.arange(G, dtype=jnp.int32)
    frequency = jnp.where(indices < G // 2, indices, indices - G)
    squared = frequency[:, None, None] ** 2 + frequency[None, :, None] ** 2 + frequency[None, None, :] ** 2
    inside = squared <= CUTOFF * CUTOFF
    dropped = jax.random.randint(key, (G, G, G), 0, 48) == 0
    mirror = (G - indices) % G
    flipped = jnp.take(jnp.take(jnp.take(dropped, mirror, axis=0), mirror, axis=1), mirror, axis=2)
    removed = jnp.logical_or(dropped, flipped)
    return jnp.logical_and(inside, jnp.logical_not(removed)).astype(jnp.int32)


def levels(rng, dims, cuts, least, largest):
    def one(position, shards_of):
        heights = jax.random.uniform(jax.random.fold_in(jax.random.fold_in(rng, 6), position), (shards_of,), jnp.float32, least / len(cuts), largest / len(cuts))
        return jnp.repeat(jnp.exp(heights), dims[position] // shards_of).reshape((-1,) + (1,) * (len(dims) - position - 1))

    factor_of = one(*cuts[0])
    for cut in cuts[1:]:
        factor_of = factor_of * one(*cut)
    return factor_of


def scatter_about(rng, shape, spread, most, cuts=(), kind=jnp.bfloat16):
    entries = jax.random.normal(rng, shape, jnp.float32) * spread
    if len(cuts) > 0:
        entries = levels(rng, shape, cuts, -0.22, 0.18) * entries
    return jnp.clip(entries, min=-most, max=most).astype(kind)


def setup_inputs(seed: int = 0) -> dict:
    seeds = jax.random.split(jax.random.key(seed), 4)
    orbitals = scatter_about(seeds[0], (NB, G, G, G), 1.0, 6.0, ((0, 4), (1, 64)), jnp.float32)
    occupation = jnp.clip(jnp.exp(jax.random.uniform(seeds[1], (NB,), jnp.float32, math.log(0.25), math.log(2.0))), 0.25, 2.0)
    kept_modes = draw_kept_modes(jax.random.fold_in(seeds[3], 71), 0)
    return {"orbitals": orbitals, "occupation": occupation, "kept_modes": kept_modes}


def coulomb_kernel(points, kept_modes):
    indices = jnp.arange(points, dtype=jnp.int32)
    frequency = jnp.where(indices < points // 2, indices, indices - points)
    squared = frequency[:, None, None] ** 2 + frequency[None, :, None] ** 2 + frequency[None, None, :] ** 2
    safe = jnp.maximum(squared, 1).astype(jnp.float32)
    kernel = jnp.where(squared > 0, (8.0 * math.pi) / safe, jnp.float32(0.0))
    return kernel * kept_modes.astype(jnp.float32)


def reference(orbitals, occupation, kept_modes):
    kernel = coulomb_kernel(orbitals.shape[1], kept_modes)

    def one_band(target_index):
        target = orbitals[target_index]

        def accumulate(running, source_index):
            source = orbitals[source_index]
            density = source * target
            potential = jnp.real(jnp.fft.ifftn(jnp.fft.fftn(density) * kernel))
            return running - occupation[source_index] * source * potential, None

        running, unused = lax.scan(accumulate, jnp.zeros(target.shape, jnp.float32), jnp.arange(NB, dtype=jnp.int32))
        return running

    return lax.map(one_band, jnp.arange(NB, dtype=jnp.int32))
```

```python
import functools
import math

import jax
import jax.numpy as jnp
import ml_dtypes
import numpy as np
from jax import lax
from jax.experimental import pallas as pl
from jax.experimental.pallas import tpu as pltpu
from jax.sharding import PartitionSpec as P

MESH = pl.DeviceIdType.MESH
N = 128
PEERS = 64
PITCH = 16
ROWS_O = 15
ROWS_C = 12
LAST_KEPT = 57

E1S, E1R, AS, AR, AFS, FOS, FOR, FCS, FCR, BOS, BOR, BCS, BCR, E2S, E2R, X1S, X1R, DS, DR = range(19)
MR = 19
MS = 22
NSEM = 30


def row_order():
    order = list(range(24)) + [31] + list(range(24, 31)) + list(range(32, 48))
    order += [48, 55] + list(range(49, 55)) + [57, 56]
    return order


def lane_order():
    out = []
    for q in range(4):
        out += [16 * q + i for i in range(16)]
        out += [-16 * q - 16 + i for i in range(16)]
    return out


def split(table):
    high = table.astype(ml_dtypes.bfloat16)
    low = (table - high.astype(np.float64)).astype(ml_dtypes.bfloat16)
    return high, low


def left_table(table):
    high, low = split(table)
    return np.concatenate([high, low, high], axis=1)


def right_table(table):
    high, low = split(table)
    return np.concatenate([high, high, low], axis=0)


def make_tables():
    n = np.arange(N)
    ky = np.array(row_order())
    kz = np.array(lane_order())
    turn = 2.0 * np.pi / N
    angle_y = turn * ((ky[:, None] * n[None, :]) % N)
    forward_y = np.zeros((128, N))
    forward_y[: len(ky)] = np.cos(angle_y)
    forward_y[64 : 64 + len(ky)] = -np.sin(angle_y)
    weight = np.where(ky == 0, 1.0, 2.0)[:, None]
    inverse_y = np.zeros((128, N))
    inverse_y[: len(ky)] = weight * np.cos(angle_y)
    inverse_y[64 : 64 + len(ky)] = -weight * np.sin(angle_y)
    inverse_y = inverse_y.T
    angle_z = turn * ((n[:, None] * kz[None, :]) % N)
    forward_z = np.concatenate([np.cos(angle_z), np.sin(angle_z)], axis=1)
    inverse_z = np.concatenate([np.cos(angle_z.T), np.sin(angle_z.T)], axis=1)
    x = np.concatenate([np.arange(0, N, 2), np.arange(1, N, 2)])
    angle_x = turn * ((n[:, None] * x[None, :]) % N)
    forward_x = np.concatenate([np.cos(angle_x), np.sin(angle_x)], axis=0)
    inverse_x = np.concatenate([np.cos(angle_x.T), np.sin(angle_x.T)], axis=0)
    lanes = np.zeros((N, N))
    lanes[kz % N, np.arange(N)] = 1.0
    return (
        left_table(forward_y),
        right_table(forward_z),
        right_table(inverse_z),
        left_table(inverse_y),
        left_table(forward_x),
        left_table(inverse_x),
        lanes.astype(ml_dtypes.bfloat16),
    )


def dot(a, b):
    return jnp.dot(a, b, preferred_element_type=jnp.float32)


def halves(value):
    high = value.astype(jnp.bfloat16)
    low = (value - high.astype(jnp.float32)).astype(jnp.bfloat16)
    return high, low


def table_times(table, value):
    high, low = halves(value)
    return dot(table, jnp.concatenate([high, high, low], axis=0))


def times_table(value, table):
    high, low = halves(value)
    return dot(jnp.concatenate([high, low, high], axis=1), table)


def lane_ids(rows):
    return lax.broadcasted_iota(jnp.int32, (rows, 128), 1)


def sublane_ids():
    return lax.broadcasted_iota(jnp.int32, (8, 128), 0)


def turn_lanes(value, by):
    return pltpu.roll(value, by % 128, 1)


def quarters(a):
    lane = lane_ids(a[0].shape[0])
    low = lane < 64
    even = (lane // 32) % 2 == 0
    u = [None] * 4
    for k in range(2):
        u[k] = jnp.where(low, a[k], turn_lanes(a[k + 2], 64))
        u[k + 2] = jnp.where(low, turn_lanes(a[k], 64), a[k + 2])
    out = [None] * 4
    for k in (0, 2):
        out[k] = jnp.where(even, u[k], turn_lanes(u[k + 1], 32))
        out[k + 1] = jnp.where(even, turn_lanes(u[k], -32), u[k + 1])
    return out


def to_chunks(q):
    def chunk(g, c):
        return q[g][8 * c : 8 * c + 8]

    sub = sublane_ids()
    mixed_x = jnp.where(sub == 0, chunk(0, 7), chunk(3, 3))
    mixed_y = jnp.where(sub == 1, chunk(0, 7), chunk(1, 6))
    out = [chunk(0, c) for c in range(7)] + [chunk(1, c) for c in range(6)]
    out += [chunk(2, c) for c in range(6)] + [chunk(3, c) for c in range(3)]
    return out + [mixed_x, mixed_y]


def from_chunks(chunks):
    sub = sublane_ids()
    zero = jnp.zeros((8, 128), jnp.float32)
    mixed_x, mixed_y = chunks[22], chunks[23]
    last = jnp.where(sub == 0, mixed_x, jnp.where(sub == 1, mixed_y, zero))
    q0 = chunks[0:7] + [last]
    q1 = chunks[7:13] + [jnp.where(sub == 1, zero, mixed_y), zero]
    q2 = chunks[13:19] + [zero, zero]
    q3 = chunks[19:22] + [jnp.where(sub == 0, zero, mixed_x)] + [zero] * 4
    return [jnp.concatenate(parts, axis=0) for parts in (q0, q1, q2, q3)]


def forward_planes(densities, ty, wz):
    e = table_times(ty, jnp.concatenate(densities, axis=1))
    real, imag = [], []
    for k in range(len(densities)):
        g = times_table(e[:, 128 * k : 128 * k + 128], wz)
        real.append(g[:64, :128] + g[64:, 128:])
        imag.append(g[64:, :128] - g[:64, 128:])
    return real, imag


def inverse_planes(real, imag, wzi, tyi):
    parts = []
    for re, im in zip(real, imag):
        g = times_table(jnp.concatenate([re, im], axis=0), wzi)
        parts.append(
            jnp.concatenate([g[:64, :128] - g[64:, 128:], g[64:, :128] + g[:64, 128:]], axis=0)
        )
    v = table_times(tyi, jnp.concatenate(parts, axis=1))
    return [v[:, 128 * k : 128 * k + 128] for k in range(len(parts))]


def store_chunks(buf, row, chunks):
    for m, value in enumerate(chunks):
        buf[pl.ds((m % 8) * 8 * PITCH + row(m // 8), 8, stride=PITCH), :] = value


def load_chunks(buf, row):
    return [buf[pl.ds((m % 8) * 8 * PITCH + row(m // 8), 8, stride=PITCH), :] for m in range(24)]


def pack_quad(buf, plane, real, imag):
    for ri, part in enumerate((real, imag)):
        store_chunks(buf, lambda j: plane * 6 + j * 2 + ri, to_chunks(quarters(part)))


def unpack_quad(buf, plane):
    return [
        quarters(from_chunks(load_chunks(buf, lambda j: plane * 6 + j * 2 + ri))) for ri in range(2)
    ]


def middle_quad(recv, send, kernel_of, tx, txi):
    blocks = []
    for r in range(6):
        blocks.append(
            jnp.concatenate(
                [recv[pl.ds(plane * 6 + r, 64, stride=PITCH), :] for plane in range(2)], axis=0
            )
        )
    p = table_times(tx, jnp.concatenate(blocks, axis=1))
    c, s = p[:128], p[128:]
    blocks = []
    for j in range(3):
        re, im = slice(256 * j, 256 * j + 128), slice(256 * j + 128, 256 * j + 256)
        blocks.append((c[:, re] + s[:, im]) * kernel_of[j])
        blocks.append((c[:, im] - s[:, re]) * kernel_of[j])
    p = table_times(txi, jnp.concatenate(blocks, axis=1))
    c, s = p[:128], p[128:]
    for j in range(3):
        re, im = slice(256 * j, 256 * j + 128), slice(256 * j + 128, 256 * j + 256)
        new = (c[:, re] - s[:, im], c[:, im] + s[:, re])
        for ri in range(2):
            for plane in range(2):
                send[pl.ds(plane * 6 + j * 2 + ri, 64, stride=PITCH), :] = new[ri][
                    64 * plane : 64 * plane + 64
                ]


def middle_single(recv, send, kernel_of, tx, txi):
    first = lane_ids(128) < 32
    low = lane_ids(64) < 64

    def cross(s):
        return jnp.where(first, turn_lanes(s, -32), -turn_lanes(s, 32))

    blocks = []
    for j in range(3):
        rows = recv[pl.ds(12 + j, 64, stride=PITCH), :]
        blocks.append(jnp.concatenate([rows, turn_lanes(rows, 64)], axis=0))
    p = table_times(tx, jnp.concatenate(blocks, axis=1))
    blocks = []
    for j in range(3):
        at = slice(128 * j, 128 * j + 128)
        blocks.append((p[:128, at] + cross(p[128:, at])) * kernel_of[j])
    p = table_times(txi, jnp.concatenate(blocks, axis=1))
    for j in range(3):
        at = slice(128 * j, 128 * j + 128)
        new = p[:128, at] - cross(p[128:, at])
        send[pl.ds(12 + j, 64, stride=PITCH), :] = jnp.where(
            low, new[:64], turn_lanes(new[64:], 64)
        )


def piece_of(t, j):
    m = j * 8 + t // 8
    sub = t % 8
    q = jnp.where(m < 7, 0, jnp.where(m < 13, 1, jnp.where(m < 19, 2, 3)))
    c = m - jnp.where(m < 7, 0, jnp.where(m < 13, 7, jnp.where(m < 19, 13, 19)))
    is_x = m == 22
    is_y = m == 23
    q = jnp.where(is_y, 1, q)
    c = jnp.where(is_x, 3, jnp.where(is_y, 6, c))
    extra = (is_x & (sub == 0)) | (is_y & (sub == 1))
    q = jnp.where(extra, 0, q)
    c = jnp.where(extra, 7, c)
    pos = c * 8 + sub
    ky = jnp.where((pos >= 25) & (pos <= 31), pos - 1, pos)
    ky = jnp.where((pos >= 50) & (pos <= 55), pos - 1, ky)
    ky = jnp.where(pos == 24, 31, ky)
    ky = jnp.where(pos == 49, 55, ky)
    ky = jnp.where(pos == 56, 57, ky)
    ky = jnp.where(pos == 57, 56, ky)
    return ky, q


def owner_of(ky, q):
    pos = jnp.where((ky >= 24) & (ky <= 30), ky + 1, ky)
    pos = jnp.where((ky >= 49) & (ky <= 54), ky + 1, pos)
    pos = jnp.where(ky == 31, 24, pos)
    pos = jnp.where(ky == 55, 49, pos)
    pos = jnp.where(ky == 57, 56, pos)
    pos = jnp.where(ky == 56, 57, pos)
    c = pos // 8
    sub = pos % 8
    full = jnp.where(q == 0, 7, jnp.where(q == 3, 3, 6))
    base = jnp.where(q == 0, 0, jnp.where(q == 1, 7, jnp.where(q == 2, 13, 19)))
    m = base + c
    m = jnp.where((q == 0) & (c == 7), 22 + sub, m)
    m = jnp.where((q == 1) & (c == 6), 23, m)
    m = jnp.where((q == 3) & (c == 3), 22, m)
    exists = (
        (c < full)
        | ((q == 0) & (c == 7))
        | ((q == 1) & (c == 6) & (sub != 1))
        | ((q == 3) & (c == 3) & (sub != 0))
    ) & (ky <= LAST_KEPT)
    m = jnp.where(exists, m, 0)
    return exists, (m % 8) * 8 + sub, m // 8


def kernel_table(mask, ky, q):
    lane = lane_ids(32)
    rows = []
    for block in range(4):
        part = jnp.where(lane // 32 == block, mask, 0.0)
        part = part + turn_lanes(part, 64)
        rows.append(part + turn_lanes(part, 32))
    kept = jnp.concatenate(rows, axis=0)
    kx = lax.broadcasted_iota(jnp.int32, (128, 128), 0)
    kx = jnp.where(kx < 64, kx, kx - 128)
    i = lane_ids(128) % 32
    kz = jnp.where(i < 16, 16 * q + i, i - 32 - 16 * q)
    squared = kx * kx + ky * ky + kz * kz
    safe = jnp.maximum(squared, 1).astype(jnp.float32)
    return jnp.where(squared > 0, (8.0 * math.pi / N**3) / safe, 0.0) * kept


def body(
    occ, orb, kept, ty, wz, wzi, tyi, tx, txi, lanes, out,
    v, w, x1, pvr, df, act, pv, pf, mask_send, mask_recv,
    f_so, f_ro, b_so, b_ro, f_sc, f_rc, b_sc, b_rc, sem, sem_x, sem_y,
):
    b = lax.axis_index("band")
    g = lax.axis_index("grid")
    half = b // 2
    core = b % 2
    other_core = half * 2 + (1 - core)
    other_half = (1 - half) * 2 + core
    ty, wz, wzi, tyi, tx, txi = (r[...] for r in (ty, wz, wzi, tyi, tx, txi))

    def on_line(stride, k):
        digit = (g // stride) % 4
        return g + ((digit + k) % 4 - digit) * stride

    barrier = pltpu.get_barrier_semaphore()
    for partner in (other_core, other_half):
        pl.semaphore_signal(barrier, inc=1, device_id={"band": partner}, device_id_type=MESH)
    for stride in (1, 4, 16):
        for k in range(1, 4):
            pl.semaphore_signal(
                barrier, inc=1, device_id={"grid": on_line(stride, k)}, device_id_type=MESH
            )
    pl.semaphore_wait(barrier, 11)

    def remote(src, dst, send, recv, band=None, grid=None):
        device = {"band": b if band is None else band, "grid": g if grid is None else grid}
        return pltpu.make_async_remote_copy(
            src_ref=src, dst_ref=dst, send_sem=sem.at[send], recv_sem=sem.at[recv],
            device_id=device, device_id_type=MESH,
        )

    to_core = remote(orb, v, E1S, E1R, band=other_core)
    to_core.start()
    to_half = remote(orb, w, AS, AR, band=other_half)

    @pl.when((half == 0) | (core == 0))
    def _():
        to_half.start()

    for k in range(1, 4):
        pl.semaphore_signal(sem_x, inc=1, device_id={"grid": on_line(4, k)}, device_id_type=MESH)
    pl.semaphore_wait(sem_x, 3)
    for k in range(1, 4):
        pl.semaphore_signal(sem_y, inc=1, device_id={"grid": on_line(16, k)}, device_id_type=MESH)

    for row in range(2):
        plane = dot(kept[:, row, :].astype(jnp.float32).astype(jnp.bfloat16), lanes[...])
        groups = quarters([plane[32 * k : 32 * k + 32] for k in range(4)])
        for q in range(4):
            mask_send[row * 4 + q] = groups[q]
    pl.semaphore_wait(sem_y, 3)

    def mask_copies(act_on_remote, act_on_local):
        def one(i, carry):
            exists, t, j = owner_of(2 * g + i // 4, i % 4)

            @pl.when(exists & (t != g))
            def _():
                act_on_remote(
                    pltpu.make_async_remote_copy(
                        src_ref=mask_send.at[i], dst_ref=mask_recv.at[j],
                        send_sem=sem.at[MS + i], recv_sem=sem.at[MR + j],
                        device_id={"grid": t}, device_id_type=MESH,
                    )
                )

            if act_on_local is not None:

                @pl.when(exists & (t == g))
                def _():
                    act_on_local(
                        pltpu.make_async_copy(mask_send.at[i], mask_recv.at[j], sem.at[MR + j])
                    )

            return carry

        lax.fori_loop(0, 8, one, 0)

    mask_copies(lambda c: c.start(), lambda c: c.start())

    def slot(t, rows):
        return pl.ds(pl.multiple_of(t * PITCH, PITCH), rows)

    def exchange(src, dst, rows, send, recv):
        def one(k, carry):
            t = lax.rem(g + k, PEERS)
            remote(src.at[slot(t, rows)], dst.at[slot(g, rows)], send, recv, grid=t).start()
            return carry

        lax.fori_loop(1, PEERS, one, 0)
        pltpu.make_async_copy(src.at[slot(g, rows)], dst.at[slot(g, rows)], sem.at[recv]).start()

    def arrived(dst, rows, recv):
        whole = dst.at[pl.ds(0, PEERS * rows)]
        pltpu.make_async_copy(whole, whole, sem.at[recv]).wait()

    def sent(src, rows, send):
        whole = src.at[pl.ds(0, (PEERS - 1) * rows)]
        pltpu.make_async_copy(whole, whole, sem.at[send]).wait()

    u = orb
    v0, v1 = core, 1 - core

    to_core.wait_recv()
    for p in range(2):
        d = [u[0, p] * u[0, p], u[0, p] * u[1, p], u[1, p] * u[1, p], u[0, p] * v[v0, p]]
        pack_quad(f_so, p, *forward_planes(d, ty, wz))
    real, imag = forward_planes([u[1, p] * v[v1, p] for p in range(2)], ty, wz)
    store_chunks(f_so, lambda j: 12 + j, to_chunks(quarters([real[0], imag[0], real[1], imag[1]])))
    exchange(f_so, f_ro, ROWS_O, FOS, FOR)

    for j in range(3):
        pltpu.make_async_copy(mask_recv.at[j], mask_recv.at[j], sem.at[MR + j]).wait()
    kernel_of = [kernel_table(mask_recv[j], *piece_of(g, j)) for j in range(3)]

    arrival = pltpu.make_async_copy(w, w, sem.at[AR])
    arrival.wait()
    forward_w = remote(w, w, AFS, AR, band=other_core)

    @pl.when((half == 0) & (core == 0))
    def _():
        forward_w.start()

    near_is_v = (half == 1) & (core == 0)

    def near(i, p):
        return jnp.where(near_is_v, v[i, p], u[i, p])

    for p in range(2):
        d = [near(i, p) * w[j, p] for i in range(2) for j in range(2)]
        pack_quad(f_sc, p, *forward_planes(d, ty, wz))
    exchange(f_sc, f_rc, ROWS_C, FCS, FCR)

    arrived(f_ro, ROWS_O, FOR)
    middle_quad(f_ro, b_so, kernel_of, tx, txi)
    middle_single(f_ro, b_so, kernel_of, tx, txi)
    exchange(b_so, b_ro, ROWS_O, BOS, BOR)
    arrived(f_rc, ROWS_C, FCR)
    middle_quad(f_rc, b_sc, kernel_of, tx, txi)
    exchange(b_sc, b_rc, ROWS_C, BCS, BCR)

    mine = half * 4 + core * 2
    theirs = half * 4 + (1 - core) * 2
    far = (1 - half) * 4 + half * 2 * core
    close = jnp.where(near_is_v, theirs, mine)
    arrived(b_ro, ROWS_O, BOR)
    q = quarters(from_chunks(load_chunks(b_ro, lambda j: 12 + j)))
    lone = inverse_planes([q[0], q[2]], [q[1], q[3]], wzi, tyi)
    for p in range(2):
        pot = inverse_planes(*unpack_quad(b_ro, p), wzi, tyi)
        u0, u1 = u[0, p], u[1, p]
        o0, o1 = occ[mine] * u0, occ[mine + 1] * u1
        act[0, p] = o0 * pot[0] + o1 * pot[1] + occ[theirs + v0] * v[v0, p] * pot[3]
        act[1, p] = o0 * pot[1] + o1 * pot[2] + occ[theirs + v1] * v[v1, p] * lone[p]
        pv[v0, p] = o0 * pot[3]
        pv[v1, p] = o1 * lone[p]

    arrived(b_rc, ROWS_C, BCR)
    for p in range(2):
        pot = inverse_planes(*unpack_quad(b_rc, p), wzi, tyi)
        n0, n1 = near(0, p), near(1, p)
        f0, f1 = occ[far] * w[0, p], occ[far + 1] * w[1, p]
        pf[0, p] = occ[close] * n0 * pot[0] + occ[close + 1] * n1 * pot[2]
        pf[1, p] = occ[close] * n0 * pot[1] + occ[close + 1] * n1 * pot[3]
        for i in range(2):
            term = f0 * pot[2 * i] + f1 * pot[2 * i + 1]
            act[i, p] += jnp.where(near_is_v, 0.0, term)
            pv[i, p] += jnp.where(near_is_v, term, 0.0)

    swap = remote(pv, pvr, E2S, E2R, band=other_core)
    swap.start()
    merge = remote(pf, x1, X1S, X1R, band=other_core)
    home = remote(pf, df, DS, DR, band=other_half)

    @pl.when((half == 0) & (core == 1))
    def _():
        merge.start()

    @pl.when((half == 0) & (core == 0))
    def _():
        merge.wait_recv()
        pf[...] += x1[...]

    @pl.when((half == 1) | (core == 0))
    def _():
        home.start()

    swap.wait_recv()
    for i in range(2):
        for p in range(2):
            act[i, p] += pvr[i, p]

    @pl.when((half == 0) | (core == 0))
    def _():
        home.wait_recv()
        out[...] = -(act[...] + df[...])

    @pl.when((half == 1) & (core == 1))
    def _():
        out[...] = -act[...]

    to_core.wait_send()

    @pl.when((half == 0) | (core == 0))
    def _():
        to_half.wait_send()

    @pl.when((half == 0) & (core == 0))
    def _():
        forward_w.wait_send()

    mask_copies(lambda c: c.wait_send(), None)
    sent(f_so, ROWS_O, FOS)
    sent(f_sc, ROWS_C, FCS)
    sent(b_so, ROWS_O, BOS)
    sent(b_sc, ROWS_C, BCS)
    swap.wait_send()

    @pl.when((half == 0) & (core == 1))
    def _():
        merge.wait_send()

    @pl.when((half == 1) | (core == 0))
    def _():
        home.wait_send()


def on_device(orbitals, occupation, kept_modes):
    block = pltpu.VMEM((2, 2, N, N), jnp.float32)
    message = pltpu.VMEM((PEERS * PITCH, 128), jnp.float32)
    whole = pl.BlockSpec(memory_space=pltpu.VMEM)
    return pl.pallas_call(
        body,
        out_shape=jax.ShapeDtypeStruct(orbitals.shape, jnp.float32),
        in_specs=[pl.BlockSpec(memory_space=pltpu.SMEM)] + [whole] * 9,
        out_specs=whole,
        scratch_shapes=[block] * 8
        + [pltpu.VMEM((8, 32, 128), jnp.float32), pltpu.VMEM((3, 32, 128), jnp.float32)]
        + [message] * 8
        + [
            pltpu.SemaphoreType.DMA((NSEM,)),
            pltpu.SemaphoreType.REGULAR,
            pltpu.SemaphoreType.REGULAR,
        ],
        compiler_params=pltpu.CompilerParams(
            collective_id=1, has_side_effects=True, vmem_limit_bytes=48 << 20
        ),
        name="exchange",
    )(occupation, orbitals, kept_modes, *(jnp.asarray(t) for t in make_tables()))


def solution(mesh):
    return jax.shard_map(
        on_device,
        mesh=mesh,
        in_specs=(P("band", "grid", None, None), P(), P(None, "grid", None)),
        out_specs=P("band", "grid", None, None),
        check_vma=False,
    )
```

```python
import functools
import math

import jax
import jax.numpy as jnp
import ml_dtypes
import numpy as np
from jax import lax
from jax.experimental import pallas as pl
from jax.experimental.pallas import tpu as pltpu
from jax.sharding import PartitionSpec as P

MESH = pl.DeviceIdType.MESH
N = 128
PEERS = 64
PITCH_O = 16
ROWS_O = 15
PITCH_C = 8
ROWS_C = 6
LAST_KEPT = 57

E1S, E1R, AS, AR, FOS, FOR, FCS, FCR, BOS, BOR, BCS, BCR = range(12)
E2S, E2R, E3S, E3R, X1S, X1R, DS, DR, MFS, MFR = range(12, 22)
MR = 22
MS = 25
LS = 33
NSEM = 42


def row_order():
    order = list(range(24)) + [31] + list(range(24, 31)) + list(range(32, 48))
    order += [48, 55] + list(range(49, 55)) + [57, 56]
    return order


def lane_order():
    out = []
    for q in range(4):
        out += [16 * q + i for i in range(16)]
        out += [-16 * q - 16 + i for i in range(16)]
    return out


def split(table):
    high = table.astype(ml_dtypes.bfloat16)
    low = (table - high.astype(np.float64)).astype(ml_dtypes.bfloat16)
    return high, low


def left_table(table):
    high, low = split(table)
    return np.concatenate([high, low, high], axis=1)


def right_table(table):
    high, low = split(table)
    return np.concatenate([high, high, low], axis=0)


def make_tables():
    n = np.arange(N)
    ky = np.array(row_order())
    kz = np.array(lane_order())
    turn = 2.0 * np.pi / N
    angle_y = turn * ((ky[:, None] * n[None, :]) % N)
    forward_y = np.zeros((128, N))
    forward_y[: len(ky)] = np.cos(angle_y)
    forward_y[64 : 64 + len(ky)] = -np.sin(angle_y)
    weight = np.where(ky == 0, 1.0, 2.0)[:, None]
    inverse_y = np.zeros((128, N))
    inverse_y[: len(ky)] = weight * np.cos(angle_y)
    inverse_y[64 : 64 + len(ky)] = -weight * np.sin(angle_y)
    inverse_y = inverse_y.T
    angle_z = turn * ((n[:, None] * kz[None, :]) % N)
    forward_z = np.concatenate([np.cos(angle_z), np.sin(angle_z)], axis=1)
    inverse_z = np.concatenate([np.cos(angle_z.T), np.sin(angle_z.T)], axis=1)
    x = np.concatenate([np.arange(0, N, 2), np.arange(1, N, 2)])
    angle_x = turn * ((n[:, None] * x[None, :]) % N)
    forward_x = np.concatenate([np.cos(angle_x), np.sin(angle_x)], axis=0)
    inverse_x = np.concatenate([np.cos(angle_x.T), np.sin(angle_x.T)], axis=0)
    lanes = np.zeros((N, N))
    lanes[kz % N, np.arange(N)] = 1.0
    return (
        left_table(forward_y),
        right_table(forward_z),
        right_table(inverse_z),
        left_table(inverse_y),
        left_table(forward_x),
        left_table(inverse_x),
        lanes.astype(ml_dtypes.bfloat16),
    )


def dot(a, b):
    return jnp.dot(a, b, preferred_element_type=jnp.float32)


def halves(value):
    high = value.astype(jnp.bfloat16)
    low = (value - high.astype(jnp.float32)).astype(jnp.bfloat16)
    return high, low


def table_times(table, value):
    high, low = halves(value)
    return dot(table, jnp.concatenate([high, high, low], axis=0))


def times_table(value, table):
    high, low = halves(value)
    return dot(jnp.concatenate([high, low, high], axis=1), table)


def lane_ids(rows):
    return lax.broadcasted_iota(jnp.int32, (rows, 128), 1)


def sublane_ids():
    return lax.broadcasted_iota(jnp.int32, (8, 128), 0)


def turn_lanes(value, by):
    return pltpu.roll(value, by % 128, 1)


def quarters(a):
    lane = lane_ids(a[0].shape[0])
    low = lane < 64
    even = (lane // 32) % 2 == 0
    u = [None] * 4
    for k in range(2):
        u[k] = jnp.where(low, a[k], turn_lanes(a[k + 2], 64))
        u[k + 2] = jnp.where(low, turn_lanes(a[k], 64), a[k + 2])
    out = [None] * 4
    for k in (0, 2):
        out[k] = jnp.where(even, u[k], turn_lanes(u[k + 1], 32))
        out[k + 1] = jnp.where(even, turn_lanes(u[k], -32), u[k + 1])
    return out


def to_chunks(q):
    def chunk(g, c):
        return q[g][8 * c : 8 * c + 8]

    sub = sublane_ids()
    mixed_x = jnp.where(sub == 0, chunk(0, 7), chunk(3, 3))
    mixed_y = jnp.where(sub == 1, chunk(0, 7), chunk(1, 6))
    out = [chunk(0, c) for c in range(7)] + [chunk(1, c) for c in range(6)]
    out += [chunk(2, c) for c in range(6)] + [chunk(3, c) for c in range(3)]
    return out + [mixed_x, mixed_y]


def from_chunks(chunks):
    sub = sublane_ids()
    zero = jnp.zeros((8, 128), jnp.float32)
    mixed_x, mixed_y = chunks[22], chunks[23]
    last = jnp.where(sub == 0, mixed_x, jnp.where(sub == 1, mixed_y, zero))
    q0 = chunks[0:7] + [last]
    q1 = chunks[7:13] + [jnp.where(sub == 1, zero, mixed_y), zero]
    q2 = chunks[13:19] + [zero, zero]
    q3 = chunks[19:22] + [jnp.where(sub == 0, zero, mixed_x)] + [zero] * 4
    return [jnp.concatenate(parts, axis=0) for parts in (q0, q1, q2, q3)]


def forward_planes(densities, ty, wz):
    e = table_times(ty, jnp.concatenate(densities, axis=1))
    real, imag = [], []
    for k in range(len(densities)):
        g = times_table(e[:, 128 * k : 128 * k + 128], wz)
        real.append(g[:64, :128] + g[64:, 128:])
        imag.append(g[64:, :128] - g[:64, 128:])
    return real, imag


def inverse_planes(real, imag, wzi, tyi):
    parts = []
    for re, im in zip(real, imag):
        g = times_table(jnp.concatenate([re, im], axis=0), wzi)
        parts.append(
            jnp.concatenate([g[:64, :128] - g[64:, 128:], g[64:, :128] + g[:64, 128:]], axis=0)
        )
    v = table_times(tyi, jnp.concatenate(parts, axis=1))
    return [v[:, 128 * k : 128 * k + 128] for k in range(len(parts))]


def store_chunks(buf, pitch, row, chunks):
    for m, value in enumerate(chunks):
        buf[pl.ds((m % 8) * 8 * pitch + row(m // 8), 8, stride=pitch), :] = value


def load_chunks(buf, pitch, row):
    return [buf[pl.ds((m % 8) * 8 * pitch + row(m // 8), 8, stride=pitch), :] for m in range(24)]


def pack_quad(buf, pitch, first, real, imag):
    for ri, part in enumerate((real, imag)):
        store_chunks(buf, pitch, lambda j: first + j * 2 + ri, to_chunks(quarters(part)))


def unpack_quad(buf, pitch, first):
    return [
        quarters(from_chunks(load_chunks(buf, pitch, lambda j: first + j * 2 + ri)))
        for ri in range(2)
    ]


def middle_quad(recv, send, pitch, second, kernel_of, tx, txi):
    blocks = []
    for r in range(6):
        blocks.append(
            jnp.concatenate(
                [recv[pl.ds(plane * second + r, 64, stride=pitch), :] for plane in range(2)], axis=0
            )
        )
    p = table_times(tx, jnp.concatenate(blocks, axis=1))
    c, s = p[:128], p[128:]
    blocks = []
    for j in range(3):
        re, im = slice(256 * j, 256 * j + 128), slice(256 * j + 128, 256 * j + 256)
        blocks.append((c[:, re] + s[:, im]) * kernel_of[j])
        blocks.append((c[:, im] - s[:, re]) * kernel_of[j])
    p = table_times(txi, jnp.concatenate(blocks, axis=1))
    c, s = p[:128], p[128:]
    for j in range(3):
        re, im = slice(256 * j, 256 * j + 128), slice(256 * j + 128, 256 * j + 256)
        new = (c[:, re] - s[:, im], c[:, im] + s[:, re])
        for ri in range(2):
            for plane in range(2):
                send[pl.ds(plane * second + j * 2 + ri, 64, stride=pitch), :] = new[ri][
                    64 * plane : 64 * plane + 64
                ]


def middle_single(recv, send, pitch, kernel_of, tx, txi):
    first = lane_ids(128) < 32
    low = lane_ids(64) < 64

    def cross(s):
        return jnp.where(first, turn_lanes(s, -32), -turn_lanes(s, 32))

    blocks = []
    for j in range(3):
        rows = recv[pl.ds(12 + j, 64, stride=pitch), :]
        blocks.append(jnp.concatenate([rows, turn_lanes(rows, 64)], axis=0))
    p = table_times(tx, jnp.concatenate(blocks, axis=1))
    blocks = []
    for j in range(3):
        at = slice(128 * j, 128 * j + 128)
        blocks.append((p[:128, at] + cross(p[128:, at])) * kernel_of[j])
    p = table_times(txi, jnp.concatenate(blocks, axis=1))
    for j in range(3):
        at = slice(128 * j, 128 * j + 128)
        new = p[:128, at] - cross(p[128:, at])
        send[pl.ds(12 + j, 64, stride=pitch), :] = jnp.where(
            low, new[:64], turn_lanes(new[64:], 64)
        )


def piece_of(t, j):
    m = j * 8 + t // 8
    sub = t % 8
    q = jnp.where(m < 7, 0, jnp.where(m < 13, 1, jnp.where(m < 19, 2, 3)))
    c = m - jnp.where(m < 7, 0, jnp.where(m < 13, 7, jnp.where(m < 19, 13, 19)))
    is_x = m == 22
    is_y = m == 23
    q = jnp.where(is_y, 1, q)
    c = jnp.where(is_x, 3, jnp.where(is_y, 6, c))
    extra = (is_x & (sub == 0)) | (is_y & (sub == 1))
    q = jnp.where(extra, 0, q)
    c = jnp.where(extra, 7, c)
    pos = c * 8 + sub
    ky = jnp.where((pos >= 25) & (pos <= 31), pos - 1, pos)
    ky = jnp.where((pos >= 50) & (pos <= 55), pos - 1, ky)
    ky = jnp.where(pos == 24, 31, ky)
    ky = jnp.where(pos == 49, 55, ky)
    ky = jnp.where(pos == 56, 57, ky)
    ky = jnp.where(pos == 57, 56, ky)
    return ky, q


def owner_of(ky, q):
    pos = jnp.where((ky >= 24) & (ky <= 30), ky + 1, ky)
    pos = jnp.where((ky >= 49) & (ky <= 54), ky + 1, pos)
    pos = jnp.where(ky == 31, 24, pos)
    pos = jnp.where(ky == 55, 49, pos)
    pos = jnp.where(ky == 57, 56, pos)
    pos = jnp.where(ky == 56, 57, pos)
    c = pos // 8
    sub = pos % 8
    full = jnp.where(q == 0, 7, jnp.where(q == 3, 3, 6))
    base = jnp.where(q == 0, 0, jnp.where(q == 1, 7, jnp.where(q == 2, 13, 19)))
    m = base + c
    m = jnp.where((q == 0) & (c == 7), 22 + sub, m)
    m = jnp.where((q == 1) & (c == 6), 23, m)
    m = jnp.where((q == 3) & (c == 3), 22, m)
    exists = (
        (c < full)
        | ((q == 0) & (c == 7))
        | ((q == 1) & (c == 6) & (sub != 1))
        | ((q == 3) & (c == 3) & (sub != 0))
    ) & (ky <= LAST_KEPT)
    m = jnp.where(exists, m, 0)
    return exists, (m % 8) * 8 + sub, m // 8


def kernel_table(mask, ky, q):
    lane = lane_ids(32)
    rows = []
    for block in range(4):
        part = jnp.where(lane // 32 == block, mask, 0.0)
        part = part + turn_lanes(part, 64)
        rows.append(part + turn_lanes(part, 32))
    kept = jnp.concatenate(rows, axis=0)
    kx = lax.broadcasted_iota(jnp.int32, (128, 128), 0)
    kx = jnp.where(kx < 64, kx, kx - 128)
    i = lane_ids(128) % 32
    kz = jnp.where(i < 16, 16 * q + i, i - 32 - 16 * q)
    squared = kx * kx + ky * ky + kz * kz
    safe = jnp.maximum(squared, 1).astype(jnp.float32)
    return jnp.where(squared > 0, (8.0 * math.pi / N**3) / safe, 0.0) * kept


def body(
    occ, orb_in, kept_in, ty_in, wz_in, wzi_in, tyi_in, tx_in, txi_in, lanes_in, out,
    chip, kept, ty, wz, wzi, tyi, tx, txi, lanes, far, pvr, df, merged, acc, pf, mask_send, mask_recv,
    f_so, f_ro, b_so, b_ro, f_sc, f_rc, b_sc, b_rc, sem, sem_x, sem_y,
):
    b = lax.axis_index("band")
    g = lax.axis_index("grid")
    half = b // 2
    core = b % 2
    other_core = half * 2 + (1 - core)
    other_half = (1 - half) * 2 + core

    u, v = chip.at[0], chip.at[1]
    act, pv = acc.at[0], acc.at[1]
    loads = [
        pltpu.make_async_copy(source, target, sem.at[LS + i])
        for i, (source, target) in enumerate(
            [
                (orb_in, u), (ty_in, ty), (wz_in, wz), (kept_in, kept), (lanes_in, lanes),
                (tx_in, tx), (txi_in, txi), (wzi_in, wzi), (tyi_in, tyi),
            ]
        )
    ]
    for load in loads:
        load.start()

    def on_line(stride, k):
        digit = (g // stride) % 4
        return g + ((digit + k) % 4 - digit) * stride

    barrier = pltpu.get_barrier_semaphore()

    def greet(semaphore, band, grid):
        pl.semaphore_signal(
            semaphore, inc=1, device_id={"band": band, "grid": grid}, device_id_type=MESH
        )

    for k in range(4):
        greet(barrier, other_half, on_line(1, k))
    for stride in (1, 4, 16):
        for k in range(1, 4):
            greet(barrier, b, on_line(stride, k))
    greet(barrier, other_core, g)

    def remote(src, dst, send, recv, band=None, grid=None):
        device = {"band": b if band is None else band, "grid": g if grid is None else grid}
        return pltpu.make_async_remote_copy(
            src_ref=src, dst_ref=dst, send_sem=sem.at[send], recv_sem=sem.at[recv],
            device_id=device, device_id_type=MESH,
        )

    for load in loads[:3]:
        load.wait()
    ty, wz = ty[...], wz[...]
    own = [
        forward_planes([u[0, p] * u[0, p], u[0, p] * u[1, p], u[1, p] * u[1, p]], ty, wz)
        for p in range(2)
    ]

    pl.semaphore_wait(barrier, 14)
    to_core = remote(u, v, E1S, E1R, band=other_core)
    to_core.start()
    to_half = remote(u.at[:, 1 - half], far.at[0], AS, AR, band=other_half)
    to_half.start()
    for k in range(1, 4):
        greet(sem_x, b, on_line(4, k))

    for load in loads[3:]:
        load.wait()
    tx, txi, wzi, tyi = tx[...], txi[...], wzi[...], tyi[...]
    for row in range(2):
        plane = dot(kept[:, row, :].astype(jnp.float32).astype(jnp.bfloat16), lanes[...])
        groups = quarters([plane[32 * k : 32 * k + 32] for k in range(4)])
        for q in range(4):
            mask_send[row * 4 + q] = groups[q]
    pl.semaphore_wait(sem_x, 3)
    for k in range(1, 4):
        greet(sem_y, b, on_line(16, k))

    v0, v1 = core, 1 - core
    to_core.wait_recv()
    real, imag = forward_planes(
        [u[0, p] * v[v0, p] for p in range(2)] + [u[1, p] * v[v1, p] for p in range(2)], ty, wz
    )
    for p in range(2):
        pack_quad(f_so, PITCH_O, p * 6, own[p][0] + [real[p]], own[p][1] + [imag[p]])
    lone = quarters([real[2], imag[2], real[3], imag[3]])
    store_chunks(f_so, PITCH_O, lambda j: 12 + j, to_chunks(lone))
    pl.semaphore_wait(sem_y, 3)

    def mask_copies(act_on_remote, act_on_local):
        def one(i, carry):
            exists, t, j = owner_of(2 * g + i // 4, i % 4)

            @pl.when(exists & (t != g))
            def _():
                act_on_remote(
                    pltpu.make_async_remote_copy(
                        src_ref=mask_send.at[i], dst_ref=mask_recv.at[j],
                        send_sem=sem.at[MS + i], recv_sem=sem.at[MR + j],
                        device_id={"band": b, "grid": t}, device_id_type=MESH,
                    )
                )

            if act_on_local is not None:

                @pl.when(exists & (t == g))
                def _():
                    act_on_local(
                        pltpu.make_async_copy(mask_send.at[i], mask_recv.at[j], sem.at[MR + j])
                    )

            return carry

        lax.fori_loop(0, 8, one, 0)

    mask_to_core = remote(mask_recv, mask_recv, MFS, MFR, band=other_core)

    @pl.when(core == 0)
    def _():
        mask_copies(lambda c: c.start(), lambda c: c.start())

    def slot(index, pitch, rows):
        return pl.ds(pl.multiple_of(index * pitch, pitch), rows)

    def exchange_own(src, dst, send, recv):
        def one(k, carry):
            t = lax.rem(g + k, PEERS)
            remote(
                src.at[slot(t, PITCH_O, ROWS_O)], dst.at[slot(g, PITCH_O, ROWS_O)], send, recv, grid=t
            ).start()
            return carry

        lax.fori_loop(1, PEERS, one, 0)
        me = slot(g, PITCH_O, ROWS_O)
        pltpu.make_async_copy(src.at[me], dst.at[me], sem.at[recv]).start()

    def exchange_cross(src, dst, send, recv):
        index = half * PEERS + g
        me = slot(index, PITCH_C, ROWS_C)

        def one(k, carry):
            t = lax.rem(index + k, 2 * PEERS)
            remote(
                src.at[slot(t, PITCH_C, ROWS_C)], dst.at[me], send, recv,
                band=(t // PEERS) * 2 + core, grid=t % PEERS,
            ).start()
            return carry

        lax.fori_loop(1, 2 * PEERS, one, 0)
        pltpu.make_async_copy(src.at[me], dst.at[me], sem.at[recv]).start()

    def arrived(dst, rows, recv):
        whole = dst.at[pl.ds(0, rows)]
        pltpu.make_async_copy(whole, whole, sem.at[recv]).wait()

    exchange_own(f_so, f_ro, FOS, FOR)

    @pl.when(core == 0)
    def _():
        for j in range(3):
            pltpu.make_async_copy(mask_recv.at[j], mask_recv.at[j], sem.at[MR + j]).wait()
        mask_to_core.start()

    @pl.when(core == 1)
    def _():
        mask_to_core.wait_recv()

    kernel_of = [kernel_table(mask_recv[j], *piece_of(g, j)) for j in range(3)]

    first_quad = half * core
    quads = ((first_quad, 0, core), (1 - first_quad, 1, 1 - core))

    def pack_cross(quad, f, n):
        near = [chip[n, i, half] for i in (0, half, 1 - half, 1)]
        d = [a * far[f, i] for a, i in zip(near, (0, 1 - half, half, 1))]
        pack_quad(f_sc, PITCH_C, quad * (PEERS * PITCH_C), *forward_planes(d, ty, wz))

    to_half.wait_recv()
    far_to_core = remote(far.at[0], far.at[1], E3S, E3R, band=other_core)
    far_to_core.start()
    pack_cross(*quads[0])
    far_to_core.wait_recv()
    pack_cross(*quads[1])
    exchange_cross(f_sc, f_rc, FCS, FCR)

    arrived(f_ro, PEERS * ROWS_O, FOR)
    middle_quad(f_ro, b_so, PITCH_O, 6, kernel_of, tx, txi)
    middle_single(f_ro, b_so, PITCH_O, kernel_of, tx, txi)
    exchange_own(b_so, b_ro, BOS, BOR)
    arrived(f_rc, 2 * PEERS * ROWS_C, FCR)
    middle_quad(f_rc, b_sc, PITCH_C, PEERS * PITCH_C, kernel_of, tx, txi)
    exchange_cross(b_sc, b_rc, BCS, BCR)

    mine = half * 4 + core * 2
    theirs = half * 4 + (1 - core) * 2
    arrived(b_ro, PEERS * ROWS_O, BOR)
    q = quarters(from_chunks(load_chunks(b_ro, PITCH_O, lambda j: 12 + j)))
    lone = inverse_planes([q[0], q[2]], [q[1], q[3]], wzi, tyi)
    for p in range(2):
        pot = inverse_planes(*unpack_quad(b_ro, PITCH_O, p * 6), wzi, tyi)
        u0, u1 = u[0, p], u[1, p]
        o0, o1 = occ[mine] * u0, occ[mine + 1] * u1
        act[0, p] = o0 * pot[0] + o1 * pot[1] + occ[theirs + v0] * v[v0, p] * pot[3]
        act[1, p] = o0 * pot[1] + o1 * pot[2] + occ[theirs + v1] * v[v1, p] * lone[p]
        pv[v0, p] = o0 * pot[3]
        pv[v1, p] = o1 * lone[p]

    arrived(b_rc, 2 * PEERS * ROWS_C, BCR)

    def cross_terms(quad, f, n):
        first = quad * (PEERS * PITCH_C)
        p00, p01, p10, p11 = inverse_planes(*unpack_quad(b_rc, PITCH_C, first), wzi, tyi)
        p01, p10 = jnp.where(half == 0, p01, p10), jnp.where(half == 0, p10, p01)
        here = half * 4 + jnp.where(n == 0, core, 1 - core) * 2
        there = (1 - half) * 4 + (core if f == 0 else 1 - core) * 2
        n0, n1 = occ[here] * chip[n, 0, half], occ[here + 1] * chip[n, 1, half]
        f0, f1 = occ[there] * far[f, 0], occ[there + 1] * far[f, 1]
        pf[f, 0] = n0 * p00 + n1 * p10
        pf[f, 1] = n0 * p01 + n1 * p11
        acc[n, 0, half] += f0 * p00 + f1 * p01
        acc[n, 1, half] += f0 * p10 + f1 * p11

    cross_terms(*quads[1])
    merge = remote(pf.at[1], merged, X1S, X1R, band=other_core)
    merge.start()
    cross_terms(*quads[0])
    merge.wait_recv()
    pf[0] += merged[...]
    home = remote(pf.at[0], df, DS, DR, band=other_half)
    home.start()
    swap = remote(pv, pvr, E2S, E2R, band=other_core)
    swap.start()
    swap.wait_recv()
    for i in range(2):
        out[i, half] = -(act[i, half] + pvr[i, half])
        acc[0, i, 1 - half] += pvr[i, 1 - half]
    home.wait_recv()
    for i in range(2):
        out[i, 1 - half] = -(act[i, 1 - half] + df[i])

    to_core.wait_send()
    to_half.wait_send()

    @pl.when(core == 0)
    def _():
        mask_to_core.wait_send()
        mask_copies(lambda c: c.wait_send(), None)

    for src, rows, send in (
        (f_so, (PEERS - 1) * ROWS_O, FOS),
        (f_sc, (2 * PEERS - 1) * ROWS_C, FCS),
        (b_so, (PEERS - 1) * ROWS_O, BOS),
        (b_sc, (2 * PEERS - 1) * ROWS_C, BCS),
    ):
        arrived(src, rows, send)
    far_to_core.wait_send()
    merge.wait_send()
    swap.wait_send()
    home.wait_send()


def on_device(orbitals, occupation, kept_modes):
    block = pltpu.VMEM((2, 2, N, N), jnp.float32)
    twice = pltpu.VMEM((2, 2, 2, N, N), jnp.float32)
    plane = pltpu.VMEM((2, N, N), jnp.float32)
    planes = pltpu.VMEM((2, 2, N, N), jnp.float32)
    message = pltpu.VMEM((PEERS * PITCH_O, 128), jnp.float32)
    tables = make_tables()
    loaded = [twice, pltpu.VMEM(kept_modes.shape, jnp.int32)]
    loaded += [pltpu.VMEM(t.shape, jnp.bfloat16) for t in tables]
    return pl.pallas_call(
        body,
        out_shape=jax.ShapeDtypeStruct(orbitals.shape, jnp.float32),
        in_specs=[pl.BlockSpec(memory_space=pltpu.SMEM)] + [pl.BlockSpec(memory_space=pl.ANY)] * 9,
        out_specs=pl.BlockSpec(memory_space=pltpu.VMEM),
        scratch_shapes=loaded
        + [planes, block, plane, plane, twice, planes]
        + [pltpu.VMEM((8, 32, 128), jnp.float32), pltpu.VMEM((3, 32, 128), jnp.float32)]
        + [message] * 8
        + [
            pltpu.SemaphoreType.DMA((NSEM,)),
            pltpu.SemaphoreType.REGULAR,
            pltpu.SemaphoreType.REGULAR,
        ],
        compiler_params=pltpu.CompilerParams(
            collective_id=1, has_side_effects=True, vmem_limit_bytes=60 << 20
        ),
        name="exchange",
    )(occupation, orbitals, kept_modes, *(jnp.asarray(t) for t in tables))


def solution(mesh):
    return jax.shard_map(
        on_device,
        mesh=mesh,
        in_specs=(P("band", "grid", None, None), P(), P(None, "grid", None)),
        out_specs=P("band", "grid", None, None),
        check_vma=False,
    )
```

```python
import functools
import math

import jax
import jax.numpy as jnp
import ml_dtypes
import numpy as np
from jax import lax
from jax.experimental import pallas as pl
from jax.experimental.pallas import tpu as pltpu
from jax.sharding import PartitionSpec as P

MESH = pl.DeviceIdType.MESH
N = 128
PEERS = 64
ROWS_1, PITCH_1 = 9, 16
ROWS_2, PITCH_2 = 6, 8
ROWS_C, PITCH_C = 6, 8
LAST_KEPT = 57
CUTS = 8

E1S, E1R, AS, AR, F1S, F1R, F2S, F2R, FCS, FCR, B1S, B1R, B2S, B2R, BCS, BCR = range(16)
E2S, E2R, E3S, E3R, X1S, X1R, DS, DR, MFS, MFR = range(16, 26)
MR = 26
MS = 29
LS = 37
NSEM = 46


def row_order():
    order = list(range(24)) + [31] + list(range(24, 31)) + list(range(32, 48))
    order += [48, 55] + list(range(49, 55)) + [57, 56]
    return order


def lane_order():
    out = []
    for q in range(4):
        out += [16 * q + i for i in range(16)]
        out += [-16 * q - 16 + i for i in range(16)]
    return out


def split(table):
    high = table.astype(ml_dtypes.bfloat16)
    low = (table - high.astype(np.float64)).astype(ml_dtypes.bfloat16)
    return high, low


def left_table(table):
    high, low = split(table)
    return np.concatenate([high, low, high], axis=1)


def right_table(table):
    high, low = split(table)
    return np.concatenate([high, high, low], axis=0)


def make_tables():
    n = np.arange(N)
    ky = np.array(row_order())
    kz = np.array(lane_order())
    turn = 2.0 * np.pi / N
    angle_y = turn * ((ky[:, None] * n[None, :]) % N)
    forward_y = np.zeros((128, N))
    forward_y[: len(ky)] = np.cos(angle_y)
    forward_y[64 : 64 + len(ky)] = -np.sin(angle_y)
    weight = np.where(ky == 0, 1.0, 2.0)[:, None]
    inverse_y = np.zeros((128, N))
    inverse_y[: len(ky)] = weight * np.cos(angle_y)
    inverse_y[64 : 64 + len(ky)] = -weight * np.sin(angle_y)
    inverse_y = inverse_y.T
    angle_z = turn * ((n[:, None] * kz[None, :]) % N)
    forward_z = np.concatenate([np.cos(angle_z), np.sin(angle_z)], axis=1)
    inverse_z = np.concatenate([np.cos(angle_z.T), np.sin(angle_z.T)], axis=1)
    x = np.concatenate([np.arange(0, N, 2), np.arange(1, N, 2)])
    angle_x = turn * ((n[:, None] * x[None, :]) % N)
    forward_x = np.concatenate([np.cos(angle_x), np.sin(angle_x)], axis=0)
    inverse_x = np.concatenate([np.cos(angle_x.T), np.sin(angle_x.T)], axis=0)
    lanes = np.zeros((N, N))
    lanes[kz % N, np.arange(N)] = 1.0
    return (
        left_table(forward_y),
        right_table(forward_z),
        right_table(inverse_z),
        left_table(inverse_y),
        left_table(forward_x),
        left_table(inverse_x),
        lanes.astype(ml_dtypes.bfloat16),
    )


def dot(a, b):
    return jnp.dot(a, b, preferred_element_type=jnp.float32)


def halves(value):
    high = value.astype(jnp.bfloat16)
    low = (value - high.astype(jnp.float32)).astype(jnp.bfloat16)
    return high, low


def table_times(table, value):
    high, low = halves(value)
    return dot(table, jnp.concatenate([high, high, low], axis=0))


def times_table(value, table):
    high, low = halves(value)
    return dot(jnp.concatenate([high, low, high], axis=1), table)


def lane_ids(rows):
    return lax.broadcasted_iota(jnp.int32, (rows, 128), 1)


def sublane_ids():
    return lax.broadcasted_iota(jnp.int32, (8, 128), 0)


def turn_lanes(value, by):
    return pltpu.roll(value, by % 128, 1)


def quarters(a):
    lane = lane_ids(a[0].shape[0])
    low = lane < 64
    even = (lane // 32) % 2 == 0
    u = [None] * 4
    for k in range(2):
        u[k] = jnp.where(low, a[k], turn_lanes(a[k + 2], 64))
        u[k + 2] = jnp.where(low, turn_lanes(a[k], 64), a[k + 2])
    out = [None] * 4
    for k in (0, 2):
        out[k] = jnp.where(even, u[k], turn_lanes(u[k + 1], 32))
        out[k + 1] = jnp.where(even, turn_lanes(u[k], -32), u[k + 1])
    return out


def to_chunks(q):
    def chunk(g, c):
        return q[g][8 * c : 8 * c + 8]

    sub = sublane_ids()
    mixed_x = jnp.where(sub == 0, chunk(0, 7), chunk(3, 3))
    mixed_y = jnp.where(sub == 1, chunk(0, 7), chunk(1, 6))
    out = [chunk(0, c) for c in range(7)] + [chunk(1, c) for c in range(6)]
    out += [chunk(2, c) for c in range(6)] + [chunk(3, c) for c in range(3)]
    return out + [mixed_x, mixed_y]


def from_chunks(chunks):
    sub = sublane_ids()
    zero = jnp.zeros((8, 128), jnp.float32)
    mixed_x, mixed_y = chunks[22], chunks[23]
    last = jnp.where(sub == 0, mixed_x, jnp.where(sub == 1, mixed_y, zero))
    q0 = chunks[0:7] + [last]
    q1 = chunks[7:13] + [jnp.where(sub == 1, zero, mixed_y), zero]
    q2 = chunks[13:19] + [zero, zero]
    q3 = chunks[19:22] + [jnp.where(sub == 0, zero, mixed_x)] + [zero] * 4
    return [jnp.concatenate(parts, axis=0) for parts in (q0, q1, q2, q3)]


def forward_planes(densities, ty, wz):
    e = table_times(ty, jnp.concatenate(densities, axis=1))
    real, imag = [], []
    for k in range(len(densities)):
        g = times_table(e[:, 128 * k : 128 * k + 128], wz)
        real.append(g[:64, :128] + g[64:, 128:])
        imag.append(g[64:, :128] - g[:64, 128:])
    return real, imag


def inverse_planes(real, imag, wzi, tyi):
    parts = []
    for re, im in zip(real, imag):
        g = times_table(jnp.concatenate([re, im], axis=0), wzi)
        parts.append(
            jnp.concatenate([g[:64, :128] - g[64:, 128:], g[64:, :128] + g[:64, 128:]], axis=0)
        )
    v = table_times(tyi, jnp.concatenate(parts, axis=1))
    return [v[:, 128 * k : 128 * k + 128] for k in range(len(parts))]


def store_chunks(buf, pitch, row, chunks):
    for m, value in enumerate(chunks):
        buf[pl.ds((m % 8) * 8 * pitch + row(m // 8), 8, stride=pitch), :] = value


def load_chunks(buf, pitch, row):
    return [buf[pl.ds((m % 8) * 8 * pitch + row(m // 8), 8, stride=pitch), :] for m in range(24)]


def pack_quad(buf, pitch, first, real, imag):
    for ri, part in enumerate((real, imag)):
        store_chunks(buf, pitch, lambda j: first + j * 2 + ri, to_chunks(quarters(part)))


def unpack(buf, pitch, row):
    return quarters(from_chunks(load_chunks(buf, pitch, row)))


def spectrum(buf, pitch, second, row):
    return jnp.concatenate(
        [buf[pl.ds(plane * second + row, 64, stride=pitch), :] for plane in range(2)], axis=0
    )


def convolve(real, imag, kernel_of, tx, txi):
    p = table_times(tx, jnp.concatenate(real + imag, axis=1))
    c, s = p[:128], p[128:]
    blocks = []
    for j in range(3):
        re, im = slice(128 * j, 128 * j + 128), slice(384 + 128 * j, 512 + 128 * j)
        blocks.append((c[:, re] + s[:, im]) * kernel_of[j])
    for j in range(3):
        re, im = slice(128 * j, 128 * j + 128), slice(384 + 128 * j, 512 + 128 * j)
        blocks.append((c[:, im] - s[:, re]) * kernel_of[j])
    p = table_times(txi, jnp.concatenate(blocks, axis=1))
    c, s = p[:128], p[128:]
    real, imag = [], []
    for j in range(3):
        re, im = slice(128 * j, 128 * j + 128), slice(384 + 128 * j, 512 + 128 * j)
        real.append(c[:, re] - s[:, im])
        imag.append(c[:, im] + s[:, re])
    return real, imag


def middle_cross(recv, send, kernel_of, tx, txi):
    second = PEERS * PITCH_C
    parts = [[spectrum(recv, PITCH_C, second, j * 2 + ri) for j in range(3)] for ri in range(2)]
    for ri, new in enumerate(convolve(*parts, kernel_of, tx, txi)):
        for j in range(3):
            for plane in range(2):
                send[pl.ds(plane * second + j * 2 + ri, 64, stride=PITCH_C), :] = new[j][
                    64 * plane : 64 * plane + 64
                ]


def middle_first(recv, send, kernel_of, tx, txi):
    lane = lane_ids(64)
    real, imag = [], []
    for j in range(3):
        r0, r1, r2 = (recv[pl.ds(j * 3 + i, 64, stride=PITCH_1), :] for i in range(3))
        real.append(jnp.concatenate([r0, r1], axis=0))
        i0 = jnp.where(lane < 32, turn_lanes(r0, 32), turn_lanes(r2, 32))
        i1 = jnp.where(lane < 32, turn_lanes(r1, 32), turn_lanes(r2, -32))
        imag.append(jnp.concatenate([i0, i1], axis=0))
    real, imag = convolve(real, imag, kernel_of, tx, txi)
    for j in range(3):
        i0, i1 = imag[j][:64], imag[j][64:]
        rows = (
            jnp.where(lane < 96, real[j][:64], turn_lanes(i0, 96)),
            jnp.where(lane < 96, real[j][64:], turn_lanes(i1, 96)),
            jnp.where(lane < 64, turn_lanes(i0, -32), turn_lanes(i1, 32)),
        )
        for i in range(3):
            send[pl.ds(j * 3 + i, 64, stride=PITCH_1), :] = rows[i]


def middle_second(recv, send, kernel_of, tx, txi):
    low = lane_ids(128) < 64

    def cross(s):
        turned = turn_lanes(s, 64)
        return jnp.where(low, turned, -turned)

    blocks = [spectrum(recv, PITCH_2, 1, j * 2) for j in range(3)]
    p = table_times(tx, jnp.concatenate(blocks, axis=1))
    blocks = []
    for j in range(3):
        at = slice(128 * j, 128 * j + 128)
        blocks.append((p[:128, at] + cross(p[128:, at])) * kernel_of[j])
    p = table_times(txi, jnp.concatenate(blocks, axis=1))
    for j in range(3):
        at = slice(128 * j, 128 * j + 128)
        new = p[:128, at] - cross(p[128:, at])
        for plane in range(2):
            send[pl.ds(j * 2 + plane, 64, stride=PITCH_2), :] = new[64 * plane : 64 * plane + 64]


def piece_of(t, j):
    m = j * 8 + t // 8
    sub = t % 8
    q = jnp.where(m < 7, 0, jnp.where(m < 13, 1, jnp.where(m < 19, 2, 3)))
    c = m - jnp.where(m < 7, 0, jnp.where(m < 13, 7, jnp.where(m < 19, 13, 19)))
    is_x = m == 22
    is_y = m == 23
    q = jnp.where(is_y, 1, q)
    c = jnp.where(is_x, 3, jnp.where(is_y, 6, c))
    extra = (is_x & (sub == 0)) | (is_y & (sub == 1))
    q = jnp.where(extra, 0, q)
    c = jnp.where(extra, 7, c)
    pos = c * 8 + sub
    ky = jnp.where((pos >= 25) & (pos <= 31), pos - 1, pos)
    ky = jnp.where((pos >= 50) & (pos <= 55), pos - 1, ky)
    ky = jnp.where(pos == 24, 31, ky)
    ky = jnp.where(pos == 49, 55, ky)
    ky = jnp.where(pos == 56, 57, ky)
    ky = jnp.where(pos == 57, 56, ky)
    return ky, q


def owner_of(ky, q):
    pos = jnp.where((ky >= 24) & (ky <= 30), ky + 1, ky)
    pos = jnp.where((ky >= 49) & (ky <= 54), ky + 1, pos)
    pos = jnp.where(ky == 31, 24, pos)
    pos = jnp.where(ky == 55, 49, pos)
    pos = jnp.where(ky == 57, 56, pos)
    pos = jnp.where(ky == 56, 57, pos)
    c = pos // 8
    sub = pos % 8
    full = jnp.where(q == 0, 7, jnp.where(q == 3, 3, 6))
    base = jnp.where(q == 0, 0, jnp.where(q == 1, 7, jnp.where(q == 2, 13, 19)))
    m = base + c
    m = jnp.where((q == 0) & (c == 7), 22 + sub, m)
    m = jnp.where((q == 1) & (c == 6), 23, m)
    m = jnp.where((q == 3) & (c == 3), 22, m)
    exists = (
        (c < full)
        | ((q == 0) & (c == 7))
        | ((q == 1) & (c == 6) & (sub != 1))
        | ((q == 3) & (c == 3) & (sub != 0))
    ) & (ky <= LAST_KEPT)
    m = jnp.where(exists, m, 0)
    return exists, (m % 8) * 8 + sub, m // 8


def kernel_table(mask, ky, q):
    lane = lane_ids(32)
    rows = []
    for block in range(4):
        part = jnp.where(lane // 32 == block, mask, 0.0)
        part = part + turn_lanes(part, 64)
        rows.append(part + turn_lanes(part, 32))
    kept = jnp.concatenate(rows, axis=0)
    kx = lax.broadcasted_iota(jnp.int32, (128, 128), 0)
    kx = jnp.where(kx < 64, kx, kx - 128)
    i = lane_ids(128) % 32
    kz = jnp.where(i < 16, 16 * q + i, i - 32 - 16 * q)
    squared = kx * kx + ky * ky + kz * kz
    safe = jnp.maximum(squared, 1).astype(jnp.float32)
    return jnp.where(squared > 0, (8.0 * math.pi / N**3) / safe, 0.0) * kept


def body(
    occ, orb_in, kept_in, ty_in, wz_in, wzi_in, tyi_in, tx_in, txi_in, lanes_in, out,
    chip, kept, ty, wz, wzi, tyi, tx, txi, lanes, far, pvr, df, merged, acc, pf, mask_send, mask_recv,
    f_s1, f_r1, b_s1, b_r1, f_s2, f_r2, b_s2, b_r2, f_sc, f_rc, b_sc, b_rc, sem, sem_xy,
):
    b = lax.axis_index("band")
    g = lax.axis_index("grid")
    half = b // 2
    core = b % 2
    other_core = half * 2 + (1 - core)
    other_half = (1 - half) * 2 + core

    u, v = chip.at[0], chip.at[1]
    act, pv = acc.at[0], acc.at[1]
    loads = [
        pltpu.make_async_copy(source, target, sem.at[LS + i])
        for i, (source, target) in enumerate(
            [
                (orb_in, u), (ty_in, ty), (wz_in, wz), (kept_in, kept), (lanes_in, lanes),
                (tx_in, tx), (txi_in, txi), (wzi_in, wzi), (tyi_in, tyi),
            ]
        )
    ]
    for load in loads:
        load.start()

    def on_line(k):
        return g - g % 4 + (g + k) % 4

    def in_plane(k):
        return ((g // 4 + k) % 16) * 4 + g % 4

    barrier = pltpu.get_barrier_semaphore()

    def greet(semaphore, band, grid):
        pl.semaphore_signal(
            semaphore, inc=1, device_id={"band": band, "grid": grid}, device_id_type=MESH
        )

    for k in range(4):
        greet(barrier, other_half, on_line(k))
    for k in range(1, 4):
        greet(barrier, b, on_line(k))
    for k in range(1, 16):
        greet(barrier, b, in_plane(k))
    greet(barrier, other_core, g)

    def remote(src, dst, send, recv, band=None, grid=None):
        device = {"band": b if band is None else band, "grid": g if grid is None else grid}
        return pltpu.make_async_remote_copy(
            src_ref=src, dst_ref=dst, send_sem=sem.at[send], recv_sem=sem.at[recv],
            device_id=device, device_id_type=MESH,
        )

    class Cut:
        def __init__(self, src, dst, send, recv, band):
            self.parts = [
                remote(src.at[i, pl.ds(r, N // CUTS)], dst.at[i, pl.ds(r, N // CUTS)], send, recv, band=band)
                for r in range(0, N, N // CUTS)
                for i in range(2)
            ]
            self.whole = remote(src, dst, send, recv, band=band)

        def start(self):
            for part in self.parts:
                part.start()

        def wait_recv(self):
            self.whole.wait_recv()

        def wait_send(self):
            self.whole.wait_send()

    pl.semaphore_wait(barrier, 23)
    for k in range(1, 16):
        greet(sem_xy, b, in_plane(k))
    loads[0].wait()
    to_half = Cut(u.at[:, 1 - half], far.at[0], AS, AR, other_half)
    to_half.start()
    to_core = remote(u, v, E1S, E1R, band=other_core)
    to_core.start()

    for load in loads[1:3]:
        load.wait()
    ty, wz = ty[...], wz[...]
    own = [
        forward_planes([u[0, p] * u[0, p], u[0, p] * u[1, p], u[1, p] * u[1, p]], ty, wz)
        for p in range(2)
    ]

    for p in range(2):
        real, imag = own[p]
        chunks = to_chunks(quarters(real + imag[:1]))
        store_chunks(f_s1, PITCH_1, lambda j: j * 3 + p, chunks)
    chunks = to_chunks(quarters(own[0][1][1:] + own[1][1][1:]))
    store_chunks(f_s1, PITCH_1, lambda j: j * 3 + 2, chunks)

    for load in loads[3:]:
        load.wait()
    tx, txi, wzi, tyi = tx[...], txi[...], wzi[...], tyi[...]
    for row in range(2):
        plane = dot(kept[:, row, :].astype(jnp.float32).astype(jnp.bfloat16), lanes[...])
        groups = quarters([plane[32 * k : 32 * k + 32] for k in range(4)])
        for q in range(4):
            mask_send[row * 4 + q] = groups[q]

    def mask_copies(act_on_remote, act_on_local):
        def one(i, carry):
            exists, t, j = owner_of(2 * g + i // 4, i % 4)

            @pl.when(exists & (t != g))
            def _():
                act_on_remote(
                    pltpu.make_async_remote_copy(
                        src_ref=mask_send.at[i], dst_ref=mask_recv.at[j],
                        send_sem=sem.at[MS + i], recv_sem=sem.at[MR + j],
                        device_id={"band": b, "grid": t}, device_id_type=MESH,
                    )
                )

            if act_on_local is not None:

                @pl.when(exists & (t == g))
                def _():
                    act_on_local(
                        pltpu.make_async_copy(mask_send.at[i], mask_recv.at[j], sem.at[MR + j])
                    )

            return carry

        lax.fori_loop(0, 8, one, 0)

    mask_to_core = remote(mask_recv, mask_recv, MFS, MFR, band=other_core)

    def peer(k):
        z = (g + jnp.where(k < 16, 2, jnp.where(k < 32, 1, jnp.where(k < 48, 3, 0)))) % 4
        return ((g // 4 + k + jnp.where(k < 48, 0, 1)) % 16) * 4 + z

    def slot(index, pitch, rows):
        return pl.ds(pl.multiple_of(index * pitch, pitch), rows)

    def exchange(src, dst, pitch, rows, send, recv):
        me = slot(g, pitch, rows)

        def one(k, carry):
            t = peer(k)
            remote(src.at[slot(t, pitch, rows)], dst.at[me], send, recv, grid=t).start()
            return carry

        lax.fori_loop(0, PEERS - 1, one, 0)
        pltpu.make_async_copy(src.at[me], dst.at[me], sem.at[recv]).start()

    def exchange_cross(src, dst, to, send, recv):
        me = slot(half * PEERS + g, PITCH_C, ROWS_C)
        band = to * 2 + core

        def copy(t):
            here = slot(to * PEERS + t, PITCH_C, ROWS_C)
            return remote(src.at[here], dst.at[me], send, recv, band=band, grid=t)

        @pl.when(to == half)
        def _():
            pltpu.make_async_copy(src.at[me], dst.at[me], sem.at[recv]).start()

        @pl.when(to != half)
        def _():
            copy(g).start()

        def one(k, carry):
            copy(peer(k)).start()
            return carry

        lax.fori_loop(0, PEERS - 1, one, 0)

    def arrived(dst, rows, recv):
        whole = dst.at[pl.ds(0, rows)]
        pltpu.make_async_copy(whole, whole, sem.at[recv]).wait()

    pl.semaphore_wait(sem_xy, 15)
    exchange(f_s1, f_r1, PITCH_1, ROWS_1, F1S, F1R)

    @pl.when(core == 0)
    def _():
        mask_copies(lambda c: c.start(), lambda c: c.start())

    v0, v1 = core, 1 - core
    to_core.wait_recv()
    real, imag = forward_planes(
        [u[0, p] * v[v0, p] for p in range(2)] + [u[1, p] * v[v1, p] for p in range(2)], ty, wz
    )
    for p in range(2):
        chunks = to_chunks(quarters([real[p], real[2 + p], imag[p], imag[2 + p]]))
        store_chunks(f_s2, PITCH_2, lambda j: j * 2 + p, chunks)

    first_quad = half * core
    quads = ((first_quad, 0, core), (1 - first_quad, 1, 1 - core))

    def pack_cross(quad, f, n):
        near = [chip[n, i, half] for i in (0, half, 1 - half, 1)]
        d = [a * far[f, i] for a, i in zip(near, (0, 1 - half, half, 1))]
        pack_quad(f_sc, PITCH_C, quad * (PEERS * PITCH_C), *forward_planes(d, ty, wz))

    to_half.wait_recv()
    far_to_core = remote(far.at[0], far.at[1], E3S, E3R, band=other_core)
    far_to_core.start()
    pack_cross(*quads[0])
    exchange_cross(f_sc, f_rc, quads[0][0], FCS, FCR)
    far_to_core.wait_recv()
    pack_cross(*quads[1])
    exchange_cross(f_sc, f_rc, quads[1][0], FCS, FCR)

    exchange(f_s2, f_r2, PITCH_2, ROWS_2, F2S, F2R)
    @pl.when(core == 0)
    def _():
        for j in range(3):
            pltpu.make_async_copy(mask_recv.at[j], mask_recv.at[j], sem.at[MR + j]).wait()
        mask_to_core.start()

    @pl.when(core == 1)
    def _():
        mask_to_core.wait_recv()

    kernel_of = [kernel_table(mask_recv[j], *piece_of(g, j)) for j in range(3)]

    arrived(f_r1, PEERS * ROWS_1, F1R)
    middle_first(f_r1, b_s1, kernel_of, tx, txi)
    exchange(b_s1, b_r1, PITCH_1, ROWS_1, B1S, B1R)
    arrived(f_r2, PEERS * ROWS_2, F2R)
    middle_second(f_r2, b_s2, kernel_of, tx, txi)
    arrived(f_rc, 2 * PEERS * ROWS_C, FCR)
    middle_cross(f_rc, b_sc, kernel_of, tx, txi)
    exchange_cross(b_sc, b_rc, half, BCS, BCR)
    exchange_cross(b_sc, b_rc, 1 - half, BCS, BCR)

    mine = half * 4 + core * 2
    theirs = half * 4 + (1 - core) * 2
    arrived(b_r1, PEERS * ROWS_1, B1R)
    rest = unpack(b_r1, PITCH_1, lambda j: j * 3 + 2)
    for p in range(2):
        parts = unpack(b_r1, PITCH_1, lambda j: j * 3 + p)
        pot = inverse_planes(parts[:3], parts[3:] + rest[2 * p : 2 * p + 2], wzi, tyi)
        o0, o1 = occ[mine] * u[0, p], occ[mine + 1] * u[1, p]
        act[0, p] = o0 * pot[0] + o1 * pot[1]
        act[1, p] = o0 * pot[1] + o1 * pot[2]

    pv[...] = jnp.zeros_like(pv)
    arrived(b_rc, 2 * PEERS * ROWS_C, BCR)

    exchange(b_s2, b_r2, PITCH_2, ROWS_2, B2S, B2R)
    def cross_terms(quad, f, n):
        first = quad * (PEERS * PITCH_C)
        real, imag = (unpack(b_rc, PITCH_C, lambda j: first + j * 2 + ri) for ri in range(2))
        p00, p01, p10, p11 = inverse_planes(real, imag, wzi, tyi)
        p01, p10 = jnp.where(half == 0, p01, p10), jnp.where(half == 0, p10, p01)
        here = half * 4 + jnp.where(n == 0, core, 1 - core) * 2
        there = (1 - half) * 4 + (core if f == 0 else 1 - core) * 2
        n0, n1 = occ[here] * chip[n, 0, half], occ[here + 1] * chip[n, 1, half]
        f0, f1 = occ[there] * far[f, 0], occ[there + 1] * far[f, 1]
        pf[f, 0] = n0 * p00 + n1 * p10
        pf[f, 1] = n0 * p01 + n1 * p11
        acc[n, 0, half] += f0 * p00 + f1 * p01
        acc[n, 1, half] += f0 * p10 + f1 * p11

    cross_terms(*quads[1])
    merge = remote(pf.at[1], merged, X1S, X1R, band=other_core)
    merge.start()
    cross_terms(*quads[0])
    merge.wait_recv()
    pf[0] += merged[...]
    home = Cut(pf.at[0], df, DS, DR, other_half)
    home.start()

    arrived(b_r2, PEERS * ROWS_2, B2R)
    for p in range(2):
        a_re, b_re, a_im, b_im = unpack(b_r2, PITCH_2, lambda j: j * 2 + p)
        pot = inverse_planes([a_re, b_re], [a_im, b_im], wzi, tyi)
        act[0, p] += occ[theirs + v0] * v[v0, p] * pot[0]
        act[1, p] += occ[theirs + v1] * v[v1, p] * pot[1]
        pv[v0, p] += occ[mine] * u[0, p] * pot[0]
        pv[v1, p] += occ[mine + 1] * u[1, p] * pot[1]
    swap = remote(pv, pvr, E2S, E2R, band=other_core)
    swap.start()
    swap.wait_recv()
    for i in range(2):
        out[i, half] = -(act[i, half] + pvr[i, half])
        acc[0, i, 1 - half] += pvr[i, 1 - half]
    home.wait_recv()
    for i in range(2):
        out[i, 1 - half] = -(act[i, 1 - half] + df[i])

    to_core.wait_send()
    to_half.wait_send()

    @pl.when(core == 0)
    def _():
        mask_to_core.wait_send()
        mask_copies(lambda c: c.wait_send(), None)

    for src, rows, send in (
        (f_s1, (PEERS - 1) * ROWS_1, F1S),
        (f_s2, (PEERS - 1) * ROWS_2, F2S),
        (f_sc, (2 * PEERS - 1) * ROWS_C, FCS),
        (b_s1, (PEERS - 1) * ROWS_1, B1S),
        (b_s2, (PEERS - 1) * ROWS_2, B2S),
        (b_sc, (2 * PEERS - 1) * ROWS_C, BCS),
    ):
        arrived(src, rows, send)
    far_to_core.wait_send()
    merge.wait_send()
    swap.wait_send()
    home.wait_send()


def on_device(orbitals, occupation, kept_modes):
    block = pltpu.VMEM((2, 2, N, N), jnp.float32)
    twice = pltpu.VMEM((2, 2, 2, N, N), jnp.float32)
    plane = pltpu.VMEM((2, N, N), jnp.float32)
    planes = pltpu.VMEM((2, 2, N, N), jnp.float32)
    messages = [
        pltpu.VMEM((slots * pitch, 128), jnp.float32)
        for slots, pitch in ((PEERS, PITCH_1), (PEERS, PITCH_2), (2 * PEERS, PITCH_C))
        for _ in range(4)
    ]
    tables = make_tables()
    loaded = [twice, pltpu.VMEM(kept_modes.shape, jnp.int32)]
    loaded += [pltpu.VMEM(t.shape, jnp.bfloat16) for t in tables]
    return pl.pallas_call(
        body,
        out_shape=jax.ShapeDtypeStruct(orbitals.shape, jnp.float32),
        in_specs=[pl.BlockSpec(memory_space=pltpu.SMEM)] + [pl.BlockSpec(memory_space=pltpu.HBM)] * 9,
        out_specs=pl.BlockSpec(memory_space=pltpu.VMEM),
        scratch_shapes=loaded
        + [planes, block, plane, plane, twice, planes]
        + [pltpu.VMEM((8, 32, 128), jnp.float32), pltpu.VMEM((3, 32, 128), jnp.float32)]
        + messages
        + [
            pltpu.SemaphoreType.DMA((NSEM,)),
            pltpu.SemaphoreType.REGULAR,
        ],
        compiler_params=pltpu.CompilerParams(
            collective_id=1, has_side_effects=True, vmem_limit_bytes=60 << 20
        ),
        name="exchange",
    )(occupation, orbitals, kept_modes, *(jnp.asarray(t) for t in tables))


def solution(mesh):
    return jax.shard_map(
        on_device,
        mesh=mesh,
        in_specs=(P("band", "grid", None, None), P(), P(None, "grid", None)),
        out_specs=P("band", "grid", None, None),
        check_vma=False,
    )
```

```python
import functools
import math

import jax
import jax.numpy as jnp
import ml_dtypes
import numpy as np
from jax import lax
from jax.experimental import pallas as pl
from jax.experimental.pallas import tpu as pltpu
from jax.sharding import PartitionSpec as P

MESH = pl.DeviceIdType.MESH
N = 128
PEERS = 64
PIECE_1, PITCH_1 = 3, 16
PIECE_2, PITCH_2 = 2, 8
PIECE_C, PITCH_C = 2, 8
CHUNKS = 23
OWN_THREE = 49
PIECES = 3 * OWN_THREE + 2 * (PEERS - OWN_THREE)
LAST_KEPT = 57
CUTS = 8

E1S, E1R, AS, AR, F1S, F1R, F2S, F2R, FCS, FCR, B1S, B1R, B2S, B2R, BCS, BCR = range(16)
E2S, E2R, E3S, E3R, X1S, X1R, DS, DR, MFS, MFR = range(16, 26)
MR = 26
MS = 30
LS = 38
NSEM = 47


def row_order():
    order = list(range(24)) + [31] + list(range(24, 31)) + list(range(32, 48))
    order += [54, 52, 53, 55, 48, 49, 50, 51] + [57, -1, -1, 56] + [-1] * 4
    return order


def lane_order():
    out = []
    for q in range(4):
        for first in (16 * q, 16 * q + 8):
            out += [first + i for i in range(8)]
            out += [-first - 1 - i for i in range(8)]
    return out


def split(table):
    high = table.astype(ml_dtypes.bfloat16)
    low = (table - high.astype(np.float64)).astype(ml_dtypes.bfloat16)
    return high, low


def left_table(table):
    high, low = split(table)
    return np.concatenate([high, low, high], axis=1)


def right_table(table):
    high, low = split(table)
    return np.concatenate([high, high, low], axis=0)


def make_tables():
    n = np.arange(N)
    ky = np.array(row_order())
    kz = np.array(lane_order())
    turn = 2.0 * np.pi / N
    angle_y = turn * ((ky[:, None] * n[None, :]) % N)
    forward_y = np.zeros((128, N))
    forward_y[:64] = np.where(ky < 0, 0.0, 1.0)[:, None] * np.cos(angle_y)
    forward_y[64:] = -np.where(ky < 0, 0.0, 1.0)[:, None] * np.sin(angle_y)
    weight = np.where(ky < 0, 0.0, np.where(ky == 0, 1.0, 2.0))[:, None]
    inverse_y = np.zeros((128, N))
    inverse_y[:64] = weight * np.cos(angle_y)
    inverse_y[64:] = -weight * np.sin(angle_y)
    inverse_y = inverse_y.T
    angle_z = turn * ((n[:, None] * kz[None, :]) % N)
    forward_z = np.concatenate([np.cos(angle_z), np.sin(angle_z)], axis=1)
    inverse_z = np.concatenate([np.cos(angle_z.T), np.sin(angle_z.T)], axis=1)
    x = np.concatenate([np.arange(0, N, 2), np.arange(1, N, 2)])
    angle_x = turn * ((n[:, None] * x[None, :]) % N)
    forward_x = np.concatenate([np.cos(angle_x), np.sin(angle_x)], axis=0)
    inverse_x = np.concatenate([np.cos(angle_x.T), np.sin(angle_x.T)], axis=0)
    lanes = np.zeros((N, N))
    lanes[kz % N, np.arange(N)] = 1.0
    return (
        left_table(forward_y),
        right_table(forward_z),
        right_table(inverse_z),
        left_table(inverse_y),
        left_table(forward_x),
        left_table(inverse_x),
        lanes.astype(ml_dtypes.bfloat16),
    )


def dot(a, b):
    return jnp.dot(a, b, preferred_element_type=jnp.float32)


def halves(value):
    high = value.astype(jnp.bfloat16)
    low = (value - high.astype(jnp.float32)).astype(jnp.bfloat16)
    return high, low


def table_times(table, value):
    high, low = halves(value)
    return dot(table, jnp.concatenate([high, high, low], axis=0))


def times_table(value, table):
    high, low = halves(value)
    return dot(jnp.concatenate([high, low, high], axis=1), table)


def lane_ids(rows):
    return lax.broadcasted_iota(jnp.int32, (rows, 128), 1)


def sublane_ids():
    return lax.broadcasted_iota(jnp.int32, (8, 128), 0)


def turn_lanes(value, by):
    return pltpu.roll(value, by % 128, 1)


def quarters(a):
    lane = lane_ids(a[0].shape[0])
    low = lane < 64
    even = (lane // 32) % 2 == 0
    u = [None] * 4
    for k in range(2):
        u[k] = jnp.where(low, a[k], turn_lanes(a[k + 2], 64))
        u[k + 2] = jnp.where(low, turn_lanes(a[k], 64), a[k + 2])
    out = [None] * 4
    for k in (0, 2):
        out[k] = jnp.where(even, u[k], turn_lanes(u[k + 1], 32))
        out[k + 1] = jnp.where(even, turn_lanes(u[k], -32), u[k + 1])
    return out


def to_chunks(q):
    def chunk(g, c):
        return q[g][8 * c : 8 * c + 8]

    def merge(first, second):
        return jnp.where(inner, first, turn_lanes(second, 16))

    sub = sublane_ids()
    inner = lane_ids(8) % 32 < 16
    x = merge(chunk(3, 2), jnp.where(sub == 0, chunk(1, 6), chunk(3, 3)))
    y = merge(chunk(2, 5), jnp.where(sub < 3, chunk(1, 6), chunk(3, 1)))
    y = jnp.where(sub == 0, chunk(2, 5), y)
    z = jnp.where(sub < 3, chunk(3, 1), jnp.where(sub == 3, chunk(0, 7), chunk(1, 6)))
    out = [chunk(0, c) for c in range(7)] + [chunk(1, c) for c in range(6)]
    out += [chunk(2, c) for c in range(5)] + [chunk(3, 0)]
    return out + [x, y, z, chunk(0, 7)]


def from_chunks(chunks):
    sub = sublane_ids()
    inner = lane_ids(8) % 32 < 16
    zero = jnp.zeros((8, 128), jnp.float32)
    x, y, z, last = chunks[19:]
    x_second = jnp.where(inner, turn_lanes(x, -16), zero)
    y_second = jnp.where(inner, turn_lanes(y, -16), zero)
    x_first = jnp.where(inner, x, zero)
    y_first = jnp.where(inner | (sub == 0), y, zero)
    q0 = chunks[0:7] + [jnp.where(sub == 0, last, jnp.where(sub == 3, z, zero))]
    mixed = jnp.where(sub == 0, x_second, jnp.where(sub < 3, y_second, jnp.where(sub == 3, zero, z)))
    q1 = chunks[7:13] + [mixed, zero]
    q2 = chunks[13:18] + [y_first, zero, zero]
    q3 = [chunks[18], jnp.where(sub < 3, z, y_second), x_first, jnp.where(sub == 0, zero, x_second)]
    q3 += [zero] * 4
    return [jnp.concatenate(parts, axis=0) for parts in (q0, q1, q2, q3)]


def forward_planes(densities, ty, wz):
    e = table_times(ty, jnp.concatenate(densities, axis=1))
    real, imag = [], []
    for k in range(len(densities)):
        g = times_table(e[:, 128 * k : 128 * k + 128], wz)
        real.append(g[:64, :128] + g[64:, 128:])
        imag.append(g[64:, :128] - g[:64, 128:])
    return real, imag


def inverse_planes(real, imag, wzi, tyi):
    parts = []
    for re, im in zip(real, imag):
        g = times_table(jnp.concatenate([re, im], axis=0), wzi)
        parts.append(
            jnp.concatenate([g[:64, :128] - g[64:, 128:], g[64:, :128] + g[:64, 128:]], axis=0)
        )
    v = table_times(tyi, jnp.concatenate(parts, axis=1))
    return [v[:, 128 * k : 128 * k + 128] for k in range(len(parts))]


def store_chunks(buf, pitch, row, chunks):
    for m, value in enumerate(chunks):
        buf[pl.ds((m % 8) * 8 * pitch + row(m // 8), 8, stride=pitch), :] = value


def load_chunks(buf, pitch, row):
    return [buf[pl.ds((m % 8) * 8 * pitch + row(m // 8), 8, stride=pitch), :] for m in range(CHUNKS)]


def pack_quad(buf, pitch, first, real, imag):
    for ri, part in enumerate((real, imag)):
        store_chunks(buf, pitch, lambda j: first + j * 2 + ri, to_chunks(quarters(part)))


def unpack(buf, pitch, row):
    return quarters(from_chunks(load_chunks(buf, pitch, row)))


def spectrum(buf, pitch, second, row):
    return jnp.concatenate(
        [buf[pl.ds(plane * second + row, 64, stride=pitch), :] for plane in range(2)], axis=0
    )


def convolve(real, imag, kernel_of, tx, txi):
    p = table_times(tx, jnp.concatenate(real + imag, axis=1))
    c, s = p[:128], p[128:]
    blocks = []
    for j in range(3):
        re, im = slice(128 * j, 128 * j + 128), slice(384 + 128 * j, 512 + 128 * j)
        blocks.append((c[:, re] + s[:, im]) * kernel_of[j])
    for j in range(3):
        re, im = slice(128 * j, 128 * j + 128), slice(384 + 128 * j, 512 + 128 * j)
        blocks.append((c[:, im] - s[:, re]) * kernel_of[j])
    p = table_times(txi, jnp.concatenate(blocks, axis=1))
    c, s = p[:128], p[128:]
    real, imag = [], []
    for j in range(3):
        re, im = slice(128 * j, 128 * j + 128), slice(384 + 128 * j, 512 + 128 * j)
        real.append(c[:, re] - s[:, im])
        imag.append(c[:, im] + s[:, re])
    return real, imag


def middle_cross(recv, send, kernel_of, tx, txi):
    second = PEERS * PITCH_C
    parts = [[spectrum(recv, PITCH_C, second, j * 2 + ri) for j in range(3)] for ri in range(2)]
    for ri, new in enumerate(convolve(*parts, kernel_of, tx, txi)):
        for j in range(3):
            for plane in range(2):
                send[pl.ds(plane * second + j * 2 + ri, 64, stride=PITCH_C), :] = new[j][
                    64 * plane : 64 * plane + 64
                ]


def middle_first(recv, send, kernel_of, tx, txi):
    lane = lane_ids(64)
    real, imag = [], []
    for j in range(3):
        r0, r1, r2 = (recv[pl.ds(j * 3 + i, 64, stride=PITCH_1), :] for i in range(3))
        real.append(jnp.concatenate([r0, r1], axis=0))
        i0 = jnp.where(lane < 32, turn_lanes(r0, 32), turn_lanes(r2, 32))
        i1 = jnp.where(lane < 32, turn_lanes(r1, 32), turn_lanes(r2, -32))
        imag.append(jnp.concatenate([i0, i1], axis=0))
    real, imag = convolve(real, imag, kernel_of, tx, txi)
    for j in range(3):
        i0, i1 = imag[j][:64], imag[j][64:]
        rows = (
            jnp.where(lane < 96, real[j][:64], turn_lanes(i0, 96)),
            jnp.where(lane < 96, real[j][64:], turn_lanes(i1, 96)),
            jnp.where(lane < 64, turn_lanes(i0, -32), turn_lanes(i1, 32)),
        )
        for i in range(3):
            send[pl.ds(j * 3 + i, 64, stride=PITCH_1), :] = rows[i]


def middle_second(recv, send, kernel_of, tx, txi):
    low = lane_ids(128) < 64

    def cross(s):
        turned = turn_lanes(s, 64)
        return jnp.where(low, turned, -turned)

    blocks = [spectrum(recv, PITCH_2, 1, j * 2) for j in range(3)]
    p = table_times(tx, jnp.concatenate(blocks, axis=1))
    blocks = []
    for j in range(3):
        at = slice(128 * j, 128 * j + 128)
        blocks.append((p[:128, at] + cross(p[128:, at])) * kernel_of[j])
    p = table_times(txi, jnp.concatenate(blocks, axis=1))
    for j in range(3):
        at = slice(128 * j, 128 * j + 128)
        new = p[:128, at] - cross(p[128:, at])
        for plane in range(2):
            send[pl.ds(j * 2 + plane, 64, stride=PITCH_2), :] = new[64 * plane : 64 * plane + 64]


def place_of(g):
    line = g // 4
    return 16 * ((g % 4 + 3 - line % 4) % 4) + line


def frequency_at(pos):
    ky = jnp.where((pos >= 25) & (pos <= 31), pos - 1, pos)
    ky = jnp.where((pos >= 52) & (pos <= 55), pos - 4, ky)
    for at, value in ((24, 31), (48, 54), (49, 52), (50, 53), (51, 55), (56, 57), (59, 56)):
        ky = jnp.where(pos == at, value, ky)
    return ky


def position_of(ky):
    pos = jnp.where((ky >= 24) & (ky <= 30), ky + 1, ky)
    pos = jnp.where((ky >= 48) & (ky <= 51), ky + 4, pos)
    for at, value in ((24, 31), (48, 54), (49, 52), (50, 53), (51, 55), (56, 57), (59, 56)):
        pos = jnp.where(ky == value, at, pos)
    return pos


def pick(cases, otherwise):
    out = otherwise
    for condition, case in reversed(cases):
        out = jnp.where(condition, case, out)
    return out


def piece_of(place, j):
    m = j * 8 + place // 8
    sub = place % 8
    in_z = m == 21
    cases = [
        (m < 7, 0), (m < 13, 1), (m < 18, 2), (m < 20, 3), (m == 20, 2),
        (in_z & (sub < 3), 3), (in_z & (sub > 3), 1),
    ]
    q = pick(cases, 0)
    cases = [
        (m < 7, m), (m < 13, m - 7), (m < 18, m - 13), (m == 18, 0), (m == 19, 2), (m == 20, 5),
        (in_z & (sub < 3), 1), (in_z & (sub > 3), 6),
    ]
    c = pick(cases, 7)
    merged = (m == 19) | ((m == 20) & (sub > 0))
    from_1 = ((m == 19) & (sub == 0)) | ((m == 20) & (sub < 3))
    q_outer = jnp.where(merged, jnp.where(from_1, 1, 3), q)
    c_outer = jnp.where(merged, jnp.where(from_1, 6, jnp.where(m == 19, 3, 1)), c)
    inner = (frequency_at(c * 8 + sub), q)
    return inner, (frequency_at(c_outer * 8 + sub), q_outer), merged


def owner_of(ky, q):
    pos = position_of(ky)
    c = pos // 8
    sub = pos % 8
    cases = [
        ((q == 0) & (c < 7), c), ((q == 0) & (sub == 0), 22), (q == 0, 21),
        ((q == 1) & (c < 6), c + 7), ((q == 1) & (sub == 0), 19), ((q == 1) & (sub < 3), 20),
        (q == 1, 21), ((q == 2) & (c < 5), c + 13), (q == 2, 20),
        (c == 0, 18), ((c == 1) & (sub < 3), 21), (c == 1, 20),
    ]
    m = pick(cases, 19)
    second = ((q == 1) & (c == 6) & (sub < 3)) | (
        (q == 3) & (((c == 1) & (sub >= 3)) | (c == 3))
    )
    exists = (
        (q == 0)
        | ((q == 1) & ((c < 6) | ((c == 6) & (sub != 3))))
        | ((q == 2) & (c < 6))
        | ((q == 3) & ((c < 3) | ((c == 3) & (sub > 0))))
    ) & (ky <= LAST_KEPT)
    m = jnp.where(exists, m, 0)
    place = (m % 8) * 8 + sub
    line = place % 16
    return exists, line * 4 + (place // 16 + 1 + line) % 4, jnp.where(second, 3, m // 8)


def kernel_table(mask, second, piece):
    (ky_inner, q_inner), (ky_outer, q_outer), merged = piece
    lane = lane_ids(32)
    mask = jnp.where((lane % 32 >= 16) & merged, turn_lanes(second, 16), mask)
    rows = []
    for block in range(4):
        part = jnp.where(lane // 32 == block, mask, 0.0)
        part = part + turn_lanes(part, 64)
        rows.append(part + turn_lanes(part, 32))
    kept = jnp.concatenate(rows, axis=0)
    kx = lax.broadcasted_iota(jnp.int32, (128, 128), 0)
    kx = jnp.where(kx < 64, kx, kx - 128)
    inner = lane_ids(128) % 32 < 16
    i = lane_ids(128) % 16
    ky = jnp.where(inner, ky_inner, ky_outer)
    first = jnp.where(inner, 16 * q_inner, 16 * q_outer + jnp.where(merged, 0, 8))
    kz = jnp.where(i < 8, first + i, 7 - first - i)
    squared = kx * kx + ky * ky + kz * kz
    safe = jnp.maximum(squared, 1).astype(jnp.float32)
    return jnp.where(squared > 0, (8.0 * math.pi / N**3) / safe, 0.0) * kept


def body(
    occ, orb_in, kept_in, ty_in, wz_in, wzi_in, tyi_in, tx_in, txi_in, lanes_in, out,
    chip, kept, ty, wz, wzi, tyi, tx, txi, lanes, far, pvr, df, merged, acc, pf, mask_send, mask_recv,
    f_s1, f_r1, b_s1, b_r1, f_s2, f_r2, b_s2, b_r2, f_sc, f_rc, b_sc, b_rc, sem, sem_xy,
):
    b = lax.axis_index("band")
    g = lax.axis_index("grid")
    half = b // 2
    core = b % 2
    other_core = half * 2 + (1 - core)
    other_half = (1 - half) * 2 + core

    mask_recv[...] = jnp.zeros_like(mask_recv)
    u, v = chip.at[0], chip.at[1]
    act, pv = acc.at[0], acc.at[1]
    loads = [
        pltpu.make_async_copy(source, target, sem.at[LS + i])
        for i, (source, target) in enumerate(
            [
                (orb_in, u), (ty_in, ty), (wz_in, wz), (kept_in, kept), (lanes_in, lanes),
                (tx_in, tx), (txi_in, txi), (wzi_in, wzi), (tyi_in, tyi),
            ]
        )
    ]
    for load in loads:
        load.start()

    def on_line(k):
        return g - g % 4 + (g + k) % 4

    def in_plane(k):
        return ((g // 4 + k) % 16) * 4 + g % 4

    barrier = pltpu.get_barrier_semaphore()

    def greet(semaphore, band, grid):
        pl.semaphore_signal(
            semaphore, inc=1, device_id={"band": band, "grid": grid}, device_id_type=MESH
        )

    for k in range(4):
        greet(barrier, other_half, on_line(k))
    for k in range(1, 4):
        greet(barrier, b, on_line(k))
    for k in range(1, 16):
        greet(barrier, b, in_plane(k))
    greet(barrier, other_core, g)

    def remote(src, dst, send, recv, band=None, grid=None):
        device = {"band": b if band is None else band, "grid": g if grid is None else grid}
        return pltpu.make_async_remote_copy(
            src_ref=src, dst_ref=dst, send_sem=sem.at[send], recv_sem=sem.at[recv],
            device_id=device, device_id_type=MESH,
        )

    class Cut:
        def __init__(self, src, dst, send, recv, band):
            self.parts = [
                remote(src.at[i, pl.ds(r, N // CUTS)], dst.at[i, pl.ds(r, N // CUTS)], send, recv, band=band)
                for r in range(0, N, N // CUTS)
                for i in range(2)
            ]
            self.whole = remote(src, dst, send, recv, band=band)

        def start(self):
            for part in self.parts:
                part.start()

        def wait_recv(self):
            self.whole.wait_recv()

        def wait_send(self):
            self.whole.wait_send()

    pl.semaphore_wait(barrier, 23)
    for k in range(1, 16):
        greet(sem_xy, b, in_plane(k))
    loads[0].wait()
    to_half = Cut(u.at[:, 1 - half], far.at[0], AS, AR, other_half)
    to_half.start()
    to_core = remote(u, v, E1S, E1R, band=other_core)
    to_core.start()

    for load in loads[1:3]:
        load.wait()
    ty, wz = ty[...], wz[...]
    own = [
        forward_planes([u[0, p] * u[0, p], u[0, p] * u[1, p], u[1, p] * u[1, p]], ty, wz)
        for p in range(2)
    ]

    for p in range(2):
        real, imag = own[p]
        chunks = to_chunks(quarters(real + imag[:1]))
        store_chunks(f_s1, PITCH_1, lambda j: j * 3 + p, chunks)
    chunks = to_chunks(quarters(own[0][1][1:] + own[1][1][1:]))
    store_chunks(f_s1, PITCH_1, lambda j: j * 3 + 2, chunks)

    for load in loads[3:]:
        load.wait()
    tx, txi, wzi, tyi = tx[...], txi[...], wzi[...], tyi[...]
    for row in range(2):
        plane = dot(kept[:, row, :].astype(jnp.float32).astype(jnp.bfloat16), lanes[...])
        groups = quarters([plane[32 * k : 32 * k + 32] for k in range(4)])
        for q in range(4):
            mask_send[row * 4 + q] = groups[q]

    def mask_copies(act_on_remote, act_on_local):
        def one(i, carry):
            exists, t, j = owner_of(2 * g + i // 4, i % 4)

            @pl.when(exists & (t != g))
            def _():
                act_on_remote(
                    pltpu.make_async_remote_copy(
                        src_ref=mask_send.at[i], dst_ref=mask_recv.at[j],
                        send_sem=sem.at[MS + i], recv_sem=sem.at[MR + j],
                        device_id={"band": b, "grid": t}, device_id_type=MESH,
                    )
                )

            if act_on_local is not None:

                @pl.when(exists & (t == g))
                def _():
                    act_on_local(
                        pltpu.make_async_copy(mask_send.at[i], mask_recv.at[j], sem.at[MR + j])
                    )

            return carry

        lax.fori_loop(0, 8, one, 0)

    mask_to_core = remote(mask_recv, mask_recv, MFS, MFR, band=other_core)

    def slot(index, pitch, rows):
        return pl.ds(pl.multiple_of(index * pitch, pitch), rows)

    place = place_of(g)
    three = place < OWN_THREE

    def sized(count_three, act):
        @pl.when(count_three)
        def _():
            act(3)

        @pl.when(jnp.logical_not(count_three))
        def _():
            act(2)

    my_line, my_z = g // 4, g % 4
    my_first, my_turn = my_line % 4, my_line // 4

    def forward(src, dst, pitch, piece, send, recv, to):
        there = to * PEERS
        target_slot = (half * PEERS if dst.shape[0] == 2 * PEERS * pitch else 0) + g
        source_slot = there if dst.shape[0] == 2 * PEERS * pitch else 0

        def start(pieces, p, t):
            rows = pieces * piece
            source, target = src.at[slot(source_slot + p, pitch, rows)], dst.at[slot(target_slot, pitch, rows)]
            remote(source, target, send, recv, band=to * 2 + core, grid=t).start()

        for step in (2, 1, 3, 0):
            z = (my_z + step) % 4
            for r in (1, 2, 3, 0):
                first = (z + r) % 4

                def one(n, carry):
                    q = n + my_turn
                    line = first + 4 * jnp.where(q >= 4, q - 4, q)
                    p, t = 16 * (3 - r) + line, 4 * line + z
                    if r > 0:
                        start(3, p, t)
                    else:
                        sized(line == 0, lambda pieces: start(pieces, p, t))
                    return carry

                if step == 0:

                    @pl.when((first != my_first) | (to != half))
                    def _():
                        one(0, 0)

                lax.fori_loop(0 if step > 0 else 1, 4, one, 0)

        @pl.when(to == half)
        def _():
            def local(pieces):
                rows = pieces * piece
                source = src.at[slot(source_slot + place, pitch, rows)]
                pltpu.make_async_copy(source, dst.at[slot(target_slot, pitch, rows)], sem.at[recv]).start()

            sized(three, local)

    def backward(src, dst, pitch, piece, send, recv, to):
        both = dst.shape[0] == 2 * PEERS * pitch
        target_slot = (half * PEERS if both else 0) + place
        source_slot = to * PEERS if both else 0

        def messages(pieces):
            rows = pieces * piece
            target = dst.at[slot(target_slot, pitch, rows)]

            def start(t):
                source = src.at[slot(source_slot + t, pitch, rows)]
                remote(source, target, send, recv, band=to * 2 + core, grid=t).start()

            for step in (2, 1, 3, 0):
                z = (my_z + step) % 4

                def one(k, carry):
                    line = my_line + k
                    start(4 * jnp.where(line >= 16, line - 16, line) + z)
                    return carry

                lax.fori_loop(0 if step > 0 else 1, 16, one, 0)

            @pl.when(to != half)
            def _():
                start(g)

            @pl.when(to == half)
            def _():
                source = src.at[slot(source_slot + g, pitch, rows)]
                pltpu.make_async_copy(source, target, sem.at[recv]).start()

        sized(three, messages)

    def arrived_own(dst, count, piece, semaphore):
        sized(three, lambda pieces: arrived(dst, count * pieces * piece, semaphore))

    def arrived(dst, rows, recv):
        whole = dst.at[pl.ds(0, rows)]
        pltpu.make_async_copy(whole, whole, sem.at[recv]).wait()

    pl.semaphore_wait(sem_xy, 15)
    forward(f_s1, f_r1, PITCH_1, PIECE_1, F1S, F1R, half)

    @pl.when(core == 0)
    def _():
        mask_copies(lambda c: c.start(), lambda c: c.start())

    v0, v1 = core, 1 - core
    to_core.wait_recv()
    real, imag = forward_planes(
        [u[0, p] * v[v0, p] for p in range(2)] + [u[1, p] * v[v1, p] for p in range(2)], ty, wz
    )
    for p in range(2):
        chunks = to_chunks(quarters([real[p], real[2 + p], imag[p], imag[2 + p]]))
        store_chunks(f_s2, PITCH_2, lambda j: j * 2 + p, chunks)

    first_quad = half * core
    quads = ((first_quad, 0, core), (1 - first_quad, 1, 1 - core))

    def pack_cross(quad, f, n):
        near = [chip[n, i, half] for i in (0, half, 1 - half, 1)]
        d = [a * far[f, i] for a, i in zip(near, (0, 1 - half, half, 1))]
        pack_quad(f_sc, PITCH_C, quad * (PEERS * PITCH_C), *forward_planes(d, ty, wz))

    to_half.wait_recv()
    far_to_core = remote(far.at[0], far.at[1], E3S, E3R, band=other_core)
    far_to_core.start()
    pack_cross(*quads[0])
    forward(f_sc, f_rc, PITCH_C, PIECE_C, FCS, FCR, quads[0][0])
    far_to_core.wait_recv()
    pack_cross(*quads[1])
    forward(f_sc, f_rc, PITCH_C, PIECE_C, FCS, FCR, quads[1][0])

    forward(f_s2, f_r2, PITCH_2, PIECE_2, F2S, F2R, half)
    two_rows = piece_of(place, 2)[2] & three
    @pl.when(core == 0)
    def _():
        for j, expected in enumerate((True, True, three, two_rows)):

            @pl.when(expected)
            def _():
                pltpu.make_async_copy(mask_recv.at[j], mask_recv.at[j], sem.at[MR + j]).wait()

        mask_to_core.start()

    @pl.when(core == 1)
    def _():
        mask_to_core.wait_recv()

    kernel_of = [kernel_table(mask_recv[j], mask_recv[3], piece_of(place, j)) for j in range(3)]

    arrived_own(f_r1, PEERS, PIECE_1, F1R)
    middle_first(f_r1, b_s1, kernel_of, tx, txi)
    backward(b_s1, b_r1, PITCH_1, PIECE_1, B1S, B1R, half)
    arrived_own(f_r2, PEERS, PIECE_2, F2R)
    middle_second(f_r2, b_s2, kernel_of, tx, txi)
    arrived_own(f_rc, 2 * PEERS, PIECE_C, FCR)
    middle_cross(f_rc, b_sc, kernel_of, tx, txi)
    backward(b_sc, b_rc, PITCH_C, PIECE_C, BCS, BCR, half)
    backward(b_sc, b_rc, PITCH_C, PIECE_C, BCS, BCR, 1 - half)

    mine = half * 4 + core * 2
    theirs = half * 4 + (1 - core) * 2
    arrived(b_r1, PIECES * PIECE_1, B1R)
    rest = unpack(b_r1, PITCH_1, lambda j: j * 3 + 2)
    for p in range(2):
        parts = unpack(b_r1, PITCH_1, lambda j: j * 3 + p)
        pot = inverse_planes(parts[:3], parts[3:] + rest[2 * p : 2 * p + 2], wzi, tyi)
        o0, o1 = occ[mine] * u[0, p], occ[mine + 1] * u[1, p]
        act[0, p] = o0 * pot[0] + o1 * pot[1]
        act[1, p] = o0 * pot[1] + o1 * pot[2]

    pv[...] = jnp.zeros_like(pv)
    arrived(b_rc, 2 * PIECES * PIECE_C, BCR)

    backward(b_s2, b_r2, PITCH_2, PIECE_2, B2S, B2R, half)
    def cross_terms(quad, f, n):
        first = quad * (PEERS * PITCH_C)
        real, imag = (unpack(b_rc, PITCH_C, lambda j: first + j * 2 + ri) for ri in range(2))
        p00, p01, p10, p11 = inverse_planes(real, imag, wzi, tyi)
        p01, p10 = jnp.where(half == 0, p01, p10), jnp.where(half == 0, p10, p01)
        here = half * 4 + jnp.where(n == 0, core, 1 - core) * 2
        there = (1 - half) * 4 + (core if f == 0 else 1 - core) * 2
        n0, n1 = occ[here] * chip[n, 0, half], occ[here + 1] * chip[n, 1, half]
        f0, f1 = occ[there] * far[f, 0], occ[there + 1] * far[f, 1]
        pf[f, 0] = n0 * p00 + n1 * p10
        pf[f, 1] = n0 * p01 + n1 * p11
        acc[n, 0, half] += f0 * p00 + f1 * p01
        acc[n, 1, half] += f0 * p10 + f1 * p11

    cross_terms(*quads[1])
    merge = remote(pf.at[1], merged, X1S, X1R, band=other_core)
    merge.start()
    cross_terms(*quads[0])
    merge.wait_recv()
    pf[0] += merged[...]
    home = Cut(pf.at[0], df, DS, DR, other_half)
    home.start()

    arrived(b_r2, PIECES * PIECE_2, B2R)
    for p in range(2):
        a_re, b_re, a_im, b_im = unpack(b_r2, PITCH_2, lambda j: j * 2 + p)
        pot = inverse_planes([a_re, b_re], [a_im, b_im], wzi, tyi)
        act[0, p] += occ[theirs + v0] * v[v0, p] * pot[0]
        act[1, p] += occ[theirs + v1] * v[v1, p] * pot[1]
        pv[v0, p] += occ[mine] * u[0, p] * pot[0]
        pv[v1, p] += occ[mine + 1] * u[1, p] * pot[1]
    swap = remote(pv, pvr, E2S, E2R, band=other_core)
    swap.start()
    swap.wait_recv()
    for i in range(2):
        out[i, half] = -(act[i, half] + pvr[i, half])
        acc[0, i, 1 - half] += pvr[i, 1 - half]
    home.wait_recv()
    for i in range(2):
        out[i, 1 - half] = -(act[i, 1 - half] + df[i])

    to_core.wait_send()
    to_half.wait_send()

    @pl.when(core == 0)
    def _():
        mask_to_core.wait_send()
        mask_copies(lambda c: c.wait_send(), None)

    for src, pieces, piece, send in (
        (f_s1, PIECES, PIECE_1, F1S),
        (f_s2, PIECES, PIECE_2, F2S),
        (f_sc, 2 * PIECES, PIECE_C, FCS),
    ):
        sized(three, lambda mine: arrived(src, (pieces - mine) * piece, send))
    arrived_own(b_s1, PEERS - 1, PIECE_1, B1S)
    arrived_own(b_s2, PEERS - 1, PIECE_2, B2S)
    arrived_own(b_sc, 2 * PEERS - 1, PIECE_C, BCS)
    far_to_core.wait_send()
    merge.wait_send()
    swap.wait_send()
    home.wait_send()


def on_device(orbitals, occupation, kept_modes):
    block = pltpu.VMEM((2, 2, N, N), jnp.float32)
    twice = pltpu.VMEM((2, 2, 2, N, N), jnp.float32)
    plane = pltpu.VMEM((2, N, N), jnp.float32)
    planes = pltpu.VMEM((2, 2, N, N), jnp.float32)
    messages = [
        pltpu.VMEM((slots * pitch, 128), jnp.float32)
        for slots, pitch in ((PEERS, PITCH_1), (PEERS, PITCH_2), (2 * PEERS, PITCH_C))
        for _ in range(4)
    ]
    tables = make_tables()
    loaded = [twice, pltpu.VMEM(kept_modes.shape, jnp.int32)]
    loaded += [pltpu.VMEM(t.shape, jnp.bfloat16) for t in tables]
    return pl.pallas_call(
        body,
        out_shape=jax.ShapeDtypeStruct(orbitals.shape, jnp.float32),
        in_specs=[pl.BlockSpec(memory_space=pltpu.SMEM)] + [pl.BlockSpec(memory_space=pltpu.HBM)] * 9,
        out_specs=pl.BlockSpec(memory_space=pltpu.VMEM),
        scratch_shapes=loaded
        + [planes, block, plane, plane, twice, planes]
        + [pltpu.VMEM((8, 32, 128), jnp.float32), pltpu.VMEM((4, 32, 128), jnp.float32)]
        + messages
        + [
            pltpu.SemaphoreType.DMA((NSEM,)),
            pltpu.SemaphoreType.REGULAR,
        ],
        compiler_params=pltpu.CompilerParams(
            collective_id=1, has_side_effects=True, vmem_limit_bytes=60 << 20
        ),
        name="exchange",
    )(occupation, orbitals, kept_modes, *(jnp.asarray(t) for t in tables))


def solution(mesh):
    return jax.shard_map(
        on_device,
        mesh=mesh,
        in_specs=(P("band", "grid", None, None), P(), P(None, "grid", None)),
        out_specs=P("band", "grid", None, None),
        check_vma=False,
    )
```

```python
import functools
import math

import jax
import jax.numpy as jnp
import ml_dtypes
import numpy as np
from jax import lax
from jax.experimental import pallas as pl
from jax.experimental.pallas import tpu as pltpu
from jax.sharding import PartitionSpec as P

MESH = pl.DeviceIdType.MESH
N = 128
PEERS = 64
PIECE_1, PITCH_1 = 3, 16
PIECE_2, PITCH_2 = 2, 8
PIECE_C, PITCH_C = 2, 8
CHUNKS = 23
OWN_THREE = 49
PIECES = 3 * OWN_THREE + 2 * (PEERS - OWN_THREE)
LAST_KEPT = 57
CUTS = 8

E1S, E1R, AS, AR, F1S, F1R, F2S, F2R, FCS, FCR, B1S, B1R, B2S, B2R, BCS, BCR = range(16)
E2S, E2R, E3S, E3R, X1S, X1R, DS, DR, MFS, MFR, BOR = range(16, 27)
MR = 27
MS = 31
LS = 39
NSEM = 48


def row_order():
    order = list(range(24)) + [31] + list(range(24, 31)) + list(range(32, 48))
    order += [54, 52, 53, 55, 48, 49, 50, 51] + [57, -1, -1, 56] + [-1] * 4
    return order


def lane_order():
    out = []
    for q in range(4):
        for first in (16 * q, 16 * q + 8):
            out += [first + i for i in range(8)]
            out += [-first - 1 - i for i in range(8)]
    return out


def split(table):
    high = table.astype(ml_dtypes.bfloat16)
    low = (table - high.astype(np.float64)).astype(ml_dtypes.bfloat16)
    return high, low


def left_table(table):
    high, low = split(table)
    return np.concatenate([high, low, high], axis=1)


def right_table(table):
    high, low = split(table)
    return np.concatenate([high, high, low], axis=0)


def make_tables():
    n = np.arange(N)
    ky = np.array(row_order())
    kz = np.array(lane_order())
    turn = 2.0 * np.pi / N
    angle_y = turn * ((ky[:, None] * n[None, :]) % N)
    forward_y = np.zeros((128, N))
    forward_y[:64] = np.where(ky < 0, 0.0, 1.0)[:, None] * np.cos(angle_y)
    forward_y[64:] = -np.where(ky < 0, 0.0, 1.0)[:, None] * np.sin(angle_y)
    weight = np.where(ky < 0, 0.0, np.where(ky == 0, 1.0, 2.0))[:, None]
    inverse_y = np.zeros((128, N))
    inverse_y[:64] = weight * np.cos(angle_y)
    inverse_y[64:] = -weight * np.sin(angle_y)
    inverse_y = inverse_y.T
    angle_z = turn * ((n[:, None] * kz[None, :]) % N)
    forward_z = np.concatenate([np.cos(angle_z), np.sin(angle_z)], axis=1)
    inverse_z = np.concatenate([np.cos(angle_z.T), np.sin(angle_z.T)], axis=1)
    x = np.concatenate([np.arange(0, N, 2), np.arange(1, N, 2)])
    angle_x = turn * ((n[:, None] * x[None, :]) % N)
    forward_x = np.concatenate([np.cos(angle_x), np.sin(angle_x)], axis=0)
    inverse_x = np.concatenate([np.cos(angle_x.T), np.sin(angle_x.T)], axis=0)
    lanes = np.zeros((N, N))
    lanes[kz % N, np.arange(N)] = 1.0
    return (
        left_table(forward_y),
        right_table(forward_z),
        right_table(inverse_z),
        left_table(inverse_y),
        left_table(forward_x),
        left_table(inverse_x),
        lanes.astype(ml_dtypes.bfloat16),
    )


def dot(a, b):
    return jnp.dot(a, b, preferred_element_type=jnp.float32)


def halves(value):
    high = value.astype(jnp.bfloat16)
    low = (value - high.astype(jnp.float32)).astype(jnp.bfloat16)
    return high, low


def table_times(table, value):
    high, low = halves(value)
    return dot(table, jnp.concatenate([high, high, low], axis=0))


def times_table(value, table):
    high, low = halves(value)
    return dot(jnp.concatenate([high, low, high], axis=1), table)


def lane_ids(rows):
    return lax.broadcasted_iota(jnp.int32, (rows, 128), 1)


def sublane_ids():
    return lax.broadcasted_iota(jnp.int32, (8, 128), 0)


def turn_lanes(value, by):
    return pltpu.roll(value, by % 128, 1)


def quarters(a):
    lane = lane_ids(a[0].shape[0])
    low = lane < 64
    even = (lane // 32) % 2 == 0
    u = [None] * 4
    for k in range(2):
        u[k] = jnp.where(low, a[k], turn_lanes(a[k + 2], 64))
        u[k + 2] = jnp.where(low, turn_lanes(a[k], 64), a[k + 2])
    out = [None] * 4
    for k in (0, 2):
        out[k] = jnp.where(even, u[k], turn_lanes(u[k + 1], 32))
        out[k + 1] = jnp.where(even, turn_lanes(u[k], -32), u[k + 1])
    return out


def to_chunks(q):
    def chunk(g, c):
        return q[g][8 * c : 8 * c + 8]

    def merge(first, second):
        return jnp.where(inner, first, turn_lanes(second, 16))

    sub = sublane_ids()
    inner = lane_ids(8) % 32 < 16
    x = merge(chunk(3, 2), jnp.where(sub == 0, chunk(1, 6), chunk(3, 3)))
    y = merge(chunk(2, 5), jnp.where(sub < 3, chunk(1, 6), chunk(3, 1)))
    y = jnp.where(sub == 0, chunk(2, 5), y)
    z = jnp.where(sub < 3, chunk(3, 1), jnp.where(sub == 3, chunk(0, 7), chunk(1, 6)))
    out = [chunk(0, c) for c in range(7)] + [chunk(1, c) for c in range(6)]
    out += [chunk(2, c) for c in range(5)] + [chunk(3, 0)]
    return out + [x, y, z, chunk(0, 7)]


def from_chunks(chunks):
    sub = sublane_ids()
    inner = lane_ids(8) % 32 < 16
    zero = jnp.zeros((8, 128), jnp.float32)
    x, y, z, last = chunks[19:]
    x_second = jnp.where(inner, turn_lanes(x, -16), zero)
    y_second = jnp.where(inner, turn_lanes(y, -16), zero)
    x_first = jnp.where(inner, x, zero)
    y_first = jnp.where(inner | (sub == 0), y, zero)
    q0 = chunks[0:7] + [jnp.where(sub == 0, last, jnp.where(sub == 3, z, zero))]
    mixed = jnp.where(sub == 0, x_second, jnp.where(sub < 3, y_second, jnp.where(sub == 3, zero, z)))
    q1 = chunks[7:13] + [mixed, zero]
    q2 = chunks[13:18] + [y_first, zero, zero]
    q3 = [chunks[18], jnp.where(sub < 3, z, y_second), x_first, jnp.where(sub == 0, zero, x_second)]
    q3 += [zero] * 4
    return [jnp.concatenate(parts, axis=0) for parts in (q0, q1, q2, q3)]


def forward_planes(densities, ty, wz):
    e = table_times(ty, jnp.concatenate(densities, axis=1))
    real, imag = [], []
    for k in range(len(densities)):
        g = times_table(e[:, 128 * k : 128 * k + 128], wz)
        real.append(g[:64, :128] + g[64:, 128:])
        imag.append(g[64:, :128] - g[:64, 128:])
    return real, imag


def inverse_planes(real, imag, wzi, tyi):
    parts = []
    for re, im in zip(real, imag):
        g = times_table(jnp.concatenate([re, im], axis=0), wzi)
        parts.append(
            jnp.concatenate([g[:64, :128] - g[64:, 128:], g[64:, :128] + g[:64, 128:]], axis=0)
        )
    v = table_times(tyi, jnp.concatenate(parts, axis=1))
    return [v[:, 128 * k : 128 * k + 128] for k in range(len(parts))]


def store_chunks(buf, pitch, row, chunks):
    for m, value in enumerate(chunks):
        buf[pl.ds((m % 8) * 8 * pitch + row(m // 8), 8, stride=pitch), :] = value


def load_chunks(buf, pitch, row):
    return [buf[pl.ds((m % 8) * 8 * pitch + row(m // 8), 8, stride=pitch), :] for m in range(CHUNKS)]


def pack_quad(buf, pitch, first, real, imag):
    for ri, part in enumerate((real, imag)):
        store_chunks(buf, pitch, lambda j: first + j * 2 + ri, to_chunks(quarters(part)))


def unpack(buf, pitch, row):
    return quarters(from_chunks(load_chunks(buf, pitch, row)))


def spectrum(buf, pitch, second, row):
    return jnp.concatenate(
        [buf[pl.ds(plane * second + row, 64, stride=pitch), :] for plane in range(2)], axis=0
    )


def convolve(real, imag, kernel_of, tx, txi):
    p = table_times(tx, jnp.concatenate(real + imag, axis=1))
    c, s = p[:128], p[128:]
    blocks = []
    for j in range(3):
        re, im = slice(128 * j, 128 * j + 128), slice(384 + 128 * j, 512 + 128 * j)
        blocks.append((c[:, re] + s[:, im]) * kernel_of[j])
    for j in range(3):
        re, im = slice(128 * j, 128 * j + 128), slice(384 + 128 * j, 512 + 128 * j)
        blocks.append((c[:, im] - s[:, re]) * kernel_of[j])
    p = table_times(txi, jnp.concatenate(blocks, axis=1))
    c, s = p[:128], p[128:]
    real, imag = [], []
    for j in range(3):
        re, im = slice(128 * j, 128 * j + 128), slice(384 + 128 * j, 512 + 128 * j)
        real.append(c[:, re] - s[:, im])
        imag.append(c[:, im] + s[:, re])
    return real, imag


def middle_cross(recv, send, kernel_of, tx, txi):
    second = PEERS * PITCH_C
    parts = [[spectrum(recv, PITCH_C, second, j * 2 + ri) for j in range(3)] for ri in range(2)]
    for ri, new in enumerate(convolve(*parts, kernel_of, tx, txi)):
        for j in range(3):
            for plane in range(2):
                send[pl.ds(plane * second + j * 2 + ri, 64, stride=PITCH_C), :] = new[j][
                    64 * plane : 64 * plane + 64
                ]


def middle_first(recv, send, kernel_of, tx, txi):
    lane = lane_ids(64)
    real, imag = [], []
    for j in range(3):
        r0, r1, r2 = (recv[pl.ds(j * 3 + i, 64, stride=PITCH_1), :] for i in range(3))
        real.append(jnp.concatenate([r0, r1], axis=0))
        i0 = jnp.where(lane < 32, turn_lanes(r0, 32), turn_lanes(r2, 32))
        i1 = jnp.where(lane < 32, turn_lanes(r1, 32), turn_lanes(r2, -32))
        imag.append(jnp.concatenate([i0, i1], axis=0))
    real, imag = convolve(real, imag, kernel_of, tx, txi)
    for j in range(3):
        i0, i1 = imag[j][:64], imag[j][64:]
        rows = (
            jnp.where(lane < 96, real[j][:64], turn_lanes(i0, 96)),
            jnp.where(lane < 96, real[j][64:], turn_lanes(i1, 96)),
            jnp.where(lane < 64, turn_lanes(i0, -32), turn_lanes(i1, 32)),
        )
        for i in range(3):
            send[pl.ds(j * 3 + i, 64, stride=PITCH_1), :] = rows[i]


def middle_second(recv, send, kernel_of, tx, txi):
    low = lane_ids(128) < 64

    def cross(s):
        turned = turn_lanes(s, 64)
        return jnp.where(low, turned, -turned)

    blocks = [spectrum(recv, PITCH_2, 1, j * 2) for j in range(3)]
    p = table_times(tx, jnp.concatenate(blocks, axis=1))
    blocks = []
    for j in range(3):
        at = slice(128 * j, 128 * j + 128)
        blocks.append((p[:128, at] + cross(p[128:, at])) * kernel_of[j])
    p = table_times(txi, jnp.concatenate(blocks, axis=1))
    for j in range(3):
        at = slice(128 * j, 128 * j + 128)
        new = p[:128, at] - cross(p[128:, at])
        for plane in range(2):
            send[pl.ds(j * 2 + plane, 64, stride=PITCH_2), :] = new[64 * plane : 64 * plane + 64]


def place_of(g):
    line = g // 4
    return 16 * ((g % 4 + 3 - line % 4) % 4) + line


def frequency_at(pos):
    ky = jnp.where((pos >= 25) & (pos <= 31), pos - 1, pos)
    ky = jnp.where((pos >= 52) & (pos <= 55), pos - 4, ky)
    for at, value in ((24, 31), (48, 54), (49, 52), (50, 53), (51, 55), (56, 57), (59, 56)):
        ky = jnp.where(pos == at, value, ky)
    return ky


def position_of(ky):
    pos = jnp.where((ky >= 24) & (ky <= 30), ky + 1, ky)
    pos = jnp.where((ky >= 48) & (ky <= 51), ky + 4, pos)
    for at, value in ((24, 31), (48, 54), (49, 52), (50, 53), (51, 55), (56, 57), (59, 56)):
        pos = jnp.where(ky == value, at, pos)
    return pos


def pick(cases, otherwise):
    out = otherwise
    for condition, case in reversed(cases):
        out = jnp.where(condition, case, out)
    return out


def piece_of(place, j):
    m = j * 8 + place // 8
    sub = place % 8
    in_z = m == 21
    cases = [
        (m < 7, 0), (m < 13, 1), (m < 18, 2), (m < 20, 3), (m == 20, 2),
        (in_z & (sub < 3), 3), (in_z & (sub > 3), 1),
    ]
    q = pick(cases, 0)
    cases = [
        (m < 7, m), (m < 13, m - 7), (m < 18, m - 13), (m == 18, 0), (m == 19, 2), (m == 20, 5),
        (in_z & (sub < 3), 1), (in_z & (sub > 3), 6),
    ]
    c = pick(cases, 7)
    merged = (m == 19) | ((m == 20) & (sub > 0))
    from_1 = ((m == 19) & (sub == 0)) | ((m == 20) & (sub < 3))
    q_outer = jnp.where(merged, jnp.where(from_1, 1, 3), q)
    c_outer = jnp.where(merged, jnp.where(from_1, 6, jnp.where(m == 19, 3, 1)), c)
    inner = (frequency_at(c * 8 + sub), q)
    return inner, (frequency_at(c_outer * 8 + sub), q_outer), merged


def owner_of(ky, q):
    pos = position_of(ky)
    c = pos // 8
    sub = pos % 8
    cases = [
        ((q == 0) & (c < 7), c), ((q == 0) & (sub == 0), 22), (q == 0, 21),
        ((q == 1) & (c < 6), c + 7), ((q == 1) & (sub == 0), 19), ((q == 1) & (sub < 3), 20),
        (q == 1, 21), ((q == 2) & (c < 5), c + 13), (q == 2, 20),
        (c == 0, 18), ((c == 1) & (sub < 3), 21), (c == 1, 20),
    ]
    m = pick(cases, 19)
    second = ((q == 1) & (c == 6) & (sub < 3)) | (
        (q == 3) & (((c == 1) & (sub >= 3)) | (c == 3))
    )
    exists = (
        (q == 0)
        | ((q == 1) & ((c < 6) | ((c == 6) & (sub != 3))))
        | ((q == 2) & (c < 6))
        | ((q == 3) & ((c < 3) | ((c == 3) & (sub > 0))))
    ) & (ky <= LAST_KEPT)
    m = jnp.where(exists, m, 0)
    place = (m % 8) * 8 + sub
    line = place % 16
    return exists, line * 4 + (place // 16 + 1 + line) % 4, jnp.where(second, 3, m // 8)


def kernel_table(mask, second, piece):
    (ky_inner, q_inner), (ky_outer, q_outer), merged = piece
    lane = lane_ids(32)
    mask = jnp.where((lane % 32 >= 16) & merged, turn_lanes(second, 16), mask)
    rows = []
    for block in range(4):
        part = jnp.where(lane // 32 == block, mask, 0.0)
        part = part + turn_lanes(part, 64)
        rows.append(part + turn_lanes(part, 32))
    kept = jnp.concatenate(rows, axis=0)
    kx = lax.broadcasted_iota(jnp.int32, (128, 128), 0)
    kx = jnp.where(kx < 64, kx, kx - 128)
    inner = lane_ids(128) % 32 < 16
    i = lane_ids(128) % 16
    ky = jnp.where(inner, ky_inner, ky_outer)
    first = jnp.where(inner, 16 * q_inner, 16 * q_outer + jnp.where(merged, 0, 8))
    kz = jnp.where(i < 8, first + i, 7 - first - i)
    squared = kx * kx + ky * ky + kz * kz
    safe = jnp.maximum(squared, 1).astype(jnp.float32)
    return jnp.where(squared > 0, (8.0 * math.pi / N**3) / safe, 0.0) * kept


def body(
    occ, orb_in, kept_in, ty_in, wz_in, wzi_in, tyi_in, tx_in, txi_in, lanes_in, out,
    chip, kept, ty, wz, wzi, tyi, tx, txi, lanes, far, pvr, df, merged, acc, pf, mask_send, mask_recv,
    f_s1, f_r1, b_s1, b_r1, f_s2, f_r2, b_s2, b_r2, f_sc, f_rc, b_sc, b_rc, sem, sem_xy,
):
    b = lax.axis_index("band")
    g = lax.axis_index("grid")
    half = b // 2
    core = b % 2
    other_core = half * 2 + (1 - core)
    other_half = (1 - half) * 2 + core

    mask_recv[...] = jnp.zeros_like(mask_recv)
    u, v = chip.at[0], chip.at[1]
    act, pv = acc.at[0], acc.at[1]
    loads = [
        pltpu.make_async_copy(source, target, sem.at[LS + i])
        for i, (source, target) in enumerate(
            [
                (orb_in, u), (ty_in, ty), (wz_in, wz), (kept_in, kept), (lanes_in, lanes),
                (tx_in, tx), (txi_in, txi), (wzi_in, wzi), (tyi_in, tyi),
            ]
        )
    ]
    for load in loads:
        load.start()

    def on_line(k):
        return g - g % 4 + (g + k) % 4

    def in_plane(k):
        return ((g // 4 + k) % 16) * 4 + g % 4

    barrier = pltpu.get_barrier_semaphore()

    def greet(semaphore, band, grid):
        pl.semaphore_signal(
            semaphore, inc=1, device_id={"band": band, "grid": grid}, device_id_type=MESH
        )

    for k in range(4):
        greet(barrier, other_half, on_line(k))
    for k in range(1, 4):
        greet(barrier, b, on_line(k))
    for k in range(1, 16):
        greet(barrier, b, in_plane(k))
    greet(barrier, other_core, g)

    def remote(src, dst, send, recv, band=None, grid=None):
        device = {"band": b if band is None else band, "grid": g if grid is None else grid}
        return pltpu.make_async_remote_copy(
            src_ref=src, dst_ref=dst, send_sem=sem.at[send], recv_sem=sem.at[recv],
            device_id=device, device_id_type=MESH,
        )

    class Cut:
        def __init__(self, src, dst, send, recv, band):
            self.parts = [
                remote(src.at[i, pl.ds(r, N // CUTS)], dst.at[i, pl.ds(r, N // CUTS)], send, recv, band=band)
                for r in range(0, N, N // CUTS)
                for i in range(2)
            ]
            self.whole = remote(src, dst, send, recv, band=band)

        def start(self):
            for part in self.parts:
                part.start()

        def wait_recv(self):
            self.whole.wait_recv()

        def wait_send(self):
            self.whole.wait_send()

    pl.semaphore_wait(barrier, 23)
    for k in range(1, 16):
        greet(sem_xy, b, in_plane(k))
    loads[0].wait()
    to_half = Cut(u.at[:, 1 - half], far.at[0], AS, AR, other_half)
    to_half.start()
    to_core = remote(u, v, E1S, E1R, band=other_core)
    to_core.start()

    for load in loads[1:3]:
        load.wait()
    ty, wz = ty[...], wz[...]
    own = [
        forward_planes([u[0, p] * u[0, p], u[0, p] * u[1, p], u[1, p] * u[1, p]], ty, wz)
        for p in range(2)
    ]

    for p in range(2):
        real, imag = own[p]
        chunks = to_chunks(quarters(real + imag[:1]))
        store_chunks(f_s1, PITCH_1, lambda j: j * 3 + p, chunks)
    chunks = to_chunks(quarters(own[0][1][1:] + own[1][1][1:]))
    store_chunks(f_s1, PITCH_1, lambda j: j * 3 + 2, chunks)

    for load in loads[3:]:
        load.wait()
    tx, txi, wzi, tyi = tx[...], txi[...], wzi[...], tyi[...]
    for row in range(2):
        plane = dot(kept[:, row, :].astype(jnp.float32).astype(jnp.bfloat16), lanes[...])
        groups = quarters([plane[32 * k : 32 * k + 32] for k in range(4)])
        for q in range(4):
            mask_send[row * 4 + q] = groups[q]

    def mask_copies(act_on_remote, act_on_local):
        def one(i, carry):
            exists, t, j = owner_of(2 * g + i // 4, i % 4)

            @pl.when(exists & (t != g))
            def _():
                act_on_remote(
                    pltpu.make_async_remote_copy(
                        src_ref=mask_send.at[i], dst_ref=mask_recv.at[j],
                        send_sem=sem.at[MS + i], recv_sem=sem.at[MR + j],
                        device_id={"band": b, "grid": t}, device_id_type=MESH,
                    )
                )

            if act_on_local is not None:

                @pl.when(exists & (t == g))
                def _():
                    act_on_local(
                        pltpu.make_async_copy(mask_send.at[i], mask_recv.at[j], sem.at[MR + j])
                    )

            return carry

        lax.fori_loop(0, 8, one, 0)

    mask_to_core = remote(mask_recv, mask_recv, MFS, MFR, band=other_core)

    def slot(index, pitch, rows):
        return pl.ds(pl.multiple_of(index * pitch, pitch), rows)

    place = place_of(g)
    three = place < OWN_THREE

    def sized(count_three, act):
        @pl.when(count_three)
        def _():
            act(3)

        @pl.when(jnp.logical_not(count_three))
        def _():
            act(2)

    my_line, my_z = g // 4, g % 4
    my_first, my_turn = my_line % 4, my_line // 4

    def forward(src, dst, pitch, piece, send, recv, to):
        there = to * PEERS
        target_slot = (half * PEERS if dst.shape[0] == 2 * PEERS * pitch else 0) + g
        source_slot = there if dst.shape[0] == 2 * PEERS * pitch else 0

        def start(pieces, p, t):
            rows = pieces * piece
            source, target = src.at[slot(source_slot + p, pitch, rows)], dst.at[slot(target_slot, pitch, rows)]
            remote(source, target, send, recv, band=to * 2 + core, grid=t).start()

        for step in (2, 1, 3, 0):
            z = (my_z + step) % 4
            for r in (1, 2, 3, 0):
                first = (z + r) % 4

                def one(n, carry):
                    q = n + my_turn
                    line = first + 4 * jnp.where(q >= 4, q - 4, q)
                    p, t = 16 * (3 - r) + line, 4 * line + z
                    if r > 0:
                        start(3, p, t)
                    else:
                        sized(line == 0, lambda pieces: start(pieces, p, t))
                    return carry

                if step == 0:

                    @pl.when((first != my_first) | (to != half))
                    def _():
                        one(0, 0)

                lax.fori_loop(0 if step > 0 else 1, 4, one, 0)

        @pl.when(to == half)
        def _():
            def local(pieces):
                rows = pieces * piece
                source = src.at[slot(source_slot + place, pitch, rows)]
                pltpu.make_async_copy(source, dst.at[slot(target_slot, pitch, rows)], sem.at[recv]).start()

            sized(three, local)

    def backward(src, dst, pitch, piece, send, recv, to):
        both = dst.shape[0] == 2 * PEERS * pitch
        target_slot = (half * PEERS if both else 0) + place
        source_slot = to * PEERS if both else 0

        def messages(pieces):
            rows = pieces * piece
            target = dst.at[slot(target_slot, pitch, rows)]

            def start(t):
                source = src.at[slot(source_slot + t, pitch, rows)]
                remote(source, target, send, recv, band=to * 2 + core, grid=t).start()

            for step in (2, 1, 3, 0):
                z = (my_z + step) % 4

                def one(k, carry):
                    line = my_line + k
                    start(4 * jnp.where(line >= 16, line - 16, line) + z)
                    return carry

                lax.fori_loop(0 if step > 0 else 1, 16, one, 0)

            @pl.when(to != half)
            def _():
                start(g)

            @pl.when(to == half)
            def _():
                source = src.at[slot(source_slot + g, pitch, rows)]
                pltpu.make_async_copy(source, target, sem.at[recv]).start()

        sized(three, messages)

    def arrived_own(dst, count, piece, semaphore):
        sized(three, lambda pieces: arrived(dst, count * pieces * piece, semaphore))

    def arrived(dst, rows, recv):
        whole = dst.at[pl.ds(0, rows)]
        pltpu.make_async_copy(whole, whole, sem.at[recv]).wait()

    pl.semaphore_wait(sem_xy, 15)
    forward(f_s1, f_r1, PITCH_1, PIECE_1, F1S, F1R, half)

    @pl.when(core == 0)
    def _():
        mask_copies(lambda c: c.start(), lambda c: c.start())

    v0, v1 = core, 1 - core
    to_core.wait_recv()
    real, imag = forward_planes(
        [u[0, p] * v[v0, p] for p in range(2)] + [u[1, p] * v[v1, p] for p in range(2)], ty, wz
    )
    for p in range(2):
        chunks = to_chunks(quarters([real[p], real[2 + p], imag[p], imag[2 + p]]))
        store_chunks(f_s2, PITCH_2, lambda j: j * 2 + p, chunks)

    first_quad = half * core
    quads = ((first_quad, 0, core), (1 - first_quad, 1, 1 - core))

    def pack_cross(quad, f, n):
        near = [chip[n, i, half] for i in (0, half, 1 - half, 1)]
        d = [a * far[f, i] for a, i in zip(near, (0, 1 - half, half, 1))]
        pack_quad(f_sc, PITCH_C, quad * (PEERS * PITCH_C), *forward_planes(d, ty, wz))

    to_half.wait_recv()
    far_to_core = remote(far.at[0], far.at[1], E3S, E3R, band=other_core)
    far_to_core.start()
    pack_cross(*quads[0])
    forward(f_sc, f_rc, PITCH_C, PIECE_C, FCS, FCR, quads[0][0])
    far_to_core.wait_recv()
    pack_cross(*quads[1])
    forward(f_sc, f_rc, PITCH_C, PIECE_C, FCS, FCR, quads[1][0])

    forward(f_s2, f_r2, PITCH_2, PIECE_2, F2S, F2R, half)
    two_rows = piece_of(place, 2)[2] & three
    @pl.when(core == 0)
    def _():
        for j, expected in enumerate((True, True, three, two_rows)):

            @pl.when(expected)
            def _():
                pltpu.make_async_copy(mask_recv.at[j], mask_recv.at[j], sem.at[MR + j]).wait()

        mask_to_core.start()

    @pl.when(core == 1)
    def _():
        mask_to_core.wait_recv()

    kernel_of = [kernel_table(mask_recv[j], mask_recv[3], piece_of(place, j)) for j in range(3)]

    arrived_own(f_r1, PEERS, PIECE_1, F1R)
    middle_first(f_r1, b_s1, kernel_of, tx, txi)
    backward(b_s1, b_r1, PITCH_1, PIECE_1, B1S, B1R, half)
    arrived_own(f_r2, PEERS, PIECE_2, F2R)
    middle_second(f_r2, b_s2, kernel_of, tx, txi)
    arrived_own(f_rc, 2 * PEERS, PIECE_C, FCR)
    middle_cross(f_rc, b_sc, kernel_of, tx, txi)
    backward(b_sc, b_rc, PITCH_C, PIECE_C, BCS, BOR, 1 - half)
    backward(b_sc, b_rc, PITCH_C, PIECE_C, BCS, BCR, half)

    mine = half * 4 + core * 2
    theirs = half * 4 + (1 - core) * 2
    arrived(b_r1, PIECES * PIECE_1, B1R)
    rest = unpack(b_r1, PITCH_1, lambda j: j * 3 + 2)
    for p in range(2):
        parts = unpack(b_r1, PITCH_1, lambda j: j * 3 + p)
        pot = inverse_planes(parts[:3], parts[3:] + rest[2 * p : 2 * p + 2], wzi, tyi)
        o0, o1 = occ[mine] * u[0, p], occ[mine + 1] * u[1, p]
        act[0, p] = o0 * pot[0] + o1 * pot[1]
        act[1, p] = o0 * pot[1] + o1 * pot[2]

    pv[...] = jnp.zeros_like(pv)
    arrived(b_rc, PIECES * PIECE_C, BOR)
    backward(b_s2, b_r2, PITCH_2, PIECE_2, B2S, B2R, half)
    arrived(b_rc, PIECES * PIECE_C, BCR)

    def cross_terms(quad, f, n):
        first = quad * (PEERS * PITCH_C)
        real, imag = (unpack(b_rc, PITCH_C, lambda j: first + j * 2 + ri) for ri in range(2))
        p00, p01, p10, p11 = inverse_planes(real, imag, wzi, tyi)
        p01, p10 = jnp.where(half == 0, p01, p10), jnp.where(half == 0, p10, p01)
        here = half * 4 + jnp.where(n == 0, core, 1 - core) * 2
        there = (1 - half) * 4 + (core if f == 0 else 1 - core) * 2
        n0, n1 = occ[here] * chip[n, 0, half], occ[here + 1] * chip[n, 1, half]
        f0, f1 = occ[there] * far[f, 0], occ[there + 1] * far[f, 1]
        pf[f, 0] = n0 * p00 + n1 * p10
        pf[f, 1] = n0 * p01 + n1 * p11
        acc[n, 0, half] += f0 * p00 + f1 * p01
        acc[n, 1, half] += f0 * p10 + f1 * p11

    cross_terms(*quads[1])
    merge = remote(pf.at[1], merged, X1S, X1R, band=other_core)
    merge.start()
    cross_terms(*quads[0])
    merge.wait_recv()
    pf[0] += merged[...]
    home = Cut(pf.at[0], df, DS, DR, other_half)
    home.start()

    arrived(b_r2, PIECES * PIECE_2, B2R)
    for p in range(2):
        a_re, b_re, a_im, b_im = unpack(b_r2, PITCH_2, lambda j: j * 2 + p)
        pot = inverse_planes([a_re, b_re], [a_im, b_im], wzi, tyi)
        act[0, p] += occ[theirs + v0] * v[v0, p] * pot[0]
        act[1, p] += occ[theirs + v1] * v[v1, p] * pot[1]
        pv[v0, p] += occ[mine] * u[0, p] * pot[0]
        pv[v1, p] += occ[mine + 1] * u[1, p] * pot[1]
    swap = remote(pv, pvr, E2S, E2R, band=other_core)
    swap.start()
    swap.wait_recv()
    for i in range(2):
        out[i, half] = -(act[i, half] + pvr[i, half])
        acc[0, i, 1 - half] += pvr[i, 1 - half]
    home.wait_recv()
    for i in range(2):
        out[i, 1 - half] = -(act[i, 1 - half] + df[i])

    to_core.wait_send()
    to_half.wait_send()

    @pl.when(core == 0)
    def _():
        mask_to_core.wait_send()
        mask_copies(lambda c: c.wait_send(), None)

    for src, pieces, piece, send in (
        (f_s1, PIECES, PIECE_1, F1S),
        (f_s2, PIECES, PIECE_2, F2S),
        (f_sc, 2 * PIECES, PIECE_C, FCS),
    ):
        sized(three, lambda mine: arrived(src, (pieces - mine) * piece, send))
    arrived_own(b_s1, PEERS - 1, PIECE_1, B1S)
    arrived_own(b_s2, PEERS - 1, PIECE_2, B2S)
    arrived_own(b_sc, 2 * PEERS - 1, PIECE_C, BCS)
    far_to_core.wait_send()
    merge.wait_send()
    swap.wait_send()
    home.wait_send()


def on_device(orbitals, occupation, kept_modes):
    block = pltpu.VMEM((2, 2, N, N), jnp.float32)
    twice = pltpu.VMEM((2, 2, 2, N, N), jnp.float32)
    plane = pltpu.VMEM((2, N, N), jnp.float32)
    planes = pltpu.VMEM((2, 2, N, N), jnp.float32)
    messages = [
        pltpu.VMEM((slots * pitch, 128), jnp.float32)
        for slots, pitch in ((PEERS, PITCH_1), (PEERS, PITCH_2), (2 * PEERS, PITCH_C))
        for _ in range(4)
    ]
    tables = make_tables()
    loaded = [twice, pltpu.VMEM(kept_modes.shape, jnp.int32)]
    loaded += [pltpu.VMEM(t.shape, jnp.bfloat16) for t in tables]
    return pl.pallas_call(
        body,
        out_shape=jax.ShapeDtypeStruct(orbitals.shape, jnp.float32),
        in_specs=[pl.BlockSpec(memory_space=pltpu.SMEM)] + [pl.BlockSpec(memory_space=pltpu.HBM)] * 9,
        out_specs=pl.BlockSpec(memory_space=pltpu.VMEM),
        scratch_shapes=loaded
        + [planes, block, plane, plane, twice, planes]
        + [pltpu.VMEM((8, 32, 128), jnp.float32), pltpu.VMEM((4, 32, 128), jnp.float32)]
        + messages
        + [
            pltpu.SemaphoreType.DMA((NSEM,)),
            pltpu.SemaphoreType.REGULAR,
        ],
        compiler_params=pltpu.CompilerParams(
            collective_id=1, has_side_effects=True, vmem_limit_bytes=60 << 20
        ),
        name="exchange",
    )(occupation, orbitals, kept_modes, *(jnp.asarray(t) for t in tables))


def solution(mesh):
    return jax.shard_map(
        on_device,
        mesh=mesh,
        in_specs=(P("band", "grid", None, None), P(), P(None, "grid", None)),
        out_specs=P("band", "grid", None, None),
        check_vma=False,
    )
```

```python
import functools
import math

import jax
import jax.numpy as jnp
import ml_dtypes
import numpy as np
from jax import lax
from jax.experimental import pallas as pl
from jax.experimental.pallas import tpu as pltpu
from jax.sharding import PartitionSpec as P

MESH = pl.DeviceIdType.MESH
N = 128
PEERS = 64
PIECE_1, PITCH_1 = 3, 16
PIECE_2, PITCH_2 = 2, 8
PIECE_C, PITCH_C = 2, 8
CHUNKS = 23
OWN_THREE = 49
PIECES = 3 * OWN_THREE + 2 * (PEERS - OWN_THREE)
LAST_KEPT = 57
CUTS = 2

E1S, E1R, AS, AR, F1S, F1R, F2S, F2R, FCS, FCR, B1S, B1R, B2S, B2R, BCS, BCR = range(16)
E2S, E2R, E3S, E3R, X1S, X1R, DS, DR, MFS, MFR, BOR = range(16, 27)
MR = 27
MS = 31
LS = 39
NSEM = 48


def row_order():
    order = list(range(24)) + [31] + list(range(24, 31)) + list(range(32, 48))
    order += [54, 52, 53, 55, 48, 49, 50, 51] + [57, -1, -1, 56] + [-1] * 4
    return order


def lane_order():
    out = []
    for q in range(4):
        for first in (16 * q, 16 * q + 8):
            out += [first + i for i in range(8)]
            out += [-first - 1 - i for i in range(8)]
    return out


def split(table):
    high = table.astype(ml_dtypes.bfloat16)
    low = (table - high.astype(np.float64)).astype(ml_dtypes.bfloat16)
    return high, low


def left_table(table):
    high, low = split(table)
    return np.concatenate([high, low, high], axis=1)


def right_table(table):
    high, low = split(table)
    return np.concatenate([high, high, low], axis=0)


def make_tables():
    n = np.arange(N)
    ky = np.array(row_order())
    kz = np.array(lane_order())
    turn = 2.0 * np.pi / N
    angle_y = turn * ((ky[:, None] * n[None, :]) % N)
    forward_y = np.zeros((128, N))
    forward_y[:64] = np.where(ky < 0, 0.0, 1.0)[:, None] * np.cos(angle_y)
    forward_y[64:] = -np.where(ky < 0, 0.0, 1.0)[:, None] * np.sin(angle_y)
    weight = np.where(ky < 0, 0.0, np.where(ky == 0, 1.0, 2.0))[:, None]
    inverse_y = np.zeros((128, N))
    inverse_y[:64] = weight * np.cos(angle_y)
    inverse_y[64:] = -weight * np.sin(angle_y)
    inverse_y = inverse_y.T
    angle_z = turn * ((n[:, None] * kz[None, :]) % N)
    forward_z = np.concatenate([np.cos(angle_z), np.sin(angle_z)], axis=1)
    inverse_z = np.concatenate([np.cos(angle_z.T), np.sin(angle_z.T)], axis=1)
    x = np.concatenate([np.arange(0, N, 2), np.arange(1, N, 2)])
    angle_x = turn * ((n[:, None] * x[None, :]) % N)
    forward_x = np.concatenate([np.cos(angle_x), np.sin(angle_x)], axis=0)
    inverse_x = np.concatenate([np.cos(angle_x.T), np.sin(angle_x.T)], axis=0)
    lanes = np.zeros((N, N))
    lanes[kz % N, np.arange(N)] = 1.0
    return (
        left_table(forward_y),
        right_table(forward_z),
        right_table(inverse_z),
        left_table(inverse_y),
        left_table(forward_x),
        left_table(inverse_x),
        lanes.astype(ml_dtypes.bfloat16),
    )


def dot(a, b):
    return jnp.dot(a, b, preferred_element_type=jnp.float32)


def halves(value):
    high = value.astype(jnp.bfloat16)
    low = (value - high.astype(jnp.float32)).astype(jnp.bfloat16)
    return high, low


def table_times(table, value):
    high, low = halves(value)
    return dot(table, jnp.concatenate([high, high, low], axis=0))


def times_table(value, table):
    high, low = halves(value)
    return dot(jnp.concatenate([high, low, high], axis=1), table)


def lane_ids(rows):
    return lax.broadcasted_iota(jnp.int32, (rows, 128), 1)


def sublane_ids():
    return lax.broadcasted_iota(jnp.int32, (8, 128), 0)


def turn_lanes(value, by):
    return pltpu.roll(value, by % 128, 1)


def quarters(a):
    lane = lane_ids(a[0].shape[0])
    low = lane < 64
    even = (lane // 32) % 2 == 0
    u = [None] * 4
    for k in range(2):
        u[k] = jnp.where(low, a[k], turn_lanes(a[k + 2], 64))
        u[k + 2] = jnp.where(low, turn_lanes(a[k], 64), a[k + 2])
    out = [None] * 4
    for k in (0, 2):
        out[k] = jnp.where(even, u[k], turn_lanes(u[k + 1], 32))
        out[k + 1] = jnp.where(even, turn_lanes(u[k], -32), u[k + 1])
    return out


def to_chunks(q):
    def chunk(g, c):
        return q[g][8 * c : 8 * c + 8]

    def merge(first, second):
        return jnp.where(inner, first, turn_lanes(second, 16))

    sub = sublane_ids()
    inner = lane_ids(8) % 32 < 16
    x = merge(chunk(3, 2), jnp.where(sub == 0, chunk(1, 6), chunk(3, 3)))
    y = merge(chunk(2, 5), jnp.where(sub < 3, chunk(1, 6), chunk(3, 1)))
    y = jnp.where(sub == 0, chunk(2, 5), y)
    z = jnp.where(sub < 3, chunk(3, 1), jnp.where(sub == 3, chunk(0, 7), chunk(1, 6)))
    out = [chunk(0, c) for c in range(7)] + [chunk(1, c) for c in range(6)]
    out += [chunk(2, c) for c in range(5)] + [chunk(3, 0)]
    return out + [x, y, z, chunk(0, 7)]


def from_chunks(chunks):
    sub = sublane_ids()
    inner = lane_ids(8) % 32 < 16
    zero = jnp.zeros((8, 128), jnp.float32)
    x, y, z, last = chunks[19:]
    x_second = jnp.where(inner, turn_lanes(x, -16), zero)
    y_second = jnp.where(inner, turn_lanes(y, -16), zero)
    x_first = jnp.where(inner, x, zero)
    y_first = jnp.where(inner | (sub == 0), y, zero)
    q0 = chunks[0:7] + [jnp.where(sub == 0, last, jnp.where(sub == 3, z, zero))]
    mixed = jnp.where(sub == 0, x_second, jnp.where(sub < 3, y_second, jnp.where(sub == 3, zero, z)))
    q1 = chunks[7:13] + [mixed, zero]
    q2 = chunks[13:18] + [y_first, zero, zero]
    q3 = [chunks[18], jnp.where(sub < 3, z, y_second), x_first, jnp.where(sub == 0, zero, x_second)]
    q3 += [zero] * 4
    return [jnp.concatenate(parts, axis=0) for parts in (q0, q1, q2, q3)]


def forward_planes(densities, ty, wz):
    e = table_times(ty, jnp.concatenate(densities, axis=1))
    real, imag = [], []
    for k in range(len(densities)):
        g = times_table(e[:, 128 * k : 128 * k + 128], wz)
        real.append(g[:64, :128] + g[64:, 128:])
        imag.append(g[64:, :128] - g[:64, 128:])
    return real, imag


def inverse_planes(real, imag, wzi, tyi):
    parts = []
    for re, im in zip(real, imag):
        g = times_table(jnp.concatenate([re, im], axis=0), wzi)
        parts.append(
            jnp.concatenate([g[:64, :128] - g[64:, 128:], g[64:, :128] + g[:64, 128:]], axis=0)
        )
    v = table_times(tyi, jnp.concatenate(parts, axis=1))
    return [v[:, 128 * k : 128 * k + 128] for k in range(len(parts))]


def store_chunks(buf, pitch, row, chunks):
    for m, value in enumerate(chunks):
        buf[pl.ds((m % 8) * 8 * pitch + row(m // 8), 8, stride=pitch), :] = value


def load_chunks(buf, pitch, row):
    return [buf[pl.ds((m % 8) * 8 * pitch + row(m // 8), 8, stride=pitch), :] for m in range(CHUNKS)]


def pack_quad(buf, pitch, first, real, imag):
    for ri, part in enumerate((real, imag)):
        store_chunks(buf, pitch, lambda j: first + j * 2 + ri, to_chunks(quarters(part)))


def unpack(buf, pitch, row):
    return quarters(from_chunks(load_chunks(buf, pitch, row)))


def spectrum(buf, pitch, second, row):
    return jnp.concatenate(
        [buf[pl.ds(plane * second + row, 64, stride=pitch), :] for plane in range(2)], axis=0
    )


def convolve(real, imag, kernel_of, tx, txi):
    p = table_times(tx, jnp.concatenate(real + imag, axis=1))
    c, s = p[:128], p[128:]
    blocks = []
    for j in range(3):
        re, im = slice(128 * j, 128 * j + 128), slice(384 + 128 * j, 512 + 128 * j)
        blocks.append((c[:, re] + s[:, im]) * kernel_of[j])
    for j in range(3):
        re, im = slice(128 * j, 128 * j + 128), slice(384 + 128 * j, 512 + 128 * j)
        blocks.append((c[:, im] - s[:, re]) * kernel_of[j])
    p = table_times(txi, jnp.concatenate(blocks, axis=1))
    c, s = p[:128], p[128:]
    real, imag = [], []
    for j in range(3):
        re, im = slice(128 * j, 128 * j + 128), slice(384 + 128 * j, 512 + 128 * j)
        real.append(c[:, re] - s[:, im])
        imag.append(c[:, im] + s[:, re])
    return real, imag


def middle_cross(recv, send, kernel_of, tx, txi):
    second = PEERS * PITCH_C
    parts = [[spectrum(recv, PITCH_C, second, j * 2 + ri) for j in range(3)] for ri in range(2)]
    for ri, new in enumerate(convolve(*parts, kernel_of, tx, txi)):
        for j in range(3):
            for plane in range(2):
                send[pl.ds(plane * second + j * 2 + ri, 64, stride=PITCH_C), :] = new[j][
                    64 * plane : 64 * plane + 64
                ]


def middle_first(recv, send, kernel_of, tx, txi):
    lane = lane_ids(64)
    real, imag = [], []
    for j in range(3):
        r0, r1, r2 = (recv[pl.ds(j * 3 + i, 64, stride=PITCH_1), :] for i in range(3))
        real.append(jnp.concatenate([r0, r1], axis=0))
        i0 = jnp.where(lane < 32, turn_lanes(r0, 32), turn_lanes(r2, 32))
        i1 = jnp.where(lane < 32, turn_lanes(r1, 32), turn_lanes(r2, -32))
        imag.append(jnp.concatenate([i0, i1], axis=0))
    real, imag = convolve(real, imag, kernel_of, tx, txi)
    for j in range(3):
        i0, i1 = imag[j][:64], imag[j][64:]
        rows = (
            jnp.where(lane < 96, real[j][:64], turn_lanes(i0, 96)),
            jnp.where(lane < 96, real[j][64:], turn_lanes(i1, 96)),
            jnp.where(lane < 64, turn_lanes(i0, -32), turn_lanes(i1, 32)),
        )
        for i in range(3):
            send[pl.ds(j * 3 + i, 64, stride=PITCH_1), :] = rows[i]


def middle_second(recv, send, kernel_of, tx, txi):
    low = lane_ids(128) < 64

    def cross(s):
        turned = turn_lanes(s, 64)
        return jnp.where(low, turned, -turned)

    blocks = [spectrum(recv, PITCH_2, 1, j * 2) for j in range(3)]
    p = table_times(tx, jnp.concatenate(blocks, axis=1))
    blocks = []
    for j in range(3):
        at = slice(128 * j, 128 * j + 128)
        blocks.append((p[:128, at] + cross(p[128:, at])) * kernel_of[j])
    p = table_times(txi, jnp.concatenate(blocks, axis=1))
    for j in range(3):
        at = slice(128 * j, 128 * j + 128)
        new = p[:128, at] - cross(p[128:, at])
        for plane in range(2):
            send[pl.ds(j * 2 + plane, 64, stride=PITCH_2), :] = new[64 * plane : 64 * plane + 64]


def place_of(g):
    line = g // 4
    return 16 * ((g % 4 + 3 - line % 4) % 4) + line


def frequency_at(pos):
    ky = jnp.where((pos >= 25) & (pos <= 31), pos - 1, pos)
    ky = jnp.where((pos >= 52) & (pos <= 55), pos - 4, ky)
    for at, value in ((24, 31), (48, 54), (49, 52), (50, 53), (51, 55), (56, 57), (59, 56)):
        ky = jnp.where(pos == at, value, ky)
    return ky


def position_of(ky):
    pos = jnp.where((ky >= 24) & (ky <= 30), ky + 1, ky)
    pos = jnp.where((ky >= 48) & (ky <= 51), ky + 4, pos)
    for at, value in ((24, 31), (48, 54), (49, 52), (50, 53), (51, 55), (56, 57), (59, 56)):
        pos = jnp.where(ky == value, at, pos)
    return pos


def pick(cases, otherwise):
    out = otherwise
    for condition, case in reversed(cases):
        out = jnp.where(condition, case, out)
    return out


def piece_of(place, j):
    m = j * 8 + place // 8
    sub = place % 8
    in_z = m == 21
    cases = [
        (m < 7, 0), (m < 13, 1), (m < 18, 2), (m < 20, 3), (m == 20, 2),
        (in_z & (sub < 3), 3), (in_z & (sub > 3), 1),
    ]
    q = pick(cases, 0)
    cases = [
        (m < 7, m), (m < 13, m - 7), (m < 18, m - 13), (m == 18, 0), (m == 19, 2), (m == 20, 5),
        (in_z & (sub < 3), 1), (in_z & (sub > 3), 6),
    ]
    c = pick(cases, 7)
    merged = (m == 19) | ((m == 20) & (sub > 0))
    from_1 = ((m == 19) & (sub == 0)) | ((m == 20) & (sub < 3))
    q_outer = jnp.where(merged, jnp.where(from_1, 1, 3), q)
    c_outer = jnp.where(merged, jnp.where(from_1, 6, jnp.where(m == 19, 3, 1)), c)
    inner = (frequency_at(c * 8 + sub), q)
    return inner, (frequency_at(c_outer * 8 + sub), q_outer), merged


def owner_of(ky, q):
    pos = position_of(ky)
    c = pos // 8
    sub = pos % 8
    cases = [
        ((q == 0) & (c < 7), c), ((q == 0) & (sub == 0), 22), (q == 0, 21),
        ((q == 1) & (c < 6), c + 7), ((q == 1) & (sub == 0), 19), ((q == 1) & (sub < 3), 20),
        (q == 1, 21), ((q == 2) & (c < 5), c + 13), (q == 2, 20),
        (c == 0, 18), ((c == 1) & (sub < 3), 21), (c == 1, 20),
    ]
    m = pick(cases, 19)
    second = ((q == 1) & (c == 6) & (sub < 3)) | (
        (q == 3) & (((c == 1) & (sub >= 3)) | (c == 3))
    )
    exists = (
        (q == 0)
        | ((q == 1) & ((c < 6) | ((c == 6) & (sub != 3))))
        | ((q == 2) & (c < 6))
        | ((q == 3) & ((c < 3) | ((c == 3) & (sub > 0))))
    ) & (ky <= LAST_KEPT)
    m = jnp.where(exists, m, 0)
    place = (m % 8) * 8 + sub
    line = place % 16
    return exists, line * 4 + (place // 16 + 1 + line) % 4, jnp.where(second, 3, m // 8)


def kernel_table(mask, second, piece):
    (ky_inner, q_inner), (ky_outer, q_outer), merged = piece
    lane = lane_ids(32)
    mask = jnp.where((lane % 32 >= 16) & merged, turn_lanes(second, 16), mask)
    rows = []
    for block in range(4):
        part = jnp.where(lane // 32 == block, mask, 0.0)
        part = part + turn_lanes(part, 64)
        rows.append(part + turn_lanes(part, 32))
    kept = jnp.concatenate(rows, axis=0)
    kx = lax.broadcasted_iota(jnp.int32, (128, 128), 0)
    kx = jnp.where(kx < 64, kx, kx - 128)
    inner = lane_ids(128) % 32 < 16
    i = lane_ids(128) % 16
    ky = jnp.where(inner, ky_inner, ky_outer)
    first = jnp.where(inner, 16 * q_inner, 16 * q_outer + jnp.where(merged, 0, 8))
    kz = jnp.where(i < 8, first + i, 7 - first - i)
    squared = kx * kx + ky * ky + kz * kz
    safe = jnp.maximum(squared, 1).astype(jnp.float32)
    return jnp.where(squared > 0, (8.0 * math.pi / N**3) / safe, 0.0) * kept


def body(
    occ, orb_in, kept_in, ty_in, wz_in, wzi_in, tyi_in, tx_in, txi_in, lanes_in, out,
    chip, kept, ty, wz, wzi, tyi, tx, txi, lanes, far, pvr, df, merged, acc, pf, mask_send, mask_recv,
    f_s1, f_r1, b_s1, b_r1, f_s2, f_r2, b_s2, b_r2, f_sc, f_rc, b_sc, b_rc, sem, sem_xy,
):
    b = lax.axis_index("band")
    g = lax.axis_index("grid")
    half = b // 2
    core = b % 2
    other_core = half * 2 + (1 - core)
    other_half = (1 - half) * 2 + core

    mask_recv[...] = jnp.zeros_like(mask_recv)
    u, v = chip.at[0], chip.at[1]
    act, pv = acc.at[0], acc.at[1]
    loads = [
        pltpu.make_async_copy(source, target, sem.at[LS + i])
        for i, (source, target) in enumerate(
            [
                (orb_in, u), (ty_in, ty), (wz_in, wz), (kept_in, kept), (lanes_in, lanes),
                (tx_in, tx), (txi_in, txi), (wzi_in, wzi), (tyi_in, tyi),
            ]
        )
    ]
    for load in loads:
        load.start()

    def on_line(k):
        return g - g % 4 + (g + k) % 4

    def in_plane(k):
        return ((g // 4 + k) % 16) * 4 + g % 4

    barrier = pltpu.get_barrier_semaphore()

    def greet(semaphore, band, grid):
        pl.semaphore_signal(
            semaphore, inc=1, device_id={"band": band, "grid": grid}, device_id_type=MESH
        )

    for k in range(4):
        greet(barrier, other_half, on_line(k))
    for k in range(1, 4):
        greet(barrier, b, on_line(k))
    for k in range(1, 16):
        greet(barrier, b, in_plane(k))
    greet(barrier, other_core, g)

    def remote(src, dst, send, recv, band=None, grid=None):
        device = {"band": b if band is None else band, "grid": g if grid is None else grid}
        return pltpu.make_async_remote_copy(
            src_ref=src, dst_ref=dst, send_sem=sem.at[send], recv_sem=sem.at[recv],
            device_id=device, device_id_type=MESH,
        )

    class Cut:
        def __init__(self, src, dst, send, recv, band):
            self.parts = [
                remote(src.at[i, pl.ds(r, N // CUTS)], dst.at[i, pl.ds(r, N // CUTS)], send, recv, band=band)
                for r in range(0, N, N // CUTS)
                for i in range(2)
            ]
            self.whole = remote(src, dst, send, recv, band=band)

        def start(self):
            for part in self.parts:
                part.start()

        def wait_recv(self):
            self.whole.wait_recv()

        def wait_send(self):
            self.whole.wait_send()

    pl.semaphore_wait(barrier, 23)
    for k in range(1, 16):
        greet(sem_xy, b, in_plane(k))
    loads[0].wait()
    to_half = Cut(u.at[:, 1 - half], far.at[0], AS, AR, other_half)
    to_half.start()
    to_core = remote(u, v, E1S, E1R, band=other_core)
    to_core.start()

    for load in loads[1:3]:
        load.wait()
    ty, wz = ty[...], wz[...]
    own = [
        forward_planes([u[0, p] * u[0, p], u[0, p] * u[1, p], u[1, p] * u[1, p]], ty, wz)
        for p in range(2)
    ]

    for p in range(2):
        real, imag = own[p]
        chunks = to_chunks(quarters(real + imag[:1]))
        store_chunks(f_s1, PITCH_1, lambda j: j * 3 + p, chunks)
    chunks = to_chunks(quarters(own[0][1][1:] + own[1][1][1:]))
    store_chunks(f_s1, PITCH_1, lambda j: j * 3 + 2, chunks)

    for load in loads[3:]:
        load.wait()
    tx, txi, wzi, tyi = tx[...], txi[...], wzi[...], tyi[...]
    for row in range(2):
        plane = dot(kept[:, row, :].astype(jnp.float32).astype(jnp.bfloat16), lanes[...])
        groups = quarters([plane[32 * k : 32 * k + 32] for k in range(4)])
        for q in range(4):
            mask_send[row * 4 + q] = groups[q]

    def mask_copies(act_on_remote, act_on_local):
        def one(i, carry):
            exists, t, j = owner_of(2 * g + i // 4, i % 4)

            @pl.when(exists & (t != g))
            def _():
                act_on_remote(
                    pltpu.make_async_remote_copy(
                        src_ref=mask_send.at[i], dst_ref=mask_recv.at[j],
                        send_sem=sem.at[MS + i], recv_sem=sem.at[MR + j],
                        device_id={"band": b, "grid": t}, device_id_type=MESH,
                    )
                )

            if act_on_local is not None:

                @pl.when(exists & (t == g))
                def _():
                    act_on_local(
                        pltpu.make_async_copy(mask_send.at[i], mask_recv.at[j], sem.at[MR + j])
                    )

            return carry

        lax.fori_loop(0, 8, one, 0)

    mask_to_core = remote(mask_recv, mask_recv, MFS, MFR, band=other_core)

    def slot(index, pitch, rows):
        return pl.ds(pl.multiple_of(index * pitch, pitch), rows)

    place = place_of(g)
    three = place < OWN_THREE

    def sized(count_three, act):
        @pl.when(count_three)
        def _():
            act(3)

        @pl.when(jnp.logical_not(count_three))
        def _():
            act(2)

    my_line, my_z = g // 4, g % 4
    my_first, my_turn = my_line % 4, my_line // 4

    def forward(src, dst, pitch, piece, send, recv, to):
        there = to * PEERS
        both = dst.shape[0] > (PEERS + 1) * pitch
        target_slot = (half * PEERS if both else 0) + g
        source_slot = there if both else 0

        def start(pieces, p, t):
            rows = pieces * piece
            source, target = src.at[slot(source_slot + p, pitch, rows)], dst.at[slot(target_slot, pitch, rows)]
            remote(source, target, send, recv, band=to * 2 + core, grid=t).start()

        start_z = my_z + jnp.where(to == half, 0, 2)
        for step in (2, 1, 3, 0):
            z = (start_z + step) % 4
            for r in (1, 2, 3, 0):
                first = (z + r) % 4

                def one(n, carry):
                    q = n + my_turn
                    line = first + 4 * jnp.where(q >= 4, q - 4, q)
                    p, t = 16 * (3 - r) + line, 4 * line + z
                    if r > 0:
                        start(3, p, t)
                    else:
                        sized(line == 0, lambda pieces: start(pieces, p, t))
                    return carry

                if step == 0:

                    @pl.when((first != my_first) | (to != half))
                    def _():
                        one(0, 0)

                lax.fori_loop(0 if step > 0 else 1, 4, one, 0)

        @pl.when(to == half)
        def _():
            def local(pieces):
                rows = pieces * piece
                source = src.at[slot(source_slot + place, pitch, rows)]
                pltpu.make_async_copy(source, dst.at[slot(target_slot, pitch, rows)], sem.at[recv]).start()

            sized(three, local)

    def backward(src, dst, pitch, piece, send, recv, to):
        both = dst.shape[0] > (PEERS + 1) * pitch
        target_slot = (half * PEERS if both else 0) + place
        source_slot = to * PEERS if both else 0

        def messages(pieces):
            rows = pieces * piece
            target = dst.at[slot(target_slot, pitch, rows)]

            def start(t):
                source = src.at[slot(source_slot + t, pitch, rows)]
                remote(source, target, send, recv, band=to * 2 + core, grid=t).start()

            start_z = my_z + jnp.where(to == half, 0, 2)
            for step in (2, 1, 3, 0):
                z = (start_z + step) % 4

                def one(k, carry):
                    line = my_line + k
                    start(4 * jnp.where(line >= 16, line - 16, line) + z)
                    return carry

                lax.fori_loop(0 if step > 0 else 1, 16, one, 0)

            @pl.when(to != half)
            def _():
                start(4 * my_line + start_z % 4)

            @pl.when(to == half)
            def _():
                source = src.at[slot(source_slot + g, pitch, rows)]
                pltpu.make_async_copy(source, target, sem.at[recv]).start()

        sized(three, messages)

    def arrived_own(dst, count, piece, semaphore):
        sized(three, lambda pieces: arrived(dst, count * pieces * piece, semaphore))

    def arrived(dst, rows, recv):
        whole = dst.at[pl.ds(0, rows)]
        pltpu.make_async_copy(whole, whole, sem.at[recv]).wait()

    pl.semaphore_wait(sem_xy, 15)
    forward(f_s1, f_r1, PITCH_1, PIECE_1, F1S, F1R, half)

    @pl.when(core == 0)
    def _():
        mask_copies(lambda c: c.start(), lambda c: c.start())

    v0, v1 = core, 1 - core
    to_core.wait_recv()
    real, imag = forward_planes(
        [u[0, p] * v[v0, p] for p in range(2)] + [u[1, p] * v[v1, p] for p in range(2)], ty, wz
    )
    for p in range(2):
        chunks = to_chunks(quarters([real[p], real[2 + p], imag[p], imag[2 + p]]))
        store_chunks(f_s2, PITCH_2, lambda j: j * 2 + p, chunks)

    first_quad = half * core
    quads = ((first_quad, 0, core), (1 - first_quad, 1, 1 - core))

    def pack_cross(quad, f, n):
        near = [chip[n, i, half] for i in (0, half, 1 - half, 1)]
        d = [a * far[f, i] for a, i in zip(near, (0, 1 - half, half, 1))]
        pack_quad(f_sc, PITCH_C, quad * (PEERS * PITCH_C), *forward_planes(d, ty, wz))

    to_half.wait_recv()
    far_to_core = remote(far.at[0], far.at[1], E3S, E3R, band=other_core)
    far_to_core.start()
    pack_cross(*quads[0])
    forward(f_sc, f_rc, PITCH_C, PIECE_C, FCS, FCR, quads[0][0])
    far_to_core.wait_recv()
    pack_cross(*quads[1])
    forward(f_sc, f_rc, PITCH_C, PIECE_C, FCS, FCR, quads[1][0])

    forward(f_s2, f_r2, PITCH_2, PIECE_2, F2S, F2R, half)
    two_rows = piece_of(place, 2)[2] & three
    @pl.when(core == 0)
    def _():
        for j, expected in enumerate((True, True, three, two_rows)):

            @pl.when(expected)
            def _():
                pltpu.make_async_copy(mask_recv.at[j], mask_recv.at[j], sem.at[MR + j]).wait()

        mask_to_core.start()

    @pl.when(core == 1)
    def _():
        mask_to_core.wait_recv()

    kernel_of = [kernel_table(mask_recv[j], mask_recv[3], piece_of(place, j)) for j in range(3)]

    arrived_own(f_r1, PEERS, PIECE_1, F1R)
    middle_first(f_r1, b_s1, kernel_of, tx, txi)
    backward(b_s1, b_r1, PITCH_1, PIECE_1, B1S, B1R, half)
    arrived_own(f_r2, PEERS, PIECE_2, F2R)
    middle_second(f_r2, b_s2, kernel_of, tx, txi)
    arrived_own(f_rc, 2 * PEERS, PIECE_C, FCR)
    middle_cross(f_rc, b_sc, kernel_of, tx, txi)
    backward(b_sc, b_rc, PITCH_C, PIECE_C, BCS, BOR, 1 - half)
    backward(b_sc, b_rc, PITCH_C, PIECE_C, BCS, BCR, half)

    mine = half * 4 + core * 2
    theirs = half * 4 + (1 - core) * 2
    arrived(b_r1, PIECES * PIECE_1, B1R)
    rest = unpack(b_r1, PITCH_1, lambda j: j * 3 + 2)
    for p in range(2):
        parts = unpack(b_r1, PITCH_1, lambda j: j * 3 + p)
        pot = inverse_planes(parts[:3], parts[3:] + rest[2 * p : 2 * p + 2], wzi, tyi)
        o0, o1 = occ[mine] * u[0, p], occ[mine + 1] * u[1, p]
        act[0, p] = o0 * pot[0] + o1 * pot[1]
        act[1, p] = o0 * pot[1] + o1 * pot[2]

    pv[...] = jnp.zeros_like(pv)
    arrived(b_rc, PIECES * PIECE_C, BOR)
    backward(b_s2, b_r2, PITCH_2, PIECE_2, B2S, B2R, half)
    arrived(b_rc, PIECES * PIECE_C, BCR)

    def cross_terms(quad, f, n):
        first = quad * (PEERS * PITCH_C)
        real, imag = (unpack(b_rc, PITCH_C, lambda j: first + j * 2 + ri) for ri in range(2))
        p00, p01, p10, p11 = inverse_planes(real, imag, wzi, tyi)
        p01, p10 = jnp.where(half == 0, p01, p10), jnp.where(half == 0, p10, p01)
        here = half * 4 + jnp.where(n == 0, core, 1 - core) * 2
        there = (1 - half) * 4 + (core if f == 0 else 1 - core) * 2
        n0, n1 = occ[here] * chip[n, 0, half], occ[here + 1] * chip[n, 1, half]
        f0, f1 = occ[there] * far[f, 0], occ[there + 1] * far[f, 1]
        pf[f, 0] = n0 * p00 + n1 * p10
        pf[f, 1] = n0 * p01 + n1 * p11
        acc[n, 0, half] += f0 * p00 + f1 * p01
        acc[n, 1, half] += f0 * p10 + f1 * p11

    cross_terms(*quads[1])
    merge = remote(pf.at[1], merged, X1S, X1R, band=other_core)
    merge.start()
    cross_terms(*quads[0])
    merge.wait_recv()
    pf[0] += merged[...]
    home = Cut(pf.at[0], df, DS, DR, other_half)
    home.start()

    arrived(b_r2, PIECES * PIECE_2, B2R)
    for p in range(2):
        a_re, b_re, a_im, b_im = unpack(b_r2, PITCH_2, lambda j: j * 2 + p)
        pot = inverse_planes([a_re, b_re], [a_im, b_im], wzi, tyi)
        act[0, p] += occ[theirs + v0] * v[v0, p] * pot[0]
        act[1, p] += occ[theirs + v1] * v[v1, p] * pot[1]
        pv[v0, p] += occ[mine] * u[0, p] * pot[0]
        pv[v1, p] += occ[mine + 1] * u[1, p] * pot[1]
    swap = remote(pv, pvr, E2S, E2R, band=other_core)
    swap.start()
    swap.wait_recv()
    for i in range(2):
        out[i, half] = -(act[i, half] + pvr[i, half])
        acc[0, i, 1 - half] += pvr[i, 1 - half]
    home.wait_recv()
    for i in range(2):
        out[i, 1 - half] = -(act[i, 1 - half] + df[i])

    to_core.wait_send()
    to_half.wait_send()

    @pl.when(core == 0)
    def _():
        mask_to_core.wait_send()
        mask_copies(lambda c: c.wait_send(), None)

    for src, pieces, piece, send in (
        (f_s1, PIECES, PIECE_1, F1S),
        (f_s2, PIECES, PIECE_2, F2S),
        (f_sc, 2 * PIECES, PIECE_C, FCS),
    ):
        sized(three, lambda mine: arrived(src, (pieces - mine) * piece, send))
    arrived_own(b_s1, PEERS - 1, PIECE_1, B1S)
    arrived_own(b_s2, PEERS - 1, PIECE_2, B2S)
    arrived_own(b_sc, 2 * PEERS - 1, PIECE_C, BCS)
    far_to_core.wait_send()
    merge.wait_send()
    swap.wait_send()
    home.wait_send()


def on_device(orbitals, occupation, kept_modes):
    block = pltpu.VMEM((2, 2, N, N), jnp.float32)
    twice = pltpu.VMEM((2, 2, 2, N, N), jnp.float32)
    plane = pltpu.VMEM((2, N, N), jnp.float32)
    planes = pltpu.VMEM((2, 2, N, N), jnp.float32)
    messages = [
        pltpu.VMEM(((slots + 1) * pitch, 128), jnp.float32)
        for slots, pitch in ((PEERS, PITCH_1), (PEERS, PITCH_2), (2 * PEERS, PITCH_C))
        for _ in range(4)
    ]
    tables = make_tables()
    loaded = [twice, pltpu.VMEM(kept_modes.shape, jnp.int32)]
    loaded += [pltpu.VMEM(t.shape, jnp.bfloat16) for t in tables]
    return pl.pallas_call(
        body,
        out_shape=jax.ShapeDtypeStruct(orbitals.shape, jnp.float32),
        in_specs=[pl.BlockSpec(memory_space=pltpu.SMEM)] + [pl.BlockSpec(memory_space=pltpu.HBM)] * 9,
        out_specs=pl.BlockSpec(memory_space=pltpu.VMEM),
        scratch_shapes=loaded
        + [planes, block, plane, plane, twice, planes]
        + [pltpu.VMEM((8, 32, 128), jnp.float32), pltpu.VMEM((4, 32, 128), jnp.float32)]
        + messages
        + [
            pltpu.SemaphoreType.DMA((NSEM,)),
            pltpu.SemaphoreType.REGULAR,
        ],
        compiler_params=pltpu.CompilerParams(
            collective_id=1, has_side_effects=True, vmem_limit_bytes=60 << 20
        ),
        name="exchange",
    )(occupation, orbitals, kept_modes, *(jnp.asarray(t) for t in tables))


def solution(mesh):
    return jax.shard_map(
        on_device,
        mesh=mesh,
        in_specs=(P("band", "grid", None, None), P(), P(None, "grid", None)),
        out_specs=P("band", "grid", None, None),
        check_vma=False,
    )
```

```python
import functools
import math

import jax
import jax.numpy as jnp
import ml_dtypes
import numpy as np
from jax import lax
from jax.experimental import pallas as pl
from jax.experimental.pallas import tpu as pltpu
from jax.sharding import PartitionSpec as P

MESH = pl.DeviceIdType.MESH
N = 128
PEERS = 64
PIECE_1, PITCH_1 = 3, 16
PIECE_2, PITCH_2 = 2, 8
PIECE_C, PITCH_C = 2, 8
CHUNKS = 23
OWN_THREE = 49
PIECES = 3 * OWN_THREE + 2 * (PEERS - OWN_THREE)
LAST_KEPT = 57
CUTS = 2

E1S, E1R, AS, AR, F1S, F1R, F2S, F2R, FCS, FCR, B1S, B1R, B2S, B2R, BCS, BCR = range(16)
E2S, E2R, E3S, E3R, X1S, X1R, DS, DR, MFS, MFR, BOR = range(16, 27)
MR = 27
MS = 31
LS = 39
NSEM = 48


def row_order():
    order = list(range(24)) + [31] + list(range(24, 31)) + list(range(32, 48))
    order += [54, 52, 53, 55, 48, 49, 50, 51] + [57, -1, -1, 56] + [-1] * 4
    return order


def lane_order():
    out = []
    for q in range(4):
        for first in (16 * q, 16 * q + 8):
            out += [first + i for i in range(8)]
            out += [-first - 1 - i for i in range(8)]
    return out


def split(table):
    high = table.astype(ml_dtypes.bfloat16)
    low = (table - high.astype(np.float64)).astype(ml_dtypes.bfloat16)
    return high, low


def left_table(table):
    high, low = split(table)
    return np.concatenate([high, low, high], axis=1)


def right_table(table):
    high, low = split(table)
    return np.concatenate([high, high, low], axis=0)


def make_tables():
    n = np.arange(N)
    ky = np.array(row_order())
    kz = np.array(lane_order())
    turn = 2.0 * np.pi / N
    angle_y = turn * ((ky[:, None] * n[None, :]) % N)
    forward_y = np.zeros((128, N))
    forward_y[:64] = np.where(ky < 0, 0.0, 1.0)[:, None] * np.cos(angle_y)
    forward_y[64:] = -np.where(ky < 0, 0.0, 1.0)[:, None] * np.sin(angle_y)
    weight = np.where(ky < 0, 0.0, np.where(ky == 0, 1.0, 2.0))[:, None]
    inverse_y = np.zeros((128, N))
    inverse_y[:64] = weight * np.cos(angle_y)
    inverse_y[64:] = -weight * np.sin(angle_y)
    inverse_y = inverse_y.T
    angle_z = turn * ((n[:, None] * kz[None, :]) % N)
    forward_z = np.concatenate([np.cos(angle_z), np.sin(angle_z)], axis=1)
    inverse_z = np.concatenate([np.cos(angle_z.T), np.sin(angle_z.T)], axis=1)
    x = np.concatenate([np.arange(0, N, 2), np.arange(1, N, 2)])
    angle_x = turn * ((n[:, None] * x[None, :]) % N)
    forward_x = np.concatenate([np.cos(angle_x), np.sin(angle_x)], axis=0)
    inverse_x = np.concatenate([np.cos(angle_x.T), np.sin(angle_x.T)], axis=0)
    lanes = np.zeros((N, N))
    lanes[kz % N, np.arange(N)] = 1.0
    return (
        left_table(forward_y),
        right_table(forward_z),
        right_table(inverse_z),
        left_table(inverse_y),
        left_table(forward_x),
        left_table(inverse_x),
        lanes.astype(ml_dtypes.bfloat16),
    )


def dot(a, b):
    return jnp.dot(a, b, preferred_element_type=jnp.float32)


def halves(value):
    high = value.astype(jnp.bfloat16)
    low = (value - high.astype(jnp.float32)).astype(jnp.bfloat16)
    return high, low


def table_times(table, value):
    high, low = halves(value)
    return dot(table, jnp.concatenate([high, high, low], axis=0))


def times_table(value, table):
    high, low = halves(value)
    return dot(jnp.concatenate([high, low, high], axis=1), table)


def lane_ids(rows):
    return lax.broadcasted_iota(jnp.int32, (rows, 128), 1)


def sublane_ids():
    return lax.broadcasted_iota(jnp.int32, (8, 128), 0)


def turn_lanes(value, by):
    return pltpu.roll(value, by % 128, 1)


def quarters(a):
    lane = lane_ids(a[0].shape[0])
    low = lane < 64
    even = (lane // 32) % 2 == 0
    u = [None] * 4
    for k in range(2):
        u[k] = jnp.where(low, a[k], turn_lanes(a[k + 2], 64))
        u[k + 2] = jnp.where(low, turn_lanes(a[k], 64), a[k + 2])
    out = [None] * 4
    for k in (0, 2):
        out[k] = jnp.where(even, u[k], turn_lanes(u[k + 1], 32))
        out[k + 1] = jnp.where(even, turn_lanes(u[k], -32), u[k + 1])
    return out


def to_chunks(q):
    def chunk(g, c):
        return q[g][8 * c : 8 * c + 8]

    def merge(first, second):
        return jnp.where(inner, first, turn_lanes(second, 16))

    sub = sublane_ids()
    inner = lane_ids(8) % 32 < 16
    x = merge(chunk(3, 2), jnp.where(sub == 0, chunk(1, 6), chunk(3, 3)))
    y = merge(chunk(2, 5), jnp.where(sub < 3, chunk(1, 6), chunk(3, 1)))
    y = jnp.where(sub == 0, chunk(2, 5), y)
    z = jnp.where(sub < 3, chunk(3, 1), jnp.where(sub == 3, chunk(0, 7), chunk(1, 6)))
    out = [chunk(0, c) for c in range(7)] + [chunk(1, c) for c in range(6)]
    out += [chunk(2, c) for c in range(5)] + [chunk(3, 0)]
    return out + [x, y, z, chunk(0, 7)]


def from_chunks(chunks):
    sub = sublane_ids()
    inner = lane_ids(8) % 32 < 16
    zero = jnp.zeros((8, 128), jnp.float32)
    x, y, z, last = chunks[19:]
    x_second = jnp.where(inner, turn_lanes(x, -16), zero)
    y_second = jnp.where(inner, turn_lanes(y, -16), zero)
    x_first = jnp.where(inner, x, zero)
    y_first = jnp.where(inner | (sub == 0), y, zero)
    q0 = chunks[0:7] + [jnp.where(sub == 0, last, jnp.where(sub == 3, z, zero))]
    mixed = jnp.where(sub == 0, x_second, jnp.where(sub < 3, y_second, jnp.where(sub == 3, zero, z)))
    q1 = chunks[7:13] + [mixed, zero]
    q2 = chunks[13:18] + [y_first, zero, zero]
    q3 = [chunks[18], jnp.where(sub < 3, z, y_second), x_first, jnp.where(sub == 0, zero, x_second)]
    q3 += [zero] * 4
    return [jnp.concatenate(parts, axis=0) for parts in (q0, q1, q2, q3)]


def forward_planes(densities, ty, wz):
    e = table_times(ty, jnp.concatenate(densities, axis=1))
    real, imag = [], []
    for k in range(len(densities)):
        g = times_table(e[:, 128 * k : 128 * k + 128], wz)
        real.append(g[:64, :128] + g[64:, 128:])
        imag.append(g[64:, :128] - g[:64, 128:])
    return real, imag


def inverse_planes(real, imag, wzi, tyi):
    parts = []
    for re, im in zip(real, imag):
        g = times_table(jnp.concatenate([re, im], axis=0), wzi)
        parts.append(
            jnp.concatenate([g[:64, :128] - g[64:, 128:], g[64:, :128] + g[:64, 128:]], axis=0)
        )
    v = table_times(tyi, jnp.concatenate(parts, axis=1))
    return [v[:, 128 * k : 128 * k + 128] for k in range(len(parts))]


def store_chunks(buf, pitch, row, chunks):
    for m, value in enumerate(chunks):
        buf[pl.ds((m % 8) * 8 * pitch + row(m // 8), 8, stride=pitch), :] = value


def load_chunks(buf, pitch, row):
    return [buf[pl.ds((m % 8) * 8 * pitch + row(m // 8), 8, stride=pitch), :] for m in range(CHUNKS)]


def pack_quad(buf, pitch, first, real, imag):
    for ri, part in enumerate((real, imag)):
        store_chunks(buf, pitch, lambda j: first + j * 2 + ri, to_chunks(quarters(part)))


def unpack(buf, pitch, row):
    return quarters(from_chunks(load_chunks(buf, pitch, row)))


def spectrum(buf, pitch, second, row):
    return jnp.concatenate(
        [buf[pl.ds(plane * second + row, 64, stride=pitch), :] for plane in range(2)], axis=0
    )


def convolve(real, imag, kernel_of, tx, txi):
    p = table_times(tx, jnp.concatenate(real + imag, axis=1))
    c, s = p[:128], p[128:]
    blocks = []
    for j in range(3):
        re, im = slice(128 * j, 128 * j + 128), slice(384 + 128 * j, 512 + 128 * j)
        blocks.append((c[:, re] + s[:, im]) * kernel_of[j])
    for j in range(3):
        re, im = slice(128 * j, 128 * j + 128), slice(384 + 128 * j, 512 + 128 * j)
        blocks.append((c[:, im] - s[:, re]) * kernel_of[j])
    p = table_times(txi, jnp.concatenate(blocks, axis=1))
    c, s = p[:128], p[128:]
    real, imag = [], []
    for j in range(3):
        re, im = slice(128 * j, 128 * j + 128), slice(384 + 128 * j, 512 + 128 * j)
        real.append(c[:, re] - s[:, im])
        imag.append(c[:, im] + s[:, re])
    return real, imag


def middle_cross(recv, send, kernel_of, tx, txi):
    second = PEERS * PITCH_C
    parts = [[spectrum(recv, PITCH_C, second, j * 2 + ri) for j in range(3)] for ri in range(2)]
    for ri, new in enumerate(convolve(*parts, kernel_of, tx, txi)):
        for j in range(3):
            for plane in range(2):
                send[pl.ds(plane * second + j * 2 + ri, 64, stride=PITCH_C), :] = new[j][
                    64 * plane : 64 * plane + 64
                ]


def middle_first(recv, send, kernel_of, tx, txi):
    lane = lane_ids(64)
    real, imag = [], []
    for j in range(3):
        r0, r1, r2 = (recv[pl.ds(j * 3 + i, 64, stride=PITCH_1), :] for i in range(3))
        real.append(jnp.concatenate([r0, r1], axis=0))
        i0 = jnp.where(lane < 32, turn_lanes(r0, 32), turn_lanes(r2, 32))
        i1 = jnp.where(lane < 32, turn_lanes(r1, 32), turn_lanes(r2, -32))
        imag.append(jnp.concatenate([i0, i1], axis=0))
    real, imag = convolve(real, imag, kernel_of, tx, txi)
    for j in range(3):
        i0, i1 = imag[j][:64], imag[j][64:]
        rows = (
            jnp.where(lane < 96, real[j][:64], turn_lanes(i0, 96)),
            jnp.where(lane < 96, real[j][64:], turn_lanes(i1, 96)),
            jnp.where(lane < 64, turn_lanes(i0, -32), turn_lanes(i1, 32)),
        )
        for i in range(3):
            send[pl.ds(j * 3 + i, 64, stride=PITCH_1), :] = rows[i]


def middle_second(recv, send, kernel_of, tx, txi):
    low = lane_ids(128) < 64

    def cross(s):
        turned = turn_lanes(s, 64)
        return jnp.where(low, turned, -turned)

    blocks = [spectrum(recv, PITCH_2, 1, j * 2) for j in range(3)]
    p = table_times(tx, jnp.concatenate(blocks, axis=1))
    blocks = []
    for j in range(3):
        at = slice(128 * j, 128 * j + 128)
        blocks.append((p[:128, at] + cross(p[128:, at])) * kernel_of[j])
    p = table_times(txi, jnp.concatenate(blocks, axis=1))
    for j in range(3):
        at = slice(128 * j, 128 * j + 128)
        new = p[:128, at] - cross(p[128:, at])
        for plane in range(2):
            send[pl.ds(j * 2 + plane, 64, stride=PITCH_2), :] = new[64 * plane : 64 * plane + 64]


def place_of(g):
    line = g // 4
    return 16 * ((g % 4 + 3 - line % 4) % 4) + line


def frequency_at(pos):
    ky = jnp.where((pos >= 25) & (pos <= 31), pos - 1, pos)
    ky = jnp.where((pos >= 52) & (pos <= 55), pos - 4, ky)
    for at, value in ((24, 31), (48, 54), (49, 52), (50, 53), (51, 55), (56, 57), (59, 56)):
        ky = jnp.where(pos == at, value, ky)
    return ky


def position_of(ky):
    pos = jnp.where((ky >= 24) & (ky <= 30), ky + 1, ky)
    pos = jnp.where((ky >= 48) & (ky <= 51), ky + 4, pos)
    for at, value in ((24, 31), (48, 54), (49, 52), (50, 53), (51, 55), (56, 57), (59, 56)):
        pos = jnp.where(ky == value, at, pos)
    return pos


def pick(cases, otherwise):
    out = otherwise
    for condition, case in reversed(cases):
        out = jnp.where(condition, case, out)
    return out


def piece_of(place, j):
    m = j * 8 + place // 8
    sub = place % 8
    in_z = m == 21
    cases = [
        (m < 7, 0), (m < 13, 1), (m < 18, 2), (m < 20, 3), (m == 20, 2),
        (in_z & (sub < 3), 3), (in_z & (sub > 3), 1),
    ]
    q = pick(cases, 0)
    cases = [
        (m < 7, m), (m < 13, m - 7), (m < 18, m - 13), (m == 18, 0), (m == 19, 2), (m == 20, 5),
        (in_z & (sub < 3), 1), (in_z & (sub > 3), 6),
    ]
    c = pick(cases, 7)
    merged = (m == 19) | ((m == 20) & (sub > 0))
    from_1 = ((m == 19) & (sub == 0)) | ((m == 20) & (sub < 3))
    q_outer = jnp.where(merged, jnp.where(from_1, 1, 3), q)
    c_outer = jnp.where(merged, jnp.where(from_1, 6, jnp.where(m == 19, 3, 1)), c)
    inner = (frequency_at(c * 8 + sub), q)
    return inner, (frequency_at(c_outer * 8 + sub), q_outer), merged


def owner_of(ky, q):
    pos = position_of(ky)
    c = pos // 8
    sub = pos % 8
    cases = [
        ((q == 0) & (c < 7), c), ((q == 0) & (sub == 0), 22), (q == 0, 21),
        ((q == 1) & (c < 6), c + 7), ((q == 1) & (sub == 0), 19), ((q == 1) & (sub < 3), 20),
        (q == 1, 21), ((q == 2) & (c < 5), c + 13), (q == 2, 20),
        (c == 0, 18), ((c == 1) & (sub < 3), 21), (c == 1, 20),
    ]
    m = pick(cases, 19)
    second = ((q == 1) & (c == 6) & (sub < 3)) | (
        (q == 3) & (((c == 1) & (sub >= 3)) | (c == 3))
    )
    exists = (
        (q == 0)
        | ((q == 1) & ((c < 6) | ((c == 6) & (sub != 3))))
        | ((q == 2) & (c < 6))
        | ((q == 3) & ((c < 3) | ((c == 3) & (sub > 0))))
    ) & (ky <= LAST_KEPT)
    m = jnp.where(exists, m, 0)
    place = (m % 8) * 8 + sub
    line = place % 16
    return exists, line * 4 + (place // 16 + 1 + line) % 4, jnp.where(second, 3, m // 8)


def kernel_table(coulomb, mask, second, merged):
    lane = lane_ids(32)
    mask = jnp.where((lane % 32 >= 16) & merged, turn_lanes(second, 16), mask)
    rows = []
    for block in range(4):
        part = jnp.where(lane // 32 == block, mask, 0.0)
        part = part + turn_lanes(part, 64)
        rows.append(part + turn_lanes(part, 32))
    return coulomb * jnp.concatenate(rows, axis=0)


def coulomb_table(piece):
    (ky_inner, q_inner), (ky_outer, q_outer), merged = piece
    kx = lax.broadcasted_iota(jnp.int32, (128, 128), 0)
    kx = jnp.where(kx < 64, kx, kx - 128)
    inner = lane_ids(128) % 32 < 16
    i = lane_ids(128) % 16
    ky = jnp.where(inner, ky_inner, ky_outer)
    first = jnp.where(inner, 16 * q_inner, 16 * q_outer + jnp.where(merged, 0, 8))
    kz = jnp.where(i < 8, first + i, 7 - first - i)
    squared = kx * kx + ky * ky + kz * kz
    safe = jnp.maximum(squared, 1).astype(jnp.float32)
    return jnp.where(squared > 0, (8.0 * math.pi / N**3) / safe, 0.0)


def body(
    occ, orb_in, kept_in, ty_in, wz_in, wzi_in, tyi_in, tx_in, txi_in, lanes_in, out,
    chip, kept, ty, wz, wzi, tyi, tx, txi, lanes, far, pvr, df, merged, acc, pf, mask_send, mask_recv, coulomb,
    f_s1, f_r1, b_s1, b_r1, f_s2, f_r2, b_s2, b_r2, f_sc, f_rc, b_sc, b_rc, sem, sem_xy,
):
    b = lax.axis_index("band")
    g = lax.axis_index("grid")
    half = b // 2
    core = b % 2
    other_core = half * 2 + (1 - core)
    other_half = (1 - half) * 2 + core

    mask_recv[...] = jnp.zeros_like(mask_recv)
    u, v = chip.at[0], chip.at[1]
    act, pv = acc.at[0], acc.at[1]
    loads = [
        pltpu.make_async_copy(source, target, sem.at[LS + i])
        for i, (source, target) in enumerate(
            [
                (orb_in, u), (ty_in, ty), (wz_in, wz), (kept_in, kept), (lanes_in, lanes),
                (tx_in, tx), (txi_in, txi), (wzi_in, wzi), (tyi_in, tyi),
            ]
        )
    ]
    for load in loads:
        load.start()

    def on_line(k):
        return g - g % 4 + (g + k) % 4

    def in_plane(k):
        return ((g // 4 + k) % 16) * 4 + g % 4

    barrier = pltpu.get_barrier_semaphore()

    def greet(semaphore, band, grid):
        pl.semaphore_signal(
            semaphore, inc=1, device_id={"band": band, "grid": grid}, device_id_type=MESH
        )

    for k in range(4):
        greet(barrier, other_half, on_line(k))
    for k in range(1, 4):
        greet(barrier, b, on_line(k))
    for k in range(1, 16):
        greet(barrier, b, in_plane(k))
    greet(barrier, other_core, g)

    def remote(src, dst, send, recv, band=None, grid=None):
        device = {"band": b if band is None else band, "grid": g if grid is None else grid}
        return pltpu.make_async_remote_copy(
            src_ref=src, dst_ref=dst, send_sem=sem.at[send], recv_sem=sem.at[recv],
            device_id=device, device_id_type=MESH,
        )

    class Cut:
        def __init__(self, src, dst, send, recv, band):
            self.parts = [
                remote(src.at[i, pl.ds(r, N // CUTS)], dst.at[i, pl.ds(r, N // CUTS)], send, recv, band=band)
                for r in range(0, N, N // CUTS)
                for i in range(2)
            ]
            self.whole = remote(src, dst, send, recv, band=band)

        def start(self):
            for part in self.parts:
                part.start()

        def wait_recv(self):
            self.whole.wait_recv()

        def wait_send(self):
            self.whole.wait_send()

    pl.semaphore_wait(barrier, 23)
    for k in range(1, 16):
        greet(sem_xy, b, in_plane(k))
    loads[0].wait()
    to_half = Cut(u.at[:, 1 - half], far.at[0], AS, AR, other_half)
    to_half.start()
    to_core = remote(u, v, E1S, E1R, band=other_core)
    to_core.start()

    for load in loads[1:3]:
        load.wait()
    ty, wz = ty[...], wz[...]
    own = [
        forward_planes([u[0, p] * u[0, p], u[0, p] * u[1, p], u[1, p] * u[1, p]], ty, wz)
        for p in range(2)
    ]

    for p in range(2):
        real, imag = own[p]
        chunks = to_chunks(quarters(real + imag[:1]))
        store_chunks(f_s1, PITCH_1, lambda j: j * 3 + p, chunks)
    chunks = to_chunks(quarters(own[0][1][1:] + own[1][1][1:]))
    store_chunks(f_s1, PITCH_1, lambda j: j * 3 + 2, chunks)

    for load in loads[3:]:
        load.wait()
    tx, txi, wzi, tyi = tx[...], txi[...], wzi[...], tyi[...]
    for row in range(2):
        plane = dot(kept[:, row, :].astype(jnp.float32).astype(jnp.bfloat16), lanes[...])
        groups = quarters([plane[32 * k : 32 * k + 32] for k in range(4)])
        for q in range(4):
            mask_send[row * 4 + q] = groups[q]

    def mask_copies(act_on_remote, act_on_local):
        def one(i, carry):
            exists, t, j = owner_of(2 * g + i // 4, i % 4)

            @pl.when(exists & (t != g))
            def _():
                act_on_remote(
                    pltpu.make_async_remote_copy(
                        src_ref=mask_send.at[i], dst_ref=mask_recv.at[j],
                        send_sem=sem.at[MS + i], recv_sem=sem.at[MR + j],
                        device_id={"band": b, "grid": t}, device_id_type=MESH,
                    )
                )

            if act_on_local is not None:

                @pl.when(exists & (t == g))
                def _():
                    act_on_local(
                        pltpu.make_async_copy(mask_send.at[i], mask_recv.at[j], sem.at[MR + j])
                    )

            return carry

        lax.fori_loop(0, 8, one, 0)

    mask_to_core = remote(mask_recv, mask_recv, MFS, MFR, band=other_core)

    def slot(index, pitch, rows):
        return pl.ds(pl.multiple_of(index * pitch, pitch), rows)

    place = place_of(g)
    three = place < OWN_THREE

    def sized(count_three, act):
        @pl.when(count_three)
        def _():
            act(3)

        @pl.when(jnp.logical_not(count_three))
        def _():
            act(2)

    my_line, my_z = g // 4, g % 4
    my_first, my_turn = my_line % 4, my_line // 4

    def forward(src, dst, pitch, piece, send, recv, to):
        there = to * PEERS
        both = dst.shape[0] > (PEERS + 1) * pitch
        target_slot = (half * PEERS if both else 0) + g
        source_slot = there if both else 0

        def start(pieces, p, t):
            rows = pieces * piece
            source, target = src.at[slot(source_slot + p, pitch, rows)], dst.at[slot(target_slot, pitch, rows)]
            remote(source, target, send, recv, band=to * 2 + core, grid=t).start()

        start_z = my_z + jnp.where(to == half, 0, 2)
        for step in (2, 1, 3, 0):
            z = (start_z + step) % 4
            for r in (1, 2, 3, 0):
                first = (z + r) % 4

                def one(n, carry):
                    q = n + my_turn
                    line = first + 4 * jnp.where(q >= 4, q - 4, q)
                    p, t = 16 * (3 - r) + line, 4 * line + z
                    if r > 0:
                        start(3, p, t)
                    else:
                        sized(line == 0, lambda pieces: start(pieces, p, t))
                    return carry

                if step == 0:

                    @pl.when((first != my_first) | (to != half))
                    def _():
                        one(0, 0)

                lax.fori_loop(0 if step > 0 else 1, 4, one, 0)

        @pl.when(to == half)
        def _():
            def local(pieces):
                rows = pieces * piece
                source = src.at[slot(source_slot + place, pitch, rows)]
                pltpu.make_async_copy(source, dst.at[slot(target_slot, pitch, rows)], sem.at[recv]).start()

            sized(three, local)

    def backward(src, dst, pitch, piece, send, recv, to):
        both = dst.shape[0] > (PEERS + 1) * pitch
        target_slot = (half * PEERS if both else 0) + place
        source_slot = to * PEERS if both else 0

        def messages(pieces):
            rows = pieces * piece
            target = dst.at[slot(target_slot, pitch, rows)]

            def start(t):
                source = src.at[slot(source_slot + t, pitch, rows)]
                remote(source, target, send, recv, band=to * 2 + core, grid=t).start()

            start_z = my_z + jnp.where(to == half, 0, 2)
            for step in (2, 1, 3, 0):
                z = (start_z + step) % 4

                def one(k, carry):
                    line = my_line + k
                    start(4 * jnp.where(line >= 16, line - 16, line) + z)
                    return carry

                lax.fori_loop(0 if step > 0 else 1, 16, one, 0)

            @pl.when(to != half)
            def _():
                start(4 * my_line + start_z % 4)

            @pl.when(to == half)
            def _():
                source = src.at[slot(source_slot + g, pitch, rows)]
                pltpu.make_async_copy(source, target, sem.at[recv]).start()

        sized(three, messages)

    def arrived_own(dst, count, piece, semaphore):
        sized(three, lambda pieces: arrived(dst, count * pieces * piece, semaphore))

    def arrived(dst, rows, recv):
        whole = dst.at[pl.ds(0, rows)]
        pltpu.make_async_copy(whole, whole, sem.at[recv]).wait()

    pl.semaphore_wait(sem_xy, 15)
    forward(f_s1, f_r1, PITCH_1, PIECE_1, F1S, F1R, half)

    @pl.when(core == 0)
    def _():
        mask_copies(lambda c: c.start(), lambda c: c.start())

    v0, v1 = core, 1 - core
    to_core.wait_recv()
    real, imag = forward_planes(
        [u[0, p] * v[v0, p] for p in range(2)] + [u[1, p] * v[v1, p] for p in range(2)], ty, wz
    )
    for p in range(2):
        chunks = to_chunks(quarters([real[p], real[2 + p], imag[p], imag[2 + p]]))
        store_chunks(f_s2, PITCH_2, lambda j: j * 2 + p, chunks)

    first_quad = half * core
    quads = ((first_quad, 0, core), (1 - first_quad, 1, 1 - core))

    def pack_cross(quad, f, n):
        near = [chip[n, i, half] for i in (0, half, 1 - half, 1)]
        d = [a * far[f, i] for a, i in zip(near, (0, 1 - half, half, 1))]
        pack_quad(f_sc, PITCH_C, quad * (PEERS * PITCH_C), *forward_planes(d, ty, wz))

    pieces = [piece_of(place, j) for j in range(3)]
    for j in range(3):
        coulomb[j] = coulomb_table(pieces[j])
    to_half.wait_recv()
    far_to_core = remote(far.at[0], far.at[1], E3S, E3R, band=other_core)
    far_to_core.start()
    pack_cross(*quads[0])
    forward(f_sc, f_rc, PITCH_C, PIECE_C, FCS, FCR, quads[0][0])
    far_to_core.wait_recv()
    pack_cross(*quads[1])
    forward(f_sc, f_rc, PITCH_C, PIECE_C, FCS, FCR, quads[1][0])

    forward(f_s2, f_r2, PITCH_2, PIECE_2, F2S, F2R, half)
    two_rows = piece_of(place, 2)[2] & three
    @pl.when(core == 0)
    def _():
        for j, expected in enumerate((True, True, three, two_rows)):

            @pl.when(expected)
            def _():
                pltpu.make_async_copy(mask_recv.at[j], mask_recv.at[j], sem.at[MR + j]).wait()

        mask_to_core.start()

    @pl.when(core == 1)
    def _():
        mask_to_core.wait_recv()

    kernel_of = [
        kernel_table(coulomb[j], mask_recv[j], mask_recv[3], pieces[j][2]) for j in range(3)
    ]

    arrived_own(f_r1, PEERS, PIECE_1, F1R)
    middle_first(f_r1, b_s1, kernel_of, tx, txi)
    backward(b_s1, b_r1, PITCH_1, PIECE_1, B1S, B1R, half)
    arrived_own(f_r2, PEERS, PIECE_2, F2R)
    middle_second(f_r2, b_s2, kernel_of, tx, txi)
    arrived_own(f_rc, 2 * PEERS, PIECE_C, FCR)
    middle_cross(f_rc, b_sc, kernel_of, tx, txi)
    backward(b_sc, b_rc, PITCH_C, PIECE_C, BCS, BOR, 1 - half)
    backward(b_sc, b_rc, PITCH_C, PIECE_C, BCS, BCR, half)

    mine = half * 4 + core * 2
    theirs = half * 4 + (1 - core) * 2
    arrived(b_r1, PIECES * PIECE_1, B1R)
    rest = unpack(b_r1, PITCH_1, lambda j: j * 3 + 2)
    for p in range(2):
        parts = unpack(b_r1, PITCH_1, lambda j: j * 3 + p)
        pot = inverse_planes(parts[:3], parts[3:] + rest[2 * p : 2 * p + 2], wzi, tyi)
        o0, o1 = occ[mine] * u[0, p], occ[mine + 1] * u[1, p]
        act[0, p] = o0 * pot[0] + o1 * pot[1]
        act[1, p] = o0 * pot[1] + o1 * pot[2]

    pv[...] = jnp.zeros_like(pv)
    arrived(b_rc, PIECES * PIECE_C, BOR)
    backward(b_s2, b_r2, PITCH_2, PIECE_2, B2S, B2R, half)
    arrived(b_rc, PIECES * PIECE_C, BCR)

    def cross_terms(quad, f, n):
        first = quad * (PEERS * PITCH_C)
        real, imag = (unpack(b_rc, PITCH_C, lambda j: first + j * 2 + ri) for ri in range(2))
        p00, p01, p10, p11 = inverse_planes(real, imag, wzi, tyi)
        p01, p10 = jnp.where(half == 0, p01, p10), jnp.where(half == 0, p10, p01)
        here = half * 4 + jnp.where(n == 0, core, 1 - core) * 2
        there = (1 - half) * 4 + (core if f == 0 else 1 - core) * 2
        n0, n1 = occ[here] * chip[n, 0, half], occ[here + 1] * chip[n, 1, half]
        f0, f1 = occ[there] * far[f, 0], occ[there + 1] * far[f, 1]
        pf[f, 0] = n0 * p00 + n1 * p10
        pf[f, 1] = n0 * p01 + n1 * p11
        acc[n, 0, half] += f0 * p00 + f1 * p01
        acc[n, 1, half] += f0 * p10 + f1 * p11

    cross_terms(*quads[1])
    merge = remote(pf.at[1], merged, X1S, X1R, band=other_core)
    merge.start()
    cross_terms(*quads[0])
    merge.wait_recv()
    pf[0] += merged[...]
    home = Cut(pf.at[0], df, DS, DR, other_half)
    home.start()

    arrived(b_r2, PIECES * PIECE_2, B2R)
    for p in range(2):
        a_re, b_re, a_im, b_im = unpack(b_r2, PITCH_2, lambda j: j * 2 + p)
        pot = inverse_planes([a_re, b_re], [a_im, b_im], wzi, tyi)
        act[0, p] += occ[theirs + v0] * v[v0, p] * pot[0]
        act[1, p] += occ[theirs + v1] * v[v1, p] * pot[1]
        pv[v0, p] += occ[mine] * u[0, p] * pot[0]
        pv[v1, p] += occ[mine + 1] * u[1, p] * pot[1]
    swap = remote(pv, pvr, E2S, E2R, band=other_core)
    swap.start()
    swap.wait_recv()
    for i in range(2):
        out[i, half] = -(act[i, half] + pvr[i, half])
        acc[0, i, 1 - half] += pvr[i, 1 - half]
    home.wait_recv()
    for i in range(2):
        out[i, 1 - half] = -(act[i, 1 - half] + df[i])

    to_core.wait_send()
    to_half.wait_send()

    @pl.when(core == 0)
    def _():
        mask_to_core.wait_send()
        mask_copies(lambda c: c.wait_send(), None)

    for src, pieces, piece, send in (
        (f_s1, PIECES, PIECE_1, F1S),
        (f_s2, PIECES, PIECE_2, F2S),
        (f_sc, 2 * PIECES, PIECE_C, FCS),
    ):
        sized(three, lambda mine: arrived(src, (pieces - mine) * piece, send))
    arrived_own(b_s1, PEERS - 1, PIECE_1, B1S)
    arrived_own(b_s2, PEERS - 1, PIECE_2, B2S)
    arrived_own(b_sc, 2 * PEERS - 1, PIECE_C, BCS)
    far_to_core.wait_send()
    merge.wait_send()
    swap.wait_send()
    home.wait_send()


def on_device(orbitals, occupation, kept_modes):
    block = pltpu.VMEM((2, 2, N, N), jnp.float32)
    twice = pltpu.VMEM((2, 2, 2, N, N), jnp.float32)
    plane = pltpu.VMEM((2, N, N), jnp.float32)
    planes = pltpu.VMEM((2, 2, N, N), jnp.float32)
    messages = [
        pltpu.VMEM(((slots + 1) * pitch, 128), jnp.float32)
        for slots, pitch in ((PEERS, PITCH_1), (PEERS, PITCH_2), (2 * PEERS, PITCH_C))
        for _ in range(4)
    ]
    tables = make_tables()
    loaded = [twice, pltpu.VMEM(kept_modes.shape, jnp.int32)]
    loaded += [pltpu.VMEM(t.shape, jnp.bfloat16) for t in tables]
    return pl.pallas_call(
        body,
        out_shape=jax.ShapeDtypeStruct(orbitals.shape, jnp.float32),
        in_specs=[pl.BlockSpec(memory_space=pltpu.SMEM)] + [pl.BlockSpec(memory_space=pltpu.HBM)] * 9,
        out_specs=pl.BlockSpec(memory_space=pltpu.VMEM),
        scratch_shapes=loaded
        + [planes, block, plane, plane, twice, planes]
        + [pltpu.VMEM((8, 32, 128), jnp.float32), pltpu.VMEM((4, 32, 128), jnp.float32)]
        + [pltpu.VMEM((3, N, 128), jnp.float32)]
        + messages
        + [
            pltpu.SemaphoreType.DMA((NSEM,)),
            pltpu.SemaphoreType.REGULAR,
        ],
        compiler_params=pltpu.CompilerParams(
            collective_id=1, has_side_effects=True, vmem_limit_bytes=60 << 20
        ),
        name="exchange",
    )(occupation, orbitals, kept_modes, *(jnp.asarray(t) for t in tables))


def solution(mesh):
    return jax.shard_map(
        on_device,
        mesh=mesh,
        in_specs=(P("band", "grid", None, None), P(), P(None, "grid", None)),
        out_specs=P("band", "grid", None, None),
        check_vma=False,
    )
```

```python
import functools
import math

import jax
import jax.numpy as jnp
import ml_dtypes
import numpy as np
from jax import lax
from jax.experimental import pallas as pl
from jax.experimental.pallas import tpu as pltpu
from jax.sharding import PartitionSpec as P

MESH = pl.DeviceIdType.MESH
N = 128
PEERS = 64
PIECE_1, PITCH_1 = 3, 16
PIECE_2, PITCH_2 = 2, 8
PIECE_C, PITCH_C = 2, 8
CHUNKS = 23
OWN_THREE = 49
PIECES = 3 * OWN_THREE + 2 * (PEERS - OWN_THREE)
LAST_KEPT = 57
CUTS = 2

E1S, E1R, AS, AR, F1S, F1R, F2S, F2R, FCS, FCR, B1S, B1R, B2S, B2R, BCS, BCR = range(16)
E2S, E2R, E3S, E3R, X1S, X1R, DS, DR, MFS, MFR, BOR = range(16, 27)
MR = 27
MS = 31
LS = 39
NSEM = 48


def row_order():
    order = list(range(24)) + [31] + list(range(24, 31)) + list(range(32, 48))
    order += [54, 52, 53, 55, 48, 49, 50, 51] + [57, -1, -1, 56] + [-1] * 4
    return order


def lane_order():
    out = []
    for q in range(4):
        for first in (16 * q, 16 * q + 8):
            out += [first + i for i in range(8)]
            out += [-first - 1 - i for i in range(8)]
    return out


def split(table):
    high = table.astype(ml_dtypes.bfloat16)
    low = (table - high.astype(np.float64)).astype(ml_dtypes.bfloat16)
    return high, low


def left_table(table):
    high, low = split(table)
    return np.concatenate([high, low, high], axis=1)


def right_table(table):
    high, low = split(table)
    return np.concatenate([high, high, low], axis=0)


def make_tables():
    n = np.arange(N)
    ky = np.array(row_order())
    kz = np.array(lane_order())
    turn = 2.0 * np.pi / N
    angle_y = turn * ((ky[:, None] * n[None, :]) % N)
    forward_y = np.zeros((128, N))
    forward_y[:64] = np.where(ky < 0, 0.0, 1.0)[:, None] * np.cos(angle_y)
    forward_y[64:] = -np.where(ky < 0, 0.0, 1.0)[:, None] * np.sin(angle_y)
    weight = np.where(ky < 0, 0.0, np.where(ky == 0, 1.0, 2.0))[:, None]
    inverse_y = np.zeros((128, N))
    inverse_y[:64] = weight * np.cos(angle_y)
    inverse_y[64:] = -weight * np.sin(angle_y)
    inverse_y = inverse_y.T
    angle_z = turn * ((n[:, None] * kz[None, :]) % N)
    forward_z = np.concatenate([np.cos(angle_z), np.sin(angle_z)], axis=1)
    inverse_z = np.concatenate([np.cos(angle_z.T), np.sin(angle_z.T)], axis=1)
    x = np.concatenate([np.arange(0, N, 2), np.arange(1, N, 2)])
    angle_x = turn * ((n[:, None] * x[None, :]) % N)
    forward_x = np.concatenate([np.cos(angle_x), np.sin(angle_x)], axis=0)
    inverse_x = np.concatenate([np.cos(angle_x.T), np.sin(angle_x.T)], axis=0)
    lanes = np.zeros((N, N))
    lanes[kz % N, np.arange(N)] = 1.0
    return (
        left_table(forward_y),
        right_table(forward_z),
        right_table(inverse_z),
        left_table(inverse_y),
        left_table(forward_x),
        left_table(inverse_x),
        lanes.astype(ml_dtypes.bfloat16),
    )


def dot(a, b):
    return jnp.dot(a, b, preferred_element_type=jnp.float32)


def halves(value):
    high = value.astype(jnp.bfloat16)
    low = (value - high.astype(jnp.float32)).astype(jnp.bfloat16)
    return high, low


def table_times(table, value):
    high, low = halves(value)
    return dot(table, jnp.concatenate([high, high, low], axis=0))


def times_table(value, table):
    high, low = halves(value)
    return dot(jnp.concatenate([high, low, high], axis=1), table)


def lane_ids(rows):
    return lax.broadcasted_iota(jnp.int32, (rows, 128), 1)


def sublane_ids():
    return lax.broadcasted_iota(jnp.int32, (8, 128), 0)


def turn_lanes(value, by):
    return pltpu.roll(value, by % 128, 1)


def quarters(a):
    lane = lane_ids(a[0].shape[0])
    low = lane < 64
    even = (lane // 32) % 2 == 0
    u = [None] * 4
    for k in range(2):
        u[k] = jnp.where(low, a[k], turn_lanes(a[k + 2], 64))
        u[k + 2] = jnp.where(low, turn_lanes(a[k], 64), a[k + 2])
    out = [None] * 4
    for k in (0, 2):
        out[k] = jnp.where(even, u[k], turn_lanes(u[k + 1], 32))
        out[k + 1] = jnp.where(even, turn_lanes(u[k], -32), u[k + 1])
    return out


def to_chunks(q):
    def chunk(g, c):
        return q[g][8 * c : 8 * c + 8]

    def merge(first, second):
        return jnp.where(inner, first, turn_lanes(second, 16))

    sub = sublane_ids()
    inner = lane_ids(8) % 32 < 16
    x = merge(chunk(3, 2), jnp.where(sub == 0, chunk(1, 6), chunk(3, 3)))
    y = merge(chunk(2, 5), jnp.where(sub < 3, chunk(1, 6), chunk(3, 1)))
    y = jnp.where(sub == 0, chunk(2, 5), y)
    z = jnp.where(sub < 3, chunk(3, 1), jnp.where(sub == 3, chunk(0, 7), chunk(1, 6)))
    out = [chunk(0, c) for c in range(7)] + [chunk(1, c) for c in range(6)]
    out += [chunk(2, c) for c in range(5)] + [chunk(3, 0)]
    return out + [x, y, z, chunk(0, 7)]


def from_chunks(chunks):
    sub = sublane_ids()
    inner = lane_ids(8) % 32 < 16
    zero = jnp.zeros((8, 128), jnp.float32)
    x, y, z, last = chunks[19:]
    x_second = jnp.where(inner, turn_lanes(x, -16), zero)
    y_second = jnp.where(inner, turn_lanes(y, -16), zero)
    x_first = jnp.where(inner, x, zero)
    y_first = jnp.where(inner | (sub == 0), y, zero)
    q0 = chunks[0:7] + [jnp.where(sub == 0, last, jnp.where(sub == 3, z, zero))]
    mixed = jnp.where(sub == 0, x_second, jnp.where(sub < 3, y_second, jnp.where(sub == 3, zero, z)))
    q1 = chunks[7:13] + [mixed, zero]
    q2 = chunks[13:18] + [y_first, zero, zero]
    q3 = [chunks[18], jnp.where(sub < 3, z, y_second), x_first, jnp.where(sub == 0, zero, x_second)]
    q3 += [zero] * 4
    return [jnp.concatenate(parts, axis=0) for parts in (q0, q1, q2, q3)]


def forward_planes(densities, ty, wz):
    e = table_times(ty, jnp.concatenate(densities, axis=1))
    real, imag = [], []
    for k in range(len(densities)):
        g = times_table(e[:, 128 * k : 128 * k + 128], wz)
        real.append(g[:64, :128] + g[64:, 128:])
        imag.append(g[64:, :128] - g[:64, 128:])
    return real, imag


def inverse_planes(real, imag, wzi, tyi):
    parts = []
    for re, im in zip(real, imag):
        g = times_table(jnp.concatenate([re, im], axis=0), wzi)
        parts.append(
            jnp.concatenate([g[:64, :128] - g[64:, 128:], g[64:, :128] + g[:64, 128:]], axis=0)
        )
    v = table_times(tyi, jnp.concatenate(parts, axis=1))
    return [v[:, 128 * k : 128 * k + 128] for k in range(len(parts))]


def store_chunks(buf, pitch, row, chunks):
    for m, value in enumerate(chunks):
        buf[pl.ds((m % 8) * 8 * pitch + row(m // 8), 8, stride=pitch), :] = value


def load_chunks(buf, pitch, row):
    return [buf[pl.ds((m % 8) * 8 * pitch + row(m // 8), 8, stride=pitch), :] for m in range(CHUNKS)]


def pack_quad(buf, pitch, first, real, imag):
    for ri, part in enumerate((real, imag)):
        store_chunks(buf, pitch, lambda j: first + j * 2 + ri, to_chunks(quarters(part)))


def unpack(buf, pitch, row):
    return quarters(from_chunks(load_chunks(buf, pitch, row)))


def spectrum(buf, pitch, second, row):
    return jnp.concatenate(
        [buf[pl.ds(plane * second + row, 64, stride=pitch), :] for plane in range(2)], axis=0
    )


def convolve(real, imag, kernel_of, tx, txi):
    p = table_times(tx, jnp.concatenate(real + imag, axis=1))
    c, s = p[:128], p[128:]
    blocks = []
    for j in range(3):
        re, im = slice(128 * j, 128 * j + 128), slice(384 + 128 * j, 512 + 128 * j)
        blocks.append((c[:, re] + s[:, im]) * kernel_of[j])
    for j in range(3):
        re, im = slice(128 * j, 128 * j + 128), slice(384 + 128 * j, 512 + 128 * j)
        blocks.append((c[:, im] - s[:, re]) * kernel_of[j])
    p = table_times(txi, jnp.concatenate(blocks, axis=1))
    c, s = p[:128], p[128:]
    real, imag = [], []
    for j in range(3):
        re, im = slice(128 * j, 128 * j + 128), slice(384 + 128 * j, 512 + 128 * j)
        real.append(c[:, re] - s[:, im])
        imag.append(c[:, im] + s[:, re])
    return real, imag


def middle_cross(recv, send, kernel_of, tx, txi):
    second = PEERS * PITCH_C
    parts = [[spectrum(recv, PITCH_C, second, j * 2 + ri) for j in range(3)] for ri in range(2)]
    for ri, new in enumerate(convolve(*parts, kernel_of, tx, txi)):
        for j in range(3):
            for plane in range(2):
                send[pl.ds(plane * second + j * 2 + ri, 64, stride=PITCH_C), :] = new[j][
                    64 * plane : 64 * plane + 64
                ]


def middle_first(recv, send, kernel_of, tx, txi):
    lane = lane_ids(64)
    real, imag = [], []
    for j in range(3):
        r0, r1, r2 = (recv[pl.ds(j * 3 + i, 64, stride=PITCH_1), :] for i in range(3))
        real.append(jnp.concatenate([r0, r1], axis=0))
        i0 = jnp.where(lane < 32, turn_lanes(r0, 32), turn_lanes(r2, 32))
        i1 = jnp.where(lane < 32, turn_lanes(r1, 32), turn_lanes(r2, -32))
        imag.append(jnp.concatenate([i0, i1], axis=0))
    real, imag = convolve(real, imag, kernel_of, tx, txi)
    for j in range(3):
        i0, i1 = imag[j][:64], imag[j][64:]
        rows = (
            jnp.where(lane < 96, real[j][:64], turn_lanes(i0, 96)),
            jnp.where(lane < 96, real[j][64:], turn_lanes(i1, 96)),
            jnp.where(lane < 64, turn_lanes(i0, -32), turn_lanes(i1, 32)),
        )
        for i in range(3):
            send[pl.ds(j * 3 + i, 64, stride=PITCH_1), :] = rows[i]


def middle_second(recv, send, kernel_of, tx, txi):
    low = lane_ids(128) < 64

    def cross(s):
        turned = turn_lanes(s, 64)
        return jnp.where(low, turned, -turned)

    blocks = [spectrum(recv, PITCH_2, 1, j * 2) for j in range(3)]
    p = table_times(tx, jnp.concatenate(blocks, axis=1))
    blocks = []
    for j in range(3):
        at = slice(128 * j, 128 * j + 128)
        blocks.append((p[:128, at] + cross(p[128:, at])) * kernel_of[j])
    p = table_times(txi, jnp.concatenate(blocks, axis=1))
    for j in range(3):
        at = slice(128 * j, 128 * j + 128)
        new = p[:128, at] - cross(p[128:, at])
        for plane in range(2):
            send[pl.ds(j * 2 + plane, 64, stride=PITCH_2), :] = new[64 * plane : 64 * plane + 64]


def place_of(g):
    line = g // 4
    return 16 * ((g % 4 + 3 - line % 4) % 4) + line


def frequency_at(pos):
    ky = jnp.where((pos >= 25) & (pos <= 31), pos - 1, pos)
    ky = jnp.where((pos >= 52) & (pos <= 55), pos - 4, ky)
    for at, value in ((24, 31), (48, 54), (49, 52), (50, 53), (51, 55), (56, 57), (59, 56)):
        ky = jnp.where(pos == at, value, ky)
    return ky


def position_of(ky):
    pos = jnp.where((ky >= 24) & (ky <= 30), ky + 1, ky)
    pos = jnp.where((ky >= 48) & (ky <= 51), ky + 4, pos)
    for at, value in ((24, 31), (48, 54), (49, 52), (50, 53), (51, 55), (56, 57), (59, 56)):
        pos = jnp.where(ky == value, at, pos)
    return pos


def pick(cases, otherwise):
    out = otherwise
    for condition, case in reversed(cases):
        out = jnp.where(condition, case, out)
    return out


def piece_of(place, j):
    m = j * 8 + place // 8
    sub = place % 8
    in_z = m == 21
    cases = [
        (m < 7, 0), (m < 13, 1), (m < 18, 2), (m < 20, 3), (m == 20, 2),
        (in_z & (sub < 3), 3), (in_z & (sub > 3), 1),
    ]
    q = pick(cases, 0)
    cases = [
        (m < 7, m), (m < 13, m - 7), (m < 18, m - 13), (m == 18, 0), (m == 19, 2), (m == 20, 5),
        (in_z & (sub < 3), 1), (in_z & (sub > 3), 6),
    ]
    c = pick(cases, 7)
    merged = (m == 19) | ((m == 20) & (sub > 0))
    from_1 = ((m == 19) & (sub == 0)) | ((m == 20) & (sub < 3))
    q_outer = jnp.where(merged, jnp.where(from_1, 1, 3), q)
    c_outer = jnp.where(merged, jnp.where(from_1, 6, jnp.where(m == 19, 3, 1)), c)
    inner = (frequency_at(c * 8 + sub), q)
    return inner, (frequency_at(c_outer * 8 + sub), q_outer), merged


def owner_of(ky, q):
    pos = position_of(ky)
    c = pos // 8
    sub = pos % 8
    cases = [
        ((q == 0) & (c < 7), c), ((q == 0) & (sub == 0), 22), (q == 0, 21),
        ((q == 1) & (c < 6), c + 7), ((q == 1) & (sub == 0), 19), ((q == 1) & (sub < 3), 20),
        (q == 1, 21), ((q == 2) & (c < 5), c + 13), (q == 2, 20),
        (c == 0, 18), ((c == 1) & (sub < 3), 21), (c == 1, 20),
    ]
    m = pick(cases, 19)
    second = ((q == 1) & (c == 6) & (sub < 3)) | (
        (q == 3) & (((c == 1) & (sub >= 3)) | (c == 3))
    )
    exists = (
        (q == 0)
        | ((q == 1) & ((c < 6) | ((c == 6) & (sub != 3))))
        | ((q == 2) & (c < 6))
        | ((q == 3) & ((c < 3) | ((c == 3) & (sub > 0))))
    ) & (ky <= LAST_KEPT)
    m = jnp.where(exists, m, 0)
    place = (m % 8) * 8 + sub
    line = place % 16
    return exists, line * 4 + (place // 16 + 1 + line) % 4, jnp.where(second, 3, m // 8)


def kernel_table(coulomb, mask, second, merged):
    lane = lane_ids(32)
    mask = jnp.where((lane % 32 >= 16) & merged, turn_lanes(second, 16), mask)
    rows = []
    for block in range(4):
        part = jnp.where(lane // 32 == block, mask, 0.0)
        part = part + turn_lanes(part, 64)
        rows.append(part + turn_lanes(part, 32))
    return coulomb * jnp.concatenate(rows, axis=0)


def coulomb_table(piece):
    (ky_inner, q_inner), (ky_outer, q_outer), merged = piece
    kx = lax.broadcasted_iota(jnp.int32, (128, 128), 0)
    kx = jnp.where(kx < 64, kx, kx - 128)
    inner = lane_ids(128) % 32 < 16
    i = lane_ids(128) % 16
    ky = jnp.where(inner, ky_inner, ky_outer)
    first = jnp.where(inner, 16 * q_inner, 16 * q_outer + jnp.where(merged, 0, 8))
    kz = jnp.where(i < 8, first + i, 7 - first - i)
    squared = kx * kx + ky * ky + kz * kz
    safe = jnp.maximum(squared, 1).astype(jnp.float32)
    return jnp.where(squared > 0, (8.0 * math.pi / N**3) / safe, 0.0)


def body(
    occ, orb_in, kept_in, ty_in, wz_in, wzi_in, tyi_in, tx_in, txi_in, lanes_in, out,
    chip, kept, ty, wz, wzi, tyi, tx, txi, lanes, far, pvr, df, merged, acc, pf, mask_send, mask_recv, coulomb,
    f_s1, f_r1, b_s1, b_r1, f_s2, f_r2, b_s2, b_r2, f_sc, f_rc, b_sc, b_rc, sem, sem_xy,
):
    b = lax.axis_index("band")
    g = lax.axis_index("grid")
    half = b // 2
    core = b % 2
    other_core = half * 2 + (1 - core)
    other_half = (1 - half) * 2 + core

    mask_recv[...] = jnp.zeros_like(mask_recv)
    u, v = chip.at[0], chip.at[1]
    act, pv = acc.at[0], acc.at[1]
    loads = [
        pltpu.make_async_copy(source, target, sem.at[LS + i])
        for i, (source, target) in enumerate(
            [
                (orb_in, u), (ty_in, ty), (wz_in, wz), (kept_in, kept), (lanes_in, lanes),
                (tx_in, tx), (txi_in, txi), (wzi_in, wzi), (tyi_in, tyi),
            ]
        )
    ]
    for load in loads:
        load.start()

    def on_line(k):
        return g - g % 4 + (g + k) % 4

    def in_plane(k):
        return ((g // 4 + k) % 16) * 4 + g % 4

    barrier = pltpu.get_barrier_semaphore()

    def greet(semaphore, band, grid):
        pl.semaphore_signal(
            semaphore, inc=1, device_id={"band": band, "grid": grid}, device_id_type=MESH
        )

    for k in range(4):
        greet(barrier, other_half, on_line(k))
    for k in range(1, 4):
        greet(barrier, b, on_line(k))
    for k in range(1, 16):
        greet(barrier, b, in_plane(k))
    greet(barrier, other_core, g)

    def remote(src, dst, send, recv, band=None, grid=None):
        device = {"band": b if band is None else band, "grid": g if grid is None else grid}
        return pltpu.make_async_remote_copy(
            src_ref=src, dst_ref=dst, send_sem=sem.at[send], recv_sem=sem.at[recv],
            device_id=device, device_id_type=MESH,
        )

    class Cut:
        def __init__(self, src, dst, send, recv, band):
            self.parts = [
                remote(src.at[i, pl.ds(r, N // CUTS)], dst.at[i, pl.ds(r, N // CUTS)], send, recv, band=band)
                for r in range(0, N, N // CUTS)
                for i in range(2)
            ]
            self.whole = remote(src, dst, send, recv, band=band)

        def start(self):
            for part in self.parts:
                part.start()

        def wait_recv(self):
            self.whole.wait_recv()

        def wait_send(self):
            self.whole.wait_send()

    pl.semaphore_wait(barrier, 23)
    for k in range(1, 16):
        greet(sem_xy, b, in_plane(k))
    loads[0].wait()
    to_half = Cut(u.at[:, 1 - half], far.at[0], AS, AR, other_half)
    to_half.start()
    to_core = remote(u, v, E1S, E1R, band=other_core)
    to_core.start()

    for load in loads[1:3]:
        load.wait()
    ty, wz = ty[...], wz[...]
    own = [
        forward_planes([u[0, p] * u[0, p], u[0, p] * u[1, p], u[1, p] * u[1, p]], ty, wz)
        for p in range(2)
    ]

    for p in range(2):
        real, imag = own[p]
        chunks = to_chunks(quarters(real + imag[:1]))
        store_chunks(f_s1, PITCH_1, lambda j: j * 3 + p, chunks)
    chunks = to_chunks(quarters(own[0][1][1:] + own[1][1][1:]))
    store_chunks(f_s1, PITCH_1, lambda j: j * 3 + 2, chunks)

    for load in loads[3:]:
        load.wait()
    tx, txi, wzi, tyi = tx[...], txi[...], wzi[...], tyi[...]
    for row in range(2):
        plane = dot(kept[:, row, :].astype(jnp.float32).astype(jnp.bfloat16), lanes[...])
        groups = quarters([plane[32 * k : 32 * k + 32] for k in range(4)])
        for q in range(4):
            mask_send[row * 4 + q] = groups[q]

    def mask_copies(act_on_remote, act_on_local):
        def one(i, carry):
            exists, t, j = owner_of(2 * g + i // 4, i % 4)

            @pl.when(exists & (t != g))
            def _():
                act_on_remote(
                    pltpu.make_async_remote_copy(
                        src_ref=mask_send.at[i], dst_ref=mask_recv.at[j],
                        send_sem=sem.at[MS + i], recv_sem=sem.at[MR + j],
                        device_id={"band": b, "grid": t}, device_id_type=MESH,
                    )
                )

            if act_on_local is not None:

                @pl.when(exists & (t == g))
                def _():
                    act_on_local(
                        pltpu.make_async_copy(mask_send.at[i], mask_recv.at[j], sem.at[MR + j])
                    )

            return carry

        lax.fori_loop(0, 8, one, 0)

    mask_to_core = remote(mask_recv, mask_recv, MFS, MFR, band=other_core)

    def slot(index, pitch, rows):
        return pl.ds(pl.multiple_of(index * pitch, pitch), rows)

    place = place_of(g)
    three = place < OWN_THREE

    def sized(count_three, act):
        @pl.when(count_three)
        def _():
            act(3)

        @pl.when(jnp.logical_not(count_three))
        def _():
            act(2)

    my_line, my_z = g // 4, g % 4
    my_first, my_turn = my_line % 4, my_line // 4

    def forward(src, dst, pitch, piece, send, recv, to):
        there = to * PEERS
        both = dst.shape[0] > (PEERS + 1) * pitch
        target_slot = (half * PEERS if both else 0) + g
        source_slot = there if both else 0

        def start(pieces, p, t):
            rows = pieces * piece
            source, target = src.at[slot(source_slot + p, pitch, rows)], dst.at[slot(target_slot, pitch, rows)]
            remote(source, target, send, recv, band=to * 2 + core, grid=t).start()

        start_z = my_z + jnp.where(to == half, 0, 2)
        for step in (2, 1, 3, 0):
            z = (start_z + step) % 4
            for r in (1, 2, 3, 0):
                first = (z + r) % 4

                def one(n, carry):
                    q = n + my_turn
                    line = first + 4 * jnp.where(q >= 4, q - 4, q)
                    p, t = 16 * (3 - r) + line, 4 * line + z
                    if r > 0:
                        start(3, p, t)
                    else:
                        sized(line == 0, lambda pieces: start(pieces, p, t))
                    return carry

                if step == 0:

                    @pl.when((first != my_first) | (to != half))
                    def _():
                        one(0, 0)

                lax.fori_loop(0 if step > 0 else 1, 4, one, 0)

        @pl.when(to == half)
        def _():
            def local(pieces):
                rows = pieces * piece
                source = src.at[slot(source_slot + place, pitch, rows)]
                pltpu.make_async_copy(source, dst.at[slot(target_slot, pitch, rows)], sem.at[recv]).start()

            sized(three, local)

    def backward(src, dst, pitch, piece, send, recv, to):
        both = dst.shape[0] > (PEERS + 1) * pitch
        target_slot = (half * PEERS if both else 0) + place
        source_slot = to * PEERS if both else 0

        def messages(pieces):
            rows = pieces * piece
            target = dst.at[slot(target_slot, pitch, rows)]

            def start(t):
                source = src.at[slot(source_slot + t, pitch, rows)]
                remote(source, target, send, recv, band=to * 2 + core, grid=t).start()

            start_z = my_z + jnp.where(to == half, 0, 2)
            for step in (2, 1, 3, 0):
                z = (start_z + step) % 4

                def one(k, carry):
                    line = my_line + k
                    start(4 * jnp.where(line >= 16, line - 16, line) + z)
                    return carry

                lax.fori_loop(0 if step > 0 else 1, 16, one, 0)

            @pl.when(to != half)
            def _():
                start(4 * my_line + start_z % 4)

            @pl.when(to == half)
            def _():
                source = src.at[slot(source_slot + g, pitch, rows)]
                pltpu.make_async_copy(source, target, sem.at[recv]).start()

        sized(three, messages)

    def arrived_own(dst, count, piece, semaphore):
        sized(three, lambda pieces: arrived(dst, count * pieces * piece, semaphore))

    def arrived(dst, rows, recv):
        whole = dst.at[pl.ds(0, rows)]
        pltpu.make_async_copy(whole, whole, sem.at[recv]).wait()

    pl.semaphore_wait(sem_xy, 15)
    forward(f_s1, f_r1, PITCH_1, PIECE_1, F1S, F1R, half)

    @pl.when(core == 0)
    def _():
        mask_copies(lambda c: c.start(), lambda c: c.start())

    v0, v1 = core, 1 - core
    to_core.wait_recv()
    real, imag = forward_planes(
        [u[0, p] * v[v0, p] for p in range(2)] + [u[1, p] * v[v1, p] for p in range(2)], ty, wz
    )
    for p in range(2):
        chunks = to_chunks(quarters([real[p], real[2 + p], imag[p], imag[2 + p]]))
        store_chunks(f_s2, PITCH_2, lambda j: j * 2 + p, chunks)

    first_quad = half * core
    quads = ((first_quad, 0, core), (1 - first_quad, 1, 1 - core))

    def pack_cross(quad, f, n):
        near = [chip[n, i, half] for i in (0, half, 1 - half, 1)]
        d = [a * far[f, i] for a, i in zip(near, (0, 1 - half, half, 1))]
        pack_quad(f_sc, PITCH_C, quad * (PEERS * PITCH_C), *forward_planes(d, ty, wz))

    pieces = [piece_of(place, j) for j in range(3)]
    for j in range(3):
        coulomb[j] = coulomb_table(pieces[j])
    to_half.wait_recv()
    far_to_core = remote(far.at[0], far.at[1], E3S, E3R, band=other_core)
    far_to_core.start()
    pack_cross(*quads[0])
    forward(f_sc, f_rc, PITCH_C, PIECE_C, FCS, FCR, quads[0][0])
    far_to_core.wait_recv()
    pack_cross(*quads[1])
    forward(f_sc, f_rc, PITCH_C, PIECE_C, FCS, FCR, quads[1][0])

    forward(f_s2, f_r2, PITCH_2, PIECE_2, F2S, F2R, half)
    two_rows = piece_of(place, 2)[2] & three
    @pl.when(core == 0)
    def _():
        for j, expected in enumerate((True, True, three, two_rows)):

            @pl.when(expected)
            def _():
                pltpu.make_async_copy(mask_recv.at[j], mask_recv.at[j], sem.at[MR + j]).wait()

        mask_to_core.start()

    @pl.when(core == 1)
    def _():
        mask_to_core.wait_recv()

    kernel_of = [
        kernel_table(coulomb[j], mask_recv[j], mask_recv[3], pieces[j][2]) for j in range(3)
    ]

    arrived_own(f_r1, PEERS, PIECE_1, F1R)
    middle_first(f_r1, b_s1, kernel_of, tx, txi)
    backward(b_s1, b_r1, PITCH_1, PIECE_1, B1S, B1R, half)
    arrived_own(f_r2, PEERS, PIECE_2, F2R)
    middle_second(f_r2, b_s2, kernel_of, tx, txi)
    arrived_own(f_rc, 2 * PEERS, PIECE_C, FCR)
    middle_cross(f_rc, b_sc, kernel_of, tx, txi)
    backward(b_sc, b_rc, PITCH_C, PIECE_C, BCS, BOR, 1 - half)
    backward(b_sc, b_rc, PITCH_C, PIECE_C, BCS, BCR, half)

    mine = half * 4 + core * 2
    theirs = half * 4 + (1 - core) * 2
    arrived(b_r1, PIECES * PIECE_1, B1R)
    rest = unpack(b_r1, PITCH_1, lambda j: j * 3 + 2)
    for p in range(2):
        parts = unpack(b_r1, PITCH_1, lambda j: j * 3 + p)
        pot = inverse_planes(parts[:3], parts[3:] + rest[2 * p : 2 * p + 2], wzi, tyi)
        o0, o1 = occ[mine] * u[0, p], occ[mine + 1] * u[1, p]
        act[0, p] = o0 * pot[0] + o1 * pot[1]
        act[1, p] = o0 * pot[1] + o1 * pot[2]

    pv[...] = jnp.zeros_like(pv)
    arrived(b_rc, PIECES * PIECE_C, BOR)
    backward(b_s2, b_r2, PITCH_2, PIECE_2, B2S, B2R, half)
    arrived(b_rc, PIECES * PIECE_C, BCR)

    def cross_terms(quad, f, n, send):
        first = quad * (PEERS * PITCH_C)
        real, imag = (unpack(b_rc, PITCH_C, lambda j: first + j * 2 + ri) for ri in range(2))
        p00, p01, p10, p11 = inverse_planes(real, imag, wzi, tyi)
        p01, p10 = jnp.where(half == 0, p01, p10), jnp.where(half == 0, p10, p01)
        here = half * 4 + jnp.where(n == 0, core, 1 - core) * 2
        there = (1 - half) * 4 + (core if f == 0 else 1 - core) * 2
        n0, n1 = occ[here] * chip[n, 0, half], occ[here + 1] * chip[n, 1, half]
        f0, f1 = occ[there] * far[f, 0], occ[there + 1] * far[f, 1]
        pf[f, 0] = n0 * p00 + n1 * p10
        pf[f, 1] = n0 * p01 + n1 * p11
        send()
        acc[n, 0, half] += f0 * p00 + f1 * p01
        acc[n, 1, half] += f0 * p10 + f1 * p11

    merge = remote(pf.at[1], merged, X1S, X1R, band=other_core)
    home = Cut(pf.at[0], df, DS, DR, other_half)

    def send_home():
        merge.wait_recv()
        pf[0] += merged[...]
        home.start()

    cross_terms(*quads[1], merge.start)
    cross_terms(*quads[0], send_home)

    arrived(b_r2, PIECES * PIECE_2, B2R)
    for p in range(2):
        a_re, b_re, a_im, b_im = unpack(b_r2, PITCH_2, lambda j: j * 2 + p)
        pot = inverse_planes([a_re, b_re], [a_im, b_im], wzi, tyi)
        act[0, p] += occ[theirs + v0] * v[v0, p] * pot[0]
        act[1, p] += occ[theirs + v1] * v[v1, p] * pot[1]
        pv[v0, p] += occ[mine] * u[0, p] * pot[0]
        pv[v1, p] += occ[mine + 1] * u[1, p] * pot[1]
    swap = remote(pv, pvr, E2S, E2R, band=other_core)
    swap.start()
    swap.wait_recv()
    for i in range(2):
        out[i, half] = -(act[i, half] + pvr[i, half])
        acc[0, i, 1 - half] += pvr[i, 1 - half]
    home.wait_recv()
    for i in range(2):
        out[i, 1 - half] = -(act[i, 1 - half] + df[i])

    to_core.wait_send()
    to_half.wait_send()

    @pl.when(core == 0)
    def _():
        mask_to_core.wait_send()
        mask_copies(lambda c: c.wait_send(), None)

    for src, pieces, piece, send in (
        (f_s1, PIECES, PIECE_1, F1S),
        (f_s2, PIECES, PIECE_2, F2S),
        (f_sc, 2 * PIECES, PIECE_C, FCS),
    ):
        sized(three, lambda mine: arrived(src, (pieces - mine) * piece, send))
    arrived_own(b_s1, PEERS - 1, PIECE_1, B1S)
    arrived_own(b_s2, PEERS - 1, PIECE_2, B2S)
    arrived_own(b_sc, 2 * PEERS - 1, PIECE_C, BCS)
    far_to_core.wait_send()
    merge.wait_send()
    swap.wait_send()
    home.wait_send()


def on_device(orbitals, occupation, kept_modes):
    block = pltpu.VMEM((2, 2, N, N), jnp.float32)
    twice = pltpu.VMEM((2, 2, 2, N, N), jnp.float32)
    plane = pltpu.VMEM((2, N, N), jnp.float32)
    planes = pltpu.VMEM((2, 2, N, N), jnp.float32)
    messages = [
        pltpu.VMEM(((slots + 1) * pitch, 128), jnp.float32)
        for slots, pitch in ((PEERS, PITCH_1), (PEERS, PITCH_2), (2 * PEERS, PITCH_C))
        for _ in range(4)
    ]
    tables = make_tables()
    loaded = [twice, pltpu.VMEM(kept_modes.shape, jnp.int32)]
    loaded += [pltpu.VMEM(t.shape, jnp.bfloat16) for t in tables]
    return pl.pallas_call(
        body,
        out_shape=jax.ShapeDtypeStruct(orbitals.shape, jnp.float32),
        in_specs=[pl.BlockSpec(memory_space=pltpu.SMEM)] + [pl.BlockSpec(memory_space=pltpu.HBM)] * 9,
        out_specs=pl.BlockSpec(memory_space=pltpu.VMEM),
        scratch_shapes=loaded
        + [planes, block, plane, plane, twice, planes]
        + [pltpu.VMEM((8, 32, 128), jnp.float32), pltpu.VMEM((4, 32, 128), jnp.float32)]
        + [pltpu.VMEM((3, N, 128), jnp.float32)]
        + messages
        + [
            pltpu.SemaphoreType.DMA((NSEM,)),
            pltpu.SemaphoreType.REGULAR,
        ],
        compiler_params=pltpu.CompilerParams(
            collective_id=1, has_side_effects=True, vmem_limit_bytes=60 << 20
        ),
        name="exchange",
    )(occupation, orbitals, kept_modes, *(jnp.asarray(t) for t in tables))


def solution(mesh):
    return jax.shard_map(
        on_device,
        mesh=mesh,
        in_specs=(P("band", "grid", None, None), P(), P(None, "grid", None)),
        out_specs=P("band", "grid", None, None),
        check_vma=False,
    )
```
